32 devices in a mesh: dp: 16 (over z, y, core), mp: 2 (over x).
Axes of the slice: x: 2, y: 2, z: 4, core: 2. Of those that a mesh axis runs over, the one named last changes fastest.
Arguments:
- tokens: bfloat16 [1024, 32, 1024], P('mp', 'dp'), may hold values from -6 to 6
- memory: bfloat16 [1024, 32, 1024], P('mp', 'dp'), may hold values from -6 to 6
- cotangent: bfloat16 [1024, 32, 1024], P('mp', 'dp'), may hold values from -6 to 6
- lengths: int32 [32], P('dp'), may hold values from 1 to 1024, 24576 in all
- memory_lengths: int32 [32], P('dp'), may hold values from 1 to 1024, 24576 in all
- pair_ids: int32 [32], P('dp'), may hold values from 0 to 7
- pair_counts: int32 [8], replicated, may hold values from 128 to 1023
- self_in: bfloat16 [3, 1024, 1024], P(None, 'dp', 'mp'), may hold values from -0.1875 to 0.1875
- self_out: bfloat16 [1024, 1024], P('mp', 'dp'), may hold values from -3 to 3
- cross_in: bfloat16 [3, 1024, 1024], P(None, 'dp', 'mp'), may hold values from -0.1875 to 0.1875
- cross_out: bfloat16 [1024, 1024], P('mp', 'dp'), may hold values from -3 to 3
- fc_in: bfloat16 [1024, 4096], P('dp', 'mp'), may hold values from -0.1875 to 0.1875
- fc_out: bfloat16 [4096, 1024], P('mp', 'dp'), may hold values from -0.125 to 0.125
- head_biases: bfloat16 [4, 16, 64], P(None, 'mp', 'dp'), may hold values from -2 to 2
- inner_bias: bfloat16 [16, 256], P('mp', 'dp'), may hold values from -3 to 3
- norm_gains: float32 [3, 1024], P(None, ('dp', 'mp')), may hold values from 0.1 to 1.9
- feature_biases: float32 [6, 1024], P(None, ('dp', 'mp')), may hold values from -0.8 to 0.8
Outputs:
- output: bfloat16 [1024, 32, 1024], P('mp', 'dp')
- grad_tokens: float32 [1024, 32, 1024], P('mp', 'dp')
- grad_memory: float32 [1024, 32, 1024], P('mp', 'dp')
- grad_self_in: float32 [3, 1024, 1024], P(None, 'dp', 'mp')
- grad_self_out: float32 [1024, 1024], P('mp', 'dp')
- grad_cross_in: float32 [3, 1024, 1024], P(None, 'dp', 'mp')
- grad_cross_out: float32 [1024, 1024], P('mp', 'dp')
- grad_fc_in: float32 [1024, 4096], P('dp', 'mp')
- gradient_feedforward_output: float32 [4096, 1024], P('mp', 'dp')
- grad_head_biases: float32 [4, 16, 64], P(None, 'mp', 'dp')
- grad_inner_bias: float32 [16, 256], P('mp', 'dp')
- grad_norm_gains: float32 [3, 1024], P(None, ('dp', 'mp'))
- grad_feature_biases: float32 [6, 1024], P(None, ('dp', 'mp'))
The draws below stay inside these ranges and needn't reach their ends.
Inputs may be any that keep to these rules, and one draw needn't show every extreme that they name: `lengths`: some sequence has all 1024 positions valid. `memory_lengths`: some sequence has all 1024 memory positions valid.
All inputs are finite; a program needn't handle non-finite values. No bound on the sum of `lengths` or of `memory_lengths` on one device may be relied on, other than what follows from the above.
Results may differ from the reference program's by a relative error of at most 0.033.
Values may be sent and summed in bfloat16 or wider, within the bound.
No kernel may reach another device: no remote copies, remote signals or barrier semaphores. Data moves between devices by JAX's collectives and lax.ppermute only.
A program may use at most 216 MiB of HBM per device.

```python
import math
import jax
import jax.numpy as jnp
import numpy as np
from jax import lax

D = 1024
H = 16
DH = 64
FF = 4096
LEN = 1024
MEM = 1024
PAIRS = 8
SEQS = 32
FFH = 256


def unit_values(key, shape):
    return jax.random.truncated_normal(key, -4.0, 4.0, shape, jnp.float32)


def draw_head_biases(key, part):
    key = jax.random.fold_in(key, 11)
    base = unit_values(key, (4, H, DH))
    row_scale = jnp.array([0.5, 0.02, 0.5, 0.02], jnp.float32)[:, None, None]
    return (base * row_scale).astype(jnp.bfloat16)


def draw_feature_biases(key, part):
    key = jax.random.fold_in(key, 23)
    base = unit_values(key, (6, D))
    row_scale = jnp.array([0.02, 0.2, 0.2, 0.05, 0.05, 0.05], jnp.float32)[:, None]
    return (base * row_scale).astype(jnp.float32)


def place_ends(values, key, low, high):
    index_at = [jax.random.randint(jax.random.fold_in(key, axis), (), 0, length) for axis, length in enumerate(values.shape)]
    widest = values.shape.index(max(values.shape))
    neighbour = index_at[:widest] + [(index_at[widest] + 1) % values.shape[widest]] + index_at[widest + 1:]
    return values.at[tuple(index_at)].set(low).at[tuple(neighbour)].set(high)


def steps_of(rng, shape, split, low, top_value):
    def one(dim, parts):
        draws = jax.random.uniform(jax.random.fold_in(jax.random.fold_in(rng, 6), dim), (parts,), jnp.float32, low / len(split), top_value / len(split))
        return jnp.repeat(jnp.exp(draws), shape[dim] // parts).reshape((-1,) + (1,) * (len(shape) - dim - 1))

    level = one(*split[0])
    for cut in split[1:]:
        level = level * one(*cut)
    return level


def cumulative_ranks(count, lean):
    portions = [(1 << 20) // math.isqrt(standing ** lean) + 1 for standing in range(1, count + 1)]
    width = 1 + sum(portions) // (1 << 30)
    return np.cumsum(np.array([max(1, weight // width) for weight in portions]))


def skewed_ids(key, shape, number_of, slope):
    grid = cumulative_ranks(number_of, slope)
    pick = jax.random.randint(jax.random.fold_in(key, 1), shape, 0, int(grid[number_of - 1]))
    rank = jnp.searchsorted(jnp.asarray(grid, jnp.int32), pick, side="right")
    return jax.random.permutation(jax.random.fold_in(key, 2), number_of)[rank].astype(jnp.int32)


def split_up(count, total, reach, skew):
    weights = [(1 << 20) // math.isqrt(rank ** skew) + 1 for rank in range(2, count + 1)]
    spare, given = total - reach - (count - 1), [1] * (count - 1)
    while spare > 0:
        candidates = [i for i in range(count - 1) if given[i] < reach]
        pool, remaining = sum([weights[i] for i in candidates]), spare
        for i in candidates:
            addition = min(reach - given[i], max(1, remaining * weights[i] // pool), spare)
            given[i] = given[i] + addition
            spare = spare - addition
    return np.array([reach] + given)


def ragged_sizes(stream_key, amount, total, reach, skew):
    if amount == 2:
        one = jax.random.randint(stream_key, (), max(1, total - reach), min(reach, total - 1) + 1)
        return jnp.stack([one, total - one])
    sizes = jnp.asarray(split_up(amount, total, reach, skew), jnp.int32)
    twos = (amount - 1) // 2
    donor, receiver = sizes[1:1 + 2 * twos:2], sizes[2:2 + 2 * twos:2]
    slack = jnp.minimum(donor - 1, reach - receiver)
    passed = jax.random.randint(jax.random.fold_in(stream_key, 1), (twos,), 0, 1 << 20) % (slack + 1)
    sizes = sizes.at[1:1 + 2 * twos:2].set(donor - passed).at[2:2 + 2 * twos:2].set(receiver + passed)
    return sizes[jax.random.permutation(jax.random.fold_in(stream_key, 2), amount)]


def noise(key, shape, width, most, pieces=(), held_as=jnp.bfloat16):
    values = jax.random.normal(key, shape, jnp.float32) * width
    if len(pieces) > 0:
        values = steps_of(key, shape, pieces, -0.22, 0.18) * values
    return jnp.clip(values, min=-most, max=most).astype(held_as)


def setup_inputs(seed: int = 0) -> dict:
    arg_keys = jax.random.split(jax.random.key(seed), 18)
    return {
        "tokens": noise(arg_keys[0], (LEN, SEQS, D), 1.0, 6.0, ((0, 2), (1, 16))),
        "memory": noise(arg_keys[1], (MEM, SEQS, D), 1.0, 6.0, ((0, 2), (1, 16))),
        "cotangent": noise(arg_keys[2], (LEN, SEQS, D), 1.0, 6.0, ((0, 2), (1, 16))),
        "lengths": ragged_sizes(arg_keys[3], SEQS, SEQS * LEN * 3 // 4, LEN, 2).astype(jnp.int32),
        "memory_lengths": ragged_sizes(arg_keys[4], SEQS, SEQS * MEM * 3 // 4, MEM, 1).astype(jnp.int32),
        "pair_ids": place_ends(skewed_ids(arg_keys[5], (SEQS,), PAIRS, 2), jax.random.fold_in(arg_keys[5], 3), 0, PAIRS - 1).astype(jnp.int32),
        "pair_counts": place_ends(jax.random.randint(arg_keys[6], (PAIRS,), 128, 1024), jax.random.fold_in(arg_keys[6], 1), 128, 1023).astype(jnp.int32),
        "self_in": noise(arg_keys[7], (3, D, D), D ** -0.5, 0.1875, ((1, 16), (2, 2))),
        "self_out": noise(arg_keys[8], (D, D), (D // 256) ** -0.5, 3.0, ((0, 2), (1, 16))),
        "cross_in": noise(arg_keys[9], (3, D, D), D ** -0.5, 0.1875, ((1, 16), (2, 2))),
        "cross_out": noise(arg_keys[10], (D, D), (D // 256) ** -0.5, 3.0, ((0, 2), (1, 16))),
        "fc_in": noise(arg_keys[11], (D, FF), D ** -0.5, 0.1875, ((0, 16), (1, 2))),
        "fc_out": noise(arg_keys[12], (FF, D), (FF // 2) ** -0.5, 0.125, ((0, 2), (1, 16))),
        "head_biases": draw_head_biases(jax.random.fold_in(arg_keys[17], 71), 0),
        "inner_bias": noise(arg_keys[14], (H, FFH), 0.5, 3.0, ((0, 2), (1, 16))),
        "norm_gains": jnp.clip(1.0 + 0.18 * jax.random.normal(arg_keys[15], (3, D), jnp.float32), 0.1, 1.9),
        "feature_biases": draw_feature_biases(jax.random.fold_in(arg_keys[17], 71), 0),
    }


@jax.custom_vjp
def low(v):
    return lax.optimization_barrier(v.astype(jnp.bfloat16)).astype(jnp.float32)

@jax.custom_vjp
def low_back(v):
    return v

def low_keep(v):
    return (low(v), None)

def low_pass(kept, grad):
    return (grad,)

def back_keep(v):
    return (v, None)

def back_low(kept, grad):
    return (low(grad),)
low.defvjp(low_keep, low_pass)
low_back.defvjp(back_keep, back_low)
eps = 1e-05
precision_high = lax.Precision.HIGHEST
floor_score = -1e+30

def layer_norm(hidden, gain, shift):
    average = lax.optimization_barrier(jnp.mean(hidden, -1, keepdims=True))
    centred = hidden - average
    spread = lax.optimization_barrier(jnp.mean(centred * centred, -1, keepdims=True))
    return centred * lax.rsqrt(spread + eps) * gain + shift

def product(left, right):
    return jnp.dot(left, right, precision=precision_high)

def attend(queries, keys, values, allowed):
    length = queries.shape[0]
    block = min(512, length)

    def one_block(index):
        start = index * block
        slice_part = lax.dynamic_slice_in_dim(queries, start, block, 0)
        mask_piece = lax.dynamic_slice_in_dim(allowed, start, block, 0)
        scores = low_back(jnp.einsum('qhd,khd->hqk', slice_part, keys, precision=precision_high))
        scores = jnp.where(mask_piece[None], scores, floor_score)
        probs = low(jax.nn.softmax(scores, axis=-1))
        return jnp.einsum('hqk,khd->qhd', probs, values, precision=precision_high)
    outputs = lax.map(jax.checkpoint(one_block), jnp.arange(length // block, dtype=jnp.int32))
    return outputs.reshape(length, H * DH)

def decoder_layer(hidden_in, memory_seq, memory_limit, params):
    self_in, self_out, cross_in, cross_out, fc_in, fc_out, head_biases, inner_bias, norm_gains, feature_biases = params
    positions = jnp.arange(LEN, dtype=jnp.int32)
    causal = positions[:, None] >= positions[None, :]
    reachable = jnp.broadcast_to(jnp.arange(MEM, dtype=jnp.int32)[None, :] < memory_limit, (LEN, MEM))
    biases = head_biases.reshape(4, D)
    normed = low(layer_norm(hidden_in, norm_gains[0], feature_biases[0]))
    queries = low_back(low((product(normed, self_in[0]) + biases[0]) * 0.125))
    keys = low_back(low(product(normed, self_in[1])))
    values = low_back(low(product(normed, self_in[2]) + biases[1]))
    mixed = attend(queries.reshape(LEN, H, DH), keys.reshape(LEN, H, DH), values.reshape(LEN, H, DH), causal)
    mixed = low_back(low(mixed))
    hidden_one = hidden_in + low_back(product(mixed, self_out)) + feature_biases[3]
    normed = low(layer_norm(hidden_one, norm_gains[1], feature_biases[1]))
    queries = low_back(low((product(normed, cross_in[0]) + biases[2]) * 0.125))
    keys = low_back(low(product(memory_seq, cross_in[1])))
    values = low_back(low(product(memory_seq, cross_in[2]) + biases[3]))
    mixed = attend(queries.reshape(LEN, H, DH), keys.reshape(MEM, H, DH), values.reshape(MEM, H, DH), reachable)
    mixed = low_back(low(mixed))
    hidden_two = hidden_one + low_back(product(mixed, cross_out)) + feature_biases[4]
    normed = low(layer_norm(hidden_two, norm_gains[2], feature_biases[2]))
    inner = low_back(product(normed, fc_in) + inner_bias.reshape(FF))
    active_units = low(jax.nn.gelu(inner, approximate=True))
    return hidden_two + low_back(product(active_units, fc_out)) + feature_biases[5]

def reference(tokens, memory, cotangent, lengths, memory_lengths, pair_ids, pair_counts, self_in, self_out, cross_in, cross_out, fc_in, fc_out, head_biases, inner_bias, norm_gains, feature_biases):
    params = tuple((argument.astype(jnp.float32) for argument in (self_in, self_out, cross_in, cross_out, fc_in, fc_out, head_biases, inner_bias, norm_gains, feature_biases)))
    tokens_seq = jnp.transpose(tokens.astype(jnp.float32), (1, 0, 2))
    memory_seq = jnp.transpose(memory.astype(jnp.float32), (1, 0, 2))

    def forward(tokens_all, memory_all, weights):

        def one_sequence(carry, inputs):
            return (carry, decoder_layer(inputs[0], inputs[1], inputs[2], weights))
        carry_out, outputs = lax.scan(jax.checkpoint(one_sequence), jnp.zeros((), jnp.float32), (tokens_all, memory_all, memory_lengths))
        return outputs
    outputs, pullback = jax.vjp(forward, tokens_seq, memory_seq, params)
    counts = pair_counts.astype(jnp.float32)
    matches = (pair_ids[:, None] == jnp.arange(PAIRS, dtype=jnp.int32)[None, :]).astype(jnp.float32)
    own_count = lax.optimization_barrier(jnp.sum(matches * counts[None, :], -1))
    scale = jnp.mean(counts) / own_count
    valid = (jnp.arange(LEN, dtype=jnp.int32)[None, :] < lengths[:, None]).astype(jnp.float32)
    weighted = jnp.transpose(cotangent.astype(jnp.float32), (1, 0, 2)) * (valid * scale[:, None])[:, :, None]
    grad_tokens, grad_memory, grad_params = pullback(weighted)
    return (jnp.transpose(outputs, (1, 0, 2)).astype(jnp.bfloat16), jnp.transpose(grad_tokens, (1, 0, 2)), jnp.transpose(grad_memory, (1, 0, 2)), grad_params[0], grad_params[1], grad_params[2], grad_params[3], grad_params[4], grad_params[5], grad_params[6], grad_params[7], grad_params[8], grad_params[9])
```

```python
from functools import partial

import jax
import jax.numpy as jnp
from jax import lax
from jax.experimental import pallas as pl
from jax.experimental.pallas import tpu as pltpu
from jax.sharding import PartitionSpec as P

eps = 1e-05
floor_score = -1e30


def smooth_unit(values):
    return jax.nn.gelu(values, approximate=True)


def normalize(hidden, gain, shift):
    average = jnp.mean(hidden, -1, keepdims=True)
    centred = hidden - average
    inverse = lax.rsqrt(jnp.mean(centred * centred, -1, keepdims=True) + eps)
    unit = centred * inverse
    return (unit * gain + shift, unit, inverse)


def normalize_back(grad_normed, gain, unit, inverse):
    grad_unit = grad_normed * gain
    grad_hidden = inverse * (
        grad_unit
        - jnp.mean(grad_unit, -1, keepdims=True)
        - unit * jnp.mean(grad_unit * unit, -1, keepdims=True)
    )
    return (grad_hidden, jnp.sum(grad_normed * unit, (0, 1)), jnp.sum(grad_normed, (0, 1)))


def masked_scores(rows, keys, first, limit, causal):
    scores = jnp.einsum("qhd,khd->hqk", rows, keys, preferred_element_type=jnp.float32)
    key_place = jnp.arange(keys.shape[0], dtype=jnp.int32)[None, :]
    if causal:
        allowed = key_place <= first + jnp.arange(rows.shape[0], dtype=jnp.int32)[:, None]
    else:
        allowed = key_place < limit
    return jnp.where(allowed[None], scores, floor_score)


def attend_forward(queries, keys, values, limit, causal):
    length = queries.shape[0]
    block = min(512, length)
    outputs = []
    totals = []
    for first in range(0, length, block):
        span = first + block if causal else keys.shape[0]
        scores = masked_scores(queries[first : first + block], keys[:span], first, limit, causal)
        highest = jnp.max(scores, -1, keepdims=True)
        raised = jnp.exp(scores - highest)
        total = jnp.sum(raised, -1, keepdims=True)
        probs = (raised / total).astype(jnp.bfloat16)
        outputs.append(
            jnp.einsum("hqk,khd->qhd", probs, values[:span], preferred_element_type=jnp.float32)
        )
        totals.append((highest + jnp.log(total))[:, :, 0])
    return (jnp.concatenate(outputs, 0), jnp.concatenate(totals, 1))


def attend_backward(queries, keys, values, totals, grad_mixed, limit, causal):
    length = queries.shape[0]
    block = min(512, length)
    key_grads = jnp.zeros(keys.shape, jnp.float32)
    value_grads = jnp.zeros(values.shape, jnp.float32)
    query_grads = []
    for first in range(0, length, block):
        span = first + block if causal else keys.shape[0]
        rows = queries[first : first + block]
        grad_piece = grad_mixed[first : first + block]
        scores = masked_scores(rows, keys[:span], first, limit, causal)
        probs = jnp.exp(scores - totals[:, first : first + block, None])
        grad_probs = jnp.einsum(
            "qhd,khd->hqk", grad_piece, values[:span], preferred_element_type=jnp.float32
        )
        inner_sum = jnp.sum(probs * grad_probs, -1, keepdims=True)
        grad_scores = (probs * (grad_probs - inner_sum)).astype(jnp.bfloat16)
        query_grads.append(
            jnp.einsum("hqk,khd->qhd", grad_scores, keys[:span], preferred_element_type=jnp.float32)
        )
        key_grads = key_grads.at[:span].add(
            jnp.einsum("hqk,qhd->khd", grad_scores, rows, preferred_element_type=jnp.float32)
        )
        value_grads = value_grads.at[:span].add(
            jnp.einsum(
                "hqk,qhd->khd",
                probs.astype(jnp.bfloat16),
                grad_piece,
                preferred_element_type=jnp.float32,
            )
        )
    return (jnp.concatenate(query_grads, 0), key_grads, value_grads)


def run_forward(operands, causal):
    return attend_forward(operands[0], operands[1], operands[2], operands[3], causal)


def run_backward(operands, causal):
    return attend_backward(
        operands[0], operands[1], operands[2], operands[3], operands[4], operands[5], causal
    )


def gather_rows(normed):
    return lax.all_gather(normed, "mp", axis=0, tiled=True)


def spread_rows(term_fn, rows):
    return lax.psum_scatter(
        term_fn(jnp.int32(0), lax.axis_size("mp") * rows).astype(jnp.bfloat16),
        "mp",
        scatter_dimension=0,
        tiled=True,
    ).astype(jnp.float32)


def whole_rows(term_fn, local, start_row):
    full_rows = local.shape[0] * lax.axis_size("mp")
    term = term_fn(0, full_rows)
    placed = lax.dynamic_update_slice_in_dim(jnp.zeros_like(term), local, start_row, 0)
    return lax.psum((term + placed).astype(jnp.bfloat16), "mp").astype(jnp.float32)


def gather_grads(grad_branch):
    return lax.all_gather(grad_branch, "mp", axis=0, tiled=True)


def reduce_inputs(term_fn, rows):
    return lax.psum_scatter(
        term_fn(jnp.int32(0), lax.axis_size("mp") * rows).astype(jnp.bfloat16),
        "mp",
        scatter_dimension=0,
        tiled=True,
    ).astype(jnp.float32)


def body(
    tokens,
    memory,
    cotangent,
    lengths,
    memory_lengths,
    pair_ids,
    pair_counts,
    self_in,
    self_out,
    cross_in,
    cross_out,
    fc_in,
    fc_out,
    head_biases,
    inner_bias,
    norm_gains,
    feature_biases,
):
    shards = (self_in, self_out, cross_in, cross_out, fc_in, fc_out, head_biases, inner_bias)
    gathered = (
        lax.all_gather(shards[0], "dp", axis=1, tiled=True),
        lax.all_gather(shards[1], "dp", axis=1, tiled=True),
        lax.all_gather(shards[2], "dp", axis=1, tiled=True),
        lax.all_gather(shards[3], "dp", axis=1, tiled=True),
        lax.all_gather(shards[4], "dp", axis=0, tiled=True),
        lax.all_gather(shards[5], "dp", axis=1, tiled=True),
        lax.all_gather(shards[6], "dp", axis=2, tiled=True),
        lax.all_gather(shards[7], "dp", axis=1, tiled=True),
    )
    gains, shifts = (
        lax.all_gather(norm_gains, ("dp", "mp"), axis=1, tiled=True),
        lax.all_gather(feature_biases, ("dp", "mp"), axis=1, tiled=True),
    )
    local_rows, seq_count, width = tokens.shape
    memory_local = memory.shape[0]
    heads_here = head_biases.shape[1]
    head_size = gathered[6].shape[2]
    local_width = heads_here * head_size
    length = local_rows * lax.axis_size("mp")
    memory_length = memory_local * lax.axis_size("mp")
    shape_heads = (seq_count, length, heads_here, head_size)
    shape_memory = (seq_count, memory_length, heads_here, head_size)
    start_row = lax.axis_index("mp") * local_rows
    (
        w_self_in,
        w_self_out,
        w_cross_in,
        w_cross_out,
        feedforward_input_weight,
        feedforward_output_weight,
        w_heads,
        w_inner,
    ) = gathered
    bias_heads = w_heads.astype(jnp.float32).reshape(4, local_width)
    bias_inner = w_inner.astype(jnp.float32).reshape(-1)
    hidden_in = tokens.astype(jnp.float32)
    normed_one, unit_one, inverse_one = normalize(hidden_in, gains[0], shifts[0])
    rows_one = gather_rows(normed_one.astype(jnp.bfloat16))
    project = jnp.einsum("lsd,kde->ksle", rows_one, w_self_in, preferred_element_type=jnp.float32)
    queries_self = ((project[0] + bias_heads[0]) * 0.125).astype(jnp.bfloat16).reshape(shape_heads)
    keys_self = project[1].astype(jnp.bfloat16).reshape(shape_heads)
    values_self = (project[2] + bias_heads[1]).astype(jnp.bfloat16).reshape(shape_heads)
    mixed_self, totals_self = lax.map(
        partial(run_forward, causal=True), (queries_self, keys_self, values_self, lengths)
    )
    mixed_self = mixed_self.astype(jnp.bfloat16).reshape(seq_count, length, local_width)

    def self_term(start, count):
        slice_part = lax.dynamic_slice_in_dim(mixed_self, start, count, 1)
        return jnp.einsum("sle,ed->lsd", slice_part, w_self_out, preferred_element_type=jnp.float32)

    whole_one = whole_rows(self_term, hidden_in, start_row) + shifts[3]
    hidden_one = lax.dynamic_slice_in_dim(whole_one, start_row, local_rows, 0)
    normed_two, unit_two, inverse_two = normalize(hidden_one, gains[1], shifts[1])
    rows_two = normalize(whole_one, gains[1], shifts[1])[0].astype(jnp.bfloat16)
    memory_all = lax.all_gather(memory, "mp", axis=0, tiled=True)
    queries_cross = (
        (
            (
                jnp.einsum(
                    "lsd,de->sle", rows_two, w_cross_in[0], preferred_element_type=jnp.float32
                )
                + bias_heads[2]
            )
            * 0.125
        )
        .astype(jnp.bfloat16)
        .reshape(shape_heads)
    )
    memory_project = jnp.einsum(
        "msd,kde->ksme", memory_all, w_cross_in[1:], preferred_element_type=jnp.float32
    )
    keys_cross = memory_project[0].astype(jnp.bfloat16).reshape(shape_memory)
    values_cross = (memory_project[1] + bias_heads[3]).astype(jnp.bfloat16).reshape(shape_memory)
    mixed_cross, totals_cross = lax.map(
        partial(run_forward, causal=False),
        (queries_cross, keys_cross, values_cross, memory_lengths),
    )
    mixed_cross = mixed_cross.astype(jnp.bfloat16).reshape(seq_count, length, local_width)

    def cross_term(start, count):
        slice_part = lax.dynamic_slice_in_dim(mixed_cross, start, count, 1)
        return jnp.einsum(
            "sle,ed->lsd", slice_part, w_cross_out, preferred_element_type=jnp.float32
        )

    whole_two = whole_rows(cross_term, hidden_one, start_row) + shifts[4]
    hidden_two = lax.dynamic_slice_in_dim(whole_two, start_row, local_rows, 0)
    normed_three, unit_three, inverse_three = normalize(hidden_two, gains[2], shifts[2])
    third_rows = normalize(whole_two, gains[2], shifts[2])[0].astype(jnp.bfloat16)
    inner = (
        jnp.einsum(
            "wri,ix->wrx", third_rows, feedforward_input_weight, preferred_element_type=jnp.float32
        )
        + bias_inner
    )
    smooth_value, smooth_pull = jax.vjp(smooth_unit, inner)
    active_units = smooth_value.astype(jnp.bfloat16)

    def ffn_term(start, count):
        slice_part = lax.dynamic_slice_in_dim(active_units, start, count, 0)
        return jnp.einsum(
            "crx,xp->crp", slice_part, feedforward_output_weight, preferred_element_type=jnp.float32
        )

    output = (hidden_two + spread_rows(ffn_term, local_rows) + shifts[5]).astype(jnp.bfloat16)
    again = (
        lax.all_gather(shards[0], "dp", axis=1, tiled=True),
        lax.all_gather(shards[1], "dp", axis=1, tiled=True),
        lax.all_gather(shards[2], "dp", axis=1, tiled=True),
        lax.all_gather(shards[3], "dp", axis=1, tiled=True),
        lax.all_gather(shards[4], "dp", axis=0, tiled=True),
        lax.all_gather(shards[5], "dp", axis=1, tiled=True),
        lax.all_gather(shards[6], "dp", axis=2, tiled=True),
        lax.all_gather(shards[7], "dp", axis=1, tiled=True),
    )
    (
        w_self_in,
        w_self_out,
        w_cross_in,
        w_cross_out,
        feedforward_input_weight,
        feedforward_output_weight,
        w_heads,
        w_inner,
    ) = again
    counts = pair_counts.astype(jnp.float32)
    matches = (pair_ids[:, None] == jnp.arange(counts.shape[0], dtype=jnp.int32)[None, :]).astype(
        jnp.float32
    )
    own_count = jnp.sum(matches * counts[None, :], -1)
    scale = jnp.mean(counts) / own_count
    positions = start_row + jnp.arange(local_rows, dtype=jnp.int32)
    valid = (positions[:, None] < lengths[None, :]).astype(jnp.float32)
    grad_out = cotangent.astype(jnp.float32) * (valid * scale[None, :])[:, :, None]
    gradient_rows3 = gather_grads(grad_out.astype(jnp.bfloat16))
    gradient_feedforward_output = jnp.einsum(
        "ytb,yth->bh", active_units, gradient_rows3, preferred_element_type=jnp.float32
    )
    grad_active = jnp.einsum(
        "vmr,yr->vmy", gradient_rows3, feedforward_output_weight, preferred_element_type=jnp.float32
    )
    gradient_inner_hidden = smooth_pull(grad_active)[0].astype(jnp.bfloat16)
    grad_fc_in = jnp.einsum(
        "eoc,eoi->ci", third_rows, gradient_inner_hidden, preferred_element_type=jnp.float32
    )
    grad_inner_bias = jnp.sum(gradient_inner_hidden.astype(jnp.float32), (0, 1)).reshape(
        w_inner.shape
    )

    def ffn_back(start, count):
        slice_part = lax.dynamic_slice_in_dim(gradient_inner_hidden, start, count, 0)
        return jnp.einsum(
            "mou,tu->mot", slice_part, feedforward_input_weight, preferred_element_type=jnp.float32
        )

    grad_normed3 = reduce_inputs(ffn_back, local_rows)
    back_three, gain_three, shift_three = normalize_back(
        grad_normed3, gains[2], unit_three, inverse_three
    )
    grad_hidden2 = grad_out + back_three
    grad_rows2 = gather_grads(grad_hidden2.astype(jnp.bfloat16))
    grad_cross_out = jnp.einsum(
        "sle,lsd->ed", mixed_cross, grad_rows2, preferred_element_type=jnp.float32
    )
    grad_mixed = (
        jnp.einsum("lsd,ed->sle", grad_rows2, w_cross_out, preferred_element_type=jnp.float32)
        .astype(jnp.bfloat16)
        .reshape(shape_heads)
    )
    grad_query, grad_key, grad_value = lax.map(
        partial(run_backward, causal=False),
        (queries_cross, keys_cross, values_cross, totals_cross, grad_mixed, memory_lengths),
    )
    grad_query = (grad_query.astype(jnp.bfloat16) * 0.125).reshape(seq_count, length, local_width)
    memory_stack = jnp.stack(
        [
            grad_key.astype(jnp.bfloat16).reshape(seq_count, memory_length, local_width),
            grad_value.astype(jnp.bfloat16).reshape(seq_count, memory_length, local_width),
        ]
    )
    grad_cross_query = jnp.einsum(
        "lsd,sle->de", rows_two, grad_query, preferred_element_type=jnp.float32
    )
    grad_cross_pair = jnp.einsum(
        "msd,ksme->kde", memory_all, memory_stack, preferred_element_type=jnp.float32
    )
    grad_cross_in = jnp.concatenate([grad_cross_query[None], grad_cross_pair], 0)
    bias_query_cross = jnp.sum(grad_query.astype(jnp.float32), (0, 1))
    bias_value_cross = jnp.sum(memory_stack[1].astype(jnp.float32), (0, 1))

    def memory_back(start, count):
        return jnp.einsum(
            "ksme,kde->msd", memory_stack, w_cross_in[1:], preferred_element_type=jnp.float32
        )

    grad_memory = reduce_inputs(memory_back, memory_local)

    def cross_back(start, count):
        slice_part = lax.dynamic_slice_in_dim(grad_query, start, count, 1)
        return jnp.einsum(
            "sle,de->lsd", slice_part, w_cross_in[0], preferred_element_type=jnp.float32
        )

    grad_normed2 = reduce_inputs(cross_back, local_rows)
    back_two, gain_two, shift_two = normalize_back(grad_normed2, gains[1], unit_two, inverse_two)
    grad_hidden1 = grad_hidden2 + back_two
    grad_rows1 = gather_grads(grad_hidden1.astype(jnp.bfloat16))
    grad_self_out = jnp.einsum(
        "sle,lsd->ed", mixed_self, grad_rows1, preferred_element_type=jnp.float32
    )
    grad_mixed = (
        jnp.einsum("lsd,ed->sle", grad_rows1, w_self_out, preferred_element_type=jnp.float32)
        .astype(jnp.bfloat16)
        .reshape(shape_heads)
    )
    grad_query, grad_key, grad_value = lax.map(
        partial(run_backward, causal=True),
        (queries_self, keys_self, values_self, totals_self, grad_mixed, lengths),
    )
    flat_shape = (seq_count, length, local_width)
    self_stack = jnp.stack(
        [
            (grad_query.astype(jnp.bfloat16) * 0.125).reshape(flat_shape),
            grad_key.astype(jnp.bfloat16).reshape(flat_shape),
            grad_value.astype(jnp.bfloat16).reshape(flat_shape),
        ]
    )
    grad_self_in = jnp.einsum(
        "lsd,ksle->kde", rows_one, self_stack, preferred_element_type=jnp.float32
    )
    bias_query_self = jnp.sum(self_stack[0].astype(jnp.float32), (0, 1))
    bias_value_self = jnp.sum(self_stack[2].astype(jnp.float32), (0, 1))

    def self_back(start, count):
        slice_part = lax.dynamic_slice_in_dim(self_stack, start, count, 2)
        return jnp.einsum(
            "ksle,kde->lsd", slice_part, w_self_in, preferred_element_type=jnp.float32
        )

    grad_normed1 = reduce_inputs(self_back, local_rows)
    back_one, gain_one, shift_one = normalize_back(grad_normed1, gains[0], unit_one, inverse_one)
    grad_tokens = grad_hidden1 + back_one
    grad_heads = jnp.stack(
        [bias_query_self, bias_value_self, bias_query_cross, bias_value_cross]
    ).reshape(w_heads.shape)
    gain_grads = jnp.stack([gain_one, gain_two, gain_three])
    shift_grads = jnp.stack(
        [
            shift_one,
            shift_two,
            shift_three,
            jnp.sum(grad_hidden1, (0, 1)),
            jnp.sum(grad_hidden2, (0, 1)),
            jnp.sum(grad_out, (0, 1)),
        ]
    )
    grad_gains, grad_shifts = (
        lax.psum_scatter(gain_grads, ("dp", "mp"), scatter_dimension=1, tiled=True),
        lax.psum_scatter(shift_grads, ("dp", "mp"), scatter_dimension=1, tiled=True),
    )
    all_sums = (
        lax.psum_scatter(
            grad_self_in.astype(jnp.bfloat16), "dp", scatter_dimension=1, tiled=True
        ).astype(jnp.float32),
        lax.psum_scatter(
            grad_self_out.astype(jnp.bfloat16), "dp", scatter_dimension=1, tiled=True
        ).astype(jnp.float32),
        lax.psum_scatter(
            grad_cross_in.astype(jnp.bfloat16), "dp", scatter_dimension=1, tiled=True
        ).astype(jnp.float32),
        lax.psum_scatter(
            grad_cross_out.astype(jnp.bfloat16), "dp", scatter_dimension=1, tiled=True
        ).astype(jnp.float32),
        lax.psum_scatter(
            grad_fc_in.astype(jnp.bfloat16), "dp", scatter_dimension=0, tiled=True
        ).astype(jnp.float32),
        lax.psum_scatter(
            gradient_feedforward_output.astype(jnp.bfloat16), "dp", scatter_dimension=1, tiled=True
        ).astype(jnp.float32),
        lax.psum_scatter(
            grad_heads.astype(jnp.bfloat16), "dp", scatter_dimension=2, tiled=True
        ).astype(jnp.float32),
        lax.psum_scatter(
            grad_inner_bias.astype(jnp.bfloat16), "dp", scatter_dimension=1, tiled=True
        ).astype(jnp.float32),
    )
    (
        sum_self_in,
        sum_self_out,
        sum_cross_in,
        sum_cross_out,
        sum_fc_in,
        sum_fc_out,
        sum_heads,
        sum_inner,
    ) = all_sums
    return (
        output,
        grad_tokens,
        grad_memory,
        sum_self_in,
        sum_self_out,
        sum_cross_in,
        sum_cross_out,
        sum_fc_in,
        sum_fc_out,
        sum_heads,
        sum_inner,
        grad_gains,
        grad_shifts,
    )


LOG2E = 1.4426950408889634
LN2 = 0.6931471805599453
VM = pltpu.VMEM
ANYM = pl.ANY
F32 = jnp.float32
BF = jnp.bfloat16
NT_DIMS = (((1,), (1,)), ((), ()))
TN_DIMS = (((0,), (0,)), ((), ()))


def mm(a, b):
    return jnp.dot(a, b, preferred_element_type=F32)


def mm_nt(a, b):
    return lax.dot_general(a, b, NT_DIMS, preferred_element_type=F32)


def mm_tn(a, b):
    return lax.dot_general(a, b, TN_DIMS, preferred_element_type=F32)


def params_of(limit_mib, **more):
    return pltpu.CompilerParams(vmem_limit_bytes=limit_mib * 1024 * 1024, **more)


def cost(flops, data, exps=0):
    return pl.CostEstimate(flops=int(flops), bytes_accessed=int(data), transcendentals=int(exps))


def flow_meta(kind):
    if kind == "zxy":
        quads = [(0, 0), (1, 0), (0, 1), (1, 1)]
        return [[(k, y, c, x) for k in range(4)] for c in range(2) for (x, y) in quads]
    quads = [(0, 0), (1, 0), (0, 1), (1, 1)]
    return [[(k, y, c, x) for (x, y) in quads] for c in range(2) for k in range(4)]


def place_of(info, meta):
    k, y, c, x = meta
    slab = info[3] if x == 0 else 1 - info[3]
    zz = lax.rem(info[0] - k + 4, 4)
    yy = info[1] if y == 0 else 1 - info[1]
    cc = info[2] if c == 0 else 1 - info[2]
    return (slab, pl.multiple_of(zz * 256 + yy * 128 + cc * 64, 64))


def start_weight(info, pieces, kind, first, width, buffer, sems):
    for ref, metas in zip(pieces, flow_meta(kind)):
        for j, meta in enumerate(metas):
            slab, row = place_of(info, meta)
            pltpu.make_async_copy(
                ref.at[j, :, pl.ds(first, width)],
                buffer.at[slab, pl.ds(row, 64), :],
                sems.at[slab],
            ).start()


def wait_weight(buffer, sems, slab):
    pltpu.make_async_copy(buffer.at[slab], buffer.at[slab], sems.at[slab]).wait()


def ln_parts(hidden):
    average = jnp.mean(hidden, -1, keepdims=True)
    centred = hidden - average
    inverse = lax.rsqrt(jnp.mean(centred * centred, -1, keepdims=True) + eps)
    return (centred * inverse, inverse)


def ln_back(grad_normed, gain, unit, inverse):
    grad_unit = grad_normed * gain
    return inverse * (
        grad_unit
        - jnp.mean(grad_unit, -1, keepdims=True)
        - unit * jnp.mean(grad_unit * unit, -1, keepdims=True)
    )


def row_sum(values):
    return jnp.sum(values, 0, keepdims=True)


def transposed(values):
    return values.T


ROWS = 256


def qkv_kernel(info, par, x_ref, *rest):
    pieces, rest = rest[:24], rest[24:]
    q_ref, k_ref, v_ref, nt_ref, wq, wk, wv, sems = rest
    weights = (wq, wk, wv)

    @pl.when(pl.program_id(0) == 0)
    def _():
        for t in range(3):
            start_weight(info, pieces[8 * t : 8 * t + 8], KINDS[t], 0, 512, weights[t], sems.at[t])

    unit, _ = ln_parts(x_ref[...].astype(F32))
    normed = (unit * par[0:1, :] + par[3:4, :]).astype(BF)
    nt_ref[...] = transposed(normed)
    for t in range(3):
        for slab in range(2):

            @pl.when(pl.program_id(0) == 0)
            def _():
                wait_weight(weights[t], sems.at[t], slab)

            cols = slice(slab * 512, slab * 512 + 512)
            value = mm(normed, weights[t][slab])
            if t == 0:
                value = (value + par[9:10, cols]) * (0.125 * LOG2E)
            if t == 2:
                value = value + par[10:11, cols]
            (q_ref, k_ref, v_ref)[t][:, cols] = value.astype(BF)


KINDS = ("zxy", "xyz", "zxy")


def call_qkv(info, par, x, pieces):
    n = x.shape[0]
    out = jax.ShapeDtypeStruct((n, 1024), BF)
    rows = pl.BlockSpec((ROWS, 1024), lambda i, s: (i, 0))
    return pl.pallas_call(
        qkv_kernel,
        grid_spec=pltpu.PrefetchScalarGridSpec(
            num_scalar_prefetch=1,
            grid=(n // ROWS,),
            in_specs=[pl.BlockSpec((24, 1024), lambda i, s: (0, 0)), rows]
            + [pl.BlockSpec(memory_space=ANYM)] * 24,
            out_specs=[rows, rows, rows, pl.BlockSpec((1024, ROWS), lambda i, s: (0, i))],
            scratch_shapes=[VM((2, 1024, 512), BF)] * 3 + [pltpu.SemaphoreType.DMA((3, 2))],
        ),
        out_shape=[out, out, out, jax.ShapeDtypeStruct((1024, n), BF)],
        compiler_params=params_of(48),
        cost_estimate=cost(6.4e9, 16e6),
        name="project_self",
    )(info, par, x, *pieces)


def kv_kernel(info, par, x_ref, *rest):
    pieces, rest = rest[:8], rest[8:]
    k_ref, v_ref, nt_ref, wk, wv, sems = rest
    weights = (wk, wv)

    @pl.when(pl.program_id(0) == 0)
    def _():
        for t in range(2):
            start_weight(info, pieces, "zxy", t * 512, 512, weights[t], sems.at[t])

    rows = x_ref[...]
    nt_ref[...] = transposed(rows)
    for t in range(2):
        for slab in range(2):

            @pl.when(pl.program_id(0) == 0)
            def _():
                wait_weight(weights[t], sems.at[t], slab)

            cols = slice(slab * 512, slab * 512 + 512)
            value = mm(rows, weights[t][slab])
            if t == 1:
                value = value + par[12:13, cols]
            (k_ref, v_ref)[t][:, cols] = value.astype(BF)


def call_kv(info, par, x, pieces):
    n = x.shape[0]
    out = jax.ShapeDtypeStruct((n, 1024), BF)
    rows = pl.BlockSpec((ROWS, 1024), lambda i, s: (i, 0))
    return pl.pallas_call(
        kv_kernel,
        grid_spec=pltpu.PrefetchScalarGridSpec(
            num_scalar_prefetch=1,
            grid=(n // ROWS,),
            in_specs=[pl.BlockSpec((24, 1024), lambda i, s: (0, 0)), rows]
            + [pl.BlockSpec(memory_space=ANYM)] * 8,
            out_specs=[rows, rows, pl.BlockSpec((1024, ROWS), lambda i, s: (0, i))],
            scratch_shapes=[VM((2, 1024, 512), BF)] * 2 + [pltpu.SemaphoreType.DMA((2, 2))],
        ),
        out_shape=[out, out, jax.ShapeDtypeStruct((1024, n), BF)],
        compiler_params=params_of(48),
        cost_estimate=cost(4.3e9, 12e6),
        name="project_memory",
    )(info, par, x, *pieces)


def lane_ids(rows):
    return lax.broadcasted_iota(jnp.int32, (rows, 128), 1)


def split3(column):
    high = column.astype(BF)
    rest = column - high.astype(F32)
    middle = rest.astype(BF)
    return (high, middle, (rest - middle.astype(F32)).astype(BF))


def attend_kernel(causal, info, q_ref, k_ref, v_ref, o_ref, lse_ref):
    n, nk = q_ref.shape[0], k_ref.shape[0]
    pair = pl.program_id(0)
    lanes_k, lanes_q = lane_ids(nk), lane_ids(ROWS)
    lane_all = lane_ids(n)

    @pl.when(pair == 0)
    def _():
        lse_ref[...] = jnp.zeros(lse_ref.shape, F32)

    one = jnp.ones((), BF)
    zero = jnp.zeros((), BF)
    k_aug, v_aug = [], []
    for head in range(2):
        own = (lanes_k >= 64) if head else (lanes_k < 64)
        spare = 0 if head else 64
        keys = jnp.where(own, k_ref[...], zero)
        if not causal:
            place = lax.broadcasted_iota(jnp.int32, (nk, 128), 0)
            shut = jnp.where(place < info[4], 0.0, floor_score).astype(BF)
            keys = jnp.where(lanes_k == spare, shut, keys)
        k_aug.append(keys)
        v_aug.append(jnp.where(own, v_ref[...], jnp.where(lanes_k == spare, one, zero)))
    for first in range(0, n, ROWS):
        span = first + ROWS if causal else nk
        block = q_ref[first : first + ROWS, :]
        outs, lses = [], []
        for head in range(2):
            spare = 0 if head else 64
            query = block if causal else jnp.where(lanes_q == spare, one, block)
            scores = mm_nt(query, k_aug[head][:span])
            if causal:
                row = lax.broadcasted_iota(jnp.int32, (ROWS, ROWS), 0)
                col = lax.broadcasted_iota(jnp.int32, (ROWS, ROWS), 1)
                last = jnp.where(col <= row, scores[:, first:], floor_score)
                scores = jnp.concatenate([scores[:, :first], last], 1) if first else last
            highest = jnp.max(scores, -1, keepdims=True)
            raised = jnp.exp2(scores - highest).astype(BF)
            mixed = mm(raised, v_aug[head][:span])
            total = jnp.sum(jnp.where(lanes_q == spare, mixed, 0.0), -1, keepdims=True)
            outs.append(mixed * (1.0 / total))
            lses.append(highest + jnp.log2(total))
        o_ref[first : first + ROWS, :] = jnp.where(lanes_q < 64, outs[0], outs[1]).astype(BF)
        held = lse_ref[first : first + ROWS, :]
        held = jnp.where(lanes_q == 2 * pair, lses[0], held)
        lse_ref[first : first + ROWS, :] = jnp.where(lanes_q == 2 * pair + 1, lses[1], held)


def call_attend(info, q, k, v, causal):
    n, nk = q.shape[0], k.shape[0]
    part = 0.625 if causal else 1.0
    heads = lambda rows: pl.BlockSpec((rows, 128), lambda i, s: (0, i))
    return pl.pallas_call(
        partial(attend_kernel, causal),
        grid_spec=pltpu.PrefetchScalarGridSpec(
            num_scalar_prefetch=1,
            grid=(q.shape[1] // 128,),
            in_specs=[heads(n), heads(nk), heads(nk)],
            out_specs=[heads(n), pl.BlockSpec((n, 128), lambda i, s: (0, 0))],
        ),
        out_shape=[jax.ShapeDtypeStruct((n, 1024), BF), jax.ShapeDtypeStruct((n, 128), F32)],
        compiler_params=params_of(48),
        cost_estimate=cost(16e9 * part, 9e6, 17e6 * part),
        name="attend_self" if causal else "attend_cross",
    )(info, q, k, v)


def attend_back_kernel(causal, info, q_ref, k_ref, v_ref, o_ref, g_ref, lse_ref, dq_ref, dk_ref, dv_ref, bias_ref, acc):
    n, nk = q_ref.shape[0], k_ref.shape[0]
    pair = pl.program_id(0)
    lanes_k, lanes_q = lane_ids(nk), lane_ids(n)
    one = jnp.ones((), BF)
    zero = jnp.zeros((), BF)
    block_rows = 256
    q_all, g_all = q_ref[...], g_ref[...]
    product = g_all.astype(F32) * o_ref[...].astype(F32)
    sets = []
    for head in range(2):
        own_k = (lanes_k >= 64) if head else (lanes_k < 64)
        own_q = (lanes_q >= 64) if head else (lanes_q < 64)
        at = 0 if head else 64
        inner = jnp.sum(jnp.where(own_q, product, 0.0), -1, keepdims=True)
        lse = jnp.sum(jnp.where(lanes_q == 2 * pair + head, lse_ref[...], 0.0), -1, keepdims=True)
        q_own = jnp.where(own_q, q_all, zero)
        g_own = jnp.where(own_q, g_all, zero)
        q_aug, g_aug = q_own, g_own
        for step, (part_q, part_g) in enumerate(zip(split3(-lse), split3(-inner))):
            q_aug = jnp.where(lanes_q == at + step, part_q, q_aug)
            g_aug = jnp.where(lanes_q == at + step, part_g, g_aug)
        q_aug = jnp.where(lanes_q == at + 3, one, q_aug)
        ones_k = (lanes_k >= at) & (lanes_k < at + 3)
        k_own = jnp.where(own_k, k_ref[...], zero)
        k_aug = jnp.where(ones_k, one, k_own)
        if not causal:
            place = lax.broadcasted_iota(jnp.int32, (nk, 128), 0)
            shut = jnp.where(place < info[4], 0.0, floor_score).astype(BF)
            k_aug = jnp.where(lanes_k == at + 3, shut, k_aug)
        v_aug = jnp.where(ones_k, one, jnp.where(own_k, v_ref[...], zero))
        sets.append((q_own, g_own, q_aug, g_aug, k_own, k_aug, v_aug))
    for first in range(0, nk, block_rows):
        from_q = first if causal else 0
        dv = dk = None
        dq = None
        for head in range(2):
            q_own, g_own, q_aug, g_aug, k_own, k_aug, v_aug = sets[head]
            keys = slice(first, first + block_rows)
            scores = mm_nt(k_aug[keys], q_aug[from_q:])
            if causal:
                row = lax.broadcasted_iota(jnp.int32, (block_rows, block_rows), 0)
                col = lax.broadcasted_iota(jnp.int32, (block_rows, block_rows), 1)
                head_part = jnp.where(col >= row, scores[:, :block_rows], floor_score)
                if first + block_rows < n:
                    scores = jnp.concatenate([head_part, scores[:, block_rows:]], 1)
                else:
                    scores = head_part
            probs = jnp.exp2(scores)
            grad_probs = mm_nt(v_aug[keys], g_aug[from_q:])
            grad_scores = (probs * grad_probs).astype(BF)
            add_v = mm(probs.astype(BF), g_own[from_q:])
            add_k = mm(grad_scores, q_own[from_q:])
            add_q = mm_tn(grad_scores, k_own[keys])
            dv = add_v if dv is None else dv + add_v
            dk = add_k if dk is None else dk + add_k
            dq = add_q if dq is None else dq + add_q
        dv = dv.astype(BF)
        dv_ref[first : first + block_rows, :] = dv
        dk_ref[first : first + block_rows, :] = (dk * LN2).astype(BF)
        sums = row_sum(dv.astype(F32))
        if first == 0:
            acc[...] = dq
            bias_ref[1:2, :] = sums
        else:
            acc[from_q:, :] += dq
            bias_ref[1:2, :] += sums
    dq = acc[...].astype(BF) * jnp.asarray(0.125, BF)
    dq_ref[...] = dq
    bias_ref[0:1, :] = row_sum(dq.astype(F32))


def call_attend_back(info, q, k, v, o, g, lse, causal):
    n, nk = q.shape[0], k.shape[0]
    part = 0.625 if causal else 1.0
    heads = lambda rows: pl.BlockSpec((rows, 128), lambda i, s: (0, i))
    out = lambda rows: jax.ShapeDtypeStruct((rows, 1024), BF)
    return pl.pallas_call(
        partial(attend_back_kernel, causal),
        grid_spec=pltpu.PrefetchScalarGridSpec(
            num_scalar_prefetch=1,
            grid=(q.shape[1] // 128,),
            in_specs=[heads(n), heads(nk), heads(nk), heads(n), heads(n), pl.BlockSpec((n, 128), lambda i, s: (0, 0))],
            out_specs=[heads(n), heads(nk), heads(nk), heads(8)],
            scratch_shapes=[VM((n, 128), F32)],
        ),
        out_shape=[out(n), out(nk), out(nk), jax.ShapeDtypeStruct((8, 1024), F32)],
        compiler_params=params_of(56),
        cost_estimate=cost(40e9 * part, 20e6, 17e6 * part),
        name="attend_back_self" if causal else "attend_back_cross",
    )(info, q, k, v, o, g, lse)


def after_self_kernel(info, par, x_ref, o_ref, *rest):
    pieces, rest = rest[:8], rest[8:]
    h_ref, q_ref, nt_ref, wo, wq, sems = rest

    @pl.when(pl.program_id(0) == 0)
    def _():
        start_weight(info, pieces, "zxy", 1024, 512, wo, sems.at[0])
        start_weight(info, pieces, "zxy", 1536, 512, wq, sems.at[1])

    total = x_ref[...].astype(F32) + par[6:7, :]
    for slab in range(2):

        @pl.when(pl.program_id(0) == 0)
        def _():
            wait_weight(wo, sems.at[0], slab)

        total = total + mm_nt(o_ref[:, slab * 512 : slab * 512 + 512], wo[slab])
    h_ref[...] = total
    unit, _ = ln_parts(total)
    normed = (unit * par[1:2, :] + par[4:5, :]).astype(BF)
    nt_ref[...] = transposed(normed)
    for slab in range(2):

        @pl.when(pl.program_id(0) == 0)
        def _():
            wait_weight(wq, sems.at[1], slab)

        cols = slice(slab * 512, slab * 512 + 512)
        value = (mm(normed, wq[slab]) + par[11:12, cols]) * (0.125 * LOG2E)
        q_ref[:, cols] = value.astype(BF)


def call_after_self(info, par, x, o, pieces):
    n = x.shape[0]
    rows = pl.BlockSpec((ROWS, 1024), lambda i, s: (i, 0))
    return pl.pallas_call(
        after_self_kernel,
        grid_spec=pltpu.PrefetchScalarGridSpec(
            num_scalar_prefetch=1,
            grid=(n // ROWS,),
            in_specs=[pl.BlockSpec((24, 1024), lambda i, s: (0, 0)), rows, rows]
            + [pl.BlockSpec(memory_space=ANYM)] * 8,
            out_specs=[rows, rows, pl.BlockSpec((1024, ROWS), lambda i, s: (0, i))],
            scratch_shapes=[VM((2, 1024, 512), BF)] * 2 + [pltpu.SemaphoreType.DMA((2, 2))],
        ),
        out_shape=[
            jax.ShapeDtypeStruct((n, 1024), F32),
            jax.ShapeDtypeStruct((n, 1024), BF),
            jax.ShapeDtypeStruct((1024, n), BF),
        ],
        compiler_params=params_of(48),
        cost_estimate=cost(4.3e9, 16e6),
        name="after_self",
    )(info, par, x, o, *pieces)


def after_cross_kernel(info, par, scale, h_in, o_ref, cot_ref, *rest):
    pieces, rest = rest[:8], rest[8:]
    h_ref, n_ref, nt_ref, g_ref, gt_ref, gsum_ref, wo, sems = rest
    step = pl.program_id(0)

    @pl.when(step == 0)
    def _():
        start_weight(info, pieces, "zxy", 2048, 512, wo, sems)

    place = step * ROWS + lax.broadcasted_iota(jnp.int32, (ROWS, 1), 0)
    weight = jnp.where(place < info[5], scale[0, 0], 0.0)
    grad = cot_ref[...].astype(F32) * weight
    rounded = grad.astype(BF)
    g_ref[...] = rounded
    gt_ref[...] = transposed(rounded)
    sums = row_sum(grad)

    @pl.when(step == 0)
    def _():
        gsum_ref[...] = jnp.zeros(gsum_ref.shape, F32)

    gsum_ref[0:1, :] += sums
    total = h_in[...] + par[7:8, :]
    for slab in range(2):

        @pl.when(step == 0)
        def _():
            wait_weight(wo, sems, slab)

        total = total + mm_nt(o_ref[:, slab * 512 : slab * 512 + 512], wo[slab])
    h_ref[...] = total
    unit, _ = ln_parts(total)
    normed = (unit * par[2:3, :] + par[5:6, :]).astype(BF)
    n_ref[...] = normed
    nt_ref[...] = transposed(normed)


def call_after_cross(info, par, scale, h, o, cot, pieces):
    n = h.shape[0]
    rows = pl.BlockSpec((ROWS, 1024), lambda i, s: (i, 0))
    turned = pl.BlockSpec((1024, ROWS), lambda i, s: (0, i))
    act = jax.ShapeDtypeStruct((n, 1024), BF)
    act_t = jax.ShapeDtypeStruct((1024, n), BF)
    return pl.pallas_call(
        after_cross_kernel,
        grid_spec=pltpu.PrefetchScalarGridSpec(
            num_scalar_prefetch=1,
            grid=(n // ROWS,),
            in_specs=[
                pl.BlockSpec((24, 1024), lambda i, s: (0, 0)),
                pl.BlockSpec((8, 128), lambda i, s: (0, 0)),
                rows,
                rows,
                rows,
            ]
            + [pl.BlockSpec(memory_space=ANYM)] * 8,
            out_specs=[rows, rows, turned, rows, turned, pl.BlockSpec((8, 1024), lambda i, s: (0, 0))],
            scratch_shapes=[VM((2, 1024, 512), BF), pltpu.SemaphoreType.DMA((2,))],
        ),
        out_shape=[
            jax.ShapeDtypeStruct((n, 1024), F32),
            act,
            act_t,
            act,
            act_t,
            jax.ShapeDtypeStruct((8, 1024), F32),
        ],
        compiler_params=params_of(48),
        cost_estimate=cost(2.2e9, 26e6),
        name="after_cross",
    )(info, par, scale, h, o, cot, *pieces)


GELU_A = 0.7978845608028654
GELU_B = 0.044715


def store_blocks(info, temp, send_ref, keep_ref, zrel, kind, width):
    for yrel in range(2):
        yy = info[1] if yrel == 0 else 1 - info[1]
        for crel in range(2):
            cc = info[2] if crel == 0 else 1 - info[2]
            row = pl.multiple_of(yy * 128 + cc * 64, 64)
            block = temp[pl.ds(row, 64), :]
            target = send_ref if crel else keep_ref
            if kind == "zxy":
                target[yrel, 0, zrel, :, :] = block
            else:
                target[zrel, yrel, 0, :, :] = block


FFB = 512


def ffn_kernel(info, par, bias_ref, n_ref, nt_ref, g_ref, gt_ref, h_ref, *rest):
    pieces_in, pieces_out, rest = rest[:8], rest[8:16], rest[16:]
    (out_ref, dn_ref, send_in, keep_in, send_out, keep_out, dbias_ref, w_in, w_out, acc, active, du, temp, sems) = rest
    half, part = pl.program_id(0), pl.program_id(1)
    parts = pl.num_programs(1)
    n = n_ref.shape[0]
    slab = lax.rem(half + info[3], 2)
    first_step = (half == 0) & (part == 0)

    @pl.when(first_step)
    def _():
        start_weight(info, pieces_in, "zxy", 0, 2048, w_in, sems.at[0])
        start_weight(info, pieces_out, "xyz", 0, 2048, w_out, sems.at[1])

    @pl.when(part == 0)
    def _():
        wait_weight(w_in, sems.at[0], slab)
        wait_weight(w_out, sems.at[1], slab)

    cols = pl.ds(pl.multiple_of(part * FFB, FFB), FFB)
    first = w_in.at[slab, :, cols]
    second = w_out.at[slab, :, cols]
    total_bias = None
    for chunk in range(n // ROWS):
        rows = slice(chunk * ROWS, chunk * ROWS + ROWS)
        u = mm(n_ref[rows, :], first[...]) + bias_ref[0:1, :]
        square = u * u
        bend = jnp.tanh(u * (GELU_A + GELU_A * GELU_B * square))
        half_up = 0.5 + 0.5 * bend
        r = (u * half_up).astype(BF)
        active[rows, :] = r
        slope = half_up + 0.5 * u * (1.0 - bend * bend) * (GELU_A + 3.0 * GELU_A * GELU_B * square)
        dr = mm(g_ref[rows, :], second[...])
        d = (dr * slope).astype(BF)
        du[rows, :] = d
        sums = row_sum(d.astype(F32))
        total_bias = sums if total_bias is None else total_bias + sums
        up = mm_nt(r, second[...])
        down = mm_nt(d, first[...])

        @pl.when(first_step)
        def _():
            acc[rows, :] = up
            dn_ref[rows, :] = down

        @pl.when(jnp.logical_not(first_step))
        def _():
            acc[rows, :] += up
            dn_ref[rows, :] += down

    dbias_ref[0:1, :] = total_bias
    for zrel in range(4):
        zz = lax.rem(info[0] + zrel, 4)
        rows = pl.ds(pl.multiple_of(zz * 256, 256), 256)
        temp[...] = mm(nt_ref[rows, :], du[...]).astype(BF)
        store_blocks(info, temp, send_in, keep_in, zrel, "zxy", FFB)
        temp[...] = mm(gt_ref[rows, :], active[...]).astype(BF)
        store_blocks(info, temp, send_out, keep_out, zrel, "xyz", FFB)

    @pl.when((half == 1) & (part == parts - 1))
    def _():
        for chunk in range(n // ROWS):
            rows = slice(chunk * ROWS, chunk * ROWS + ROWS)
            out_ref[rows, :] = (h_ref[rows, :] + acc[rows, :] + par[8:9, :]).astype(BF)


def block_out(kind, width, total):
    if kind == "zxy":
        shape, block = (2, 2, 4, 64, total), (2, 1, 4, 64, width)
        spec = lambda index: pl.BlockSpec(block, index(lambda x, t: (0, x, 0, 0, t)))
    else:
        shape, block = (4, 2, 2, 64, total), (4, 2, 1, 64, width)
        spec = lambda index: pl.BlockSpec(block, index(lambda x, t: (0, 0, x, 0, t)))
    return (jax.ShapeDtypeStruct(shape, BF), spec)


def call_ffn(info, par, bias, normed, normed_t, grad, grad_t, hidden, pieces_in, pieces_out):
    n = normed.shape[0]
    parts = 2048 // FFB
    whole = lambda shape: pl.BlockSpec(shape, lambda x, t, s: (0, 0))
    shape_in, spec_in = block_out("zxy", FFB, 2048)
    shape_out, spec_out = block_out("xyz", FFB, 2048)
    index = lambda f: (lambda x, t, s: f(x, t))
    bias_spec = lambda rows: pl.BlockSpec((rows, FFB), lambda x, t, s: (0, lax.rem(x + s[3], 2) * parts + t))
    return pl.pallas_call(
        ffn_kernel,
        grid_spec=pltpu.PrefetchScalarGridSpec(
            num_scalar_prefetch=1,
            grid=(2, parts),
            in_specs=[
                whole((24, 1024)),
                bias_spec(8),
                whole((n, 1024)),
                whole((1024, n)),
                whole((n, 1024)),
                whole((1024, n)),
                whole((n, 1024)),
            ]
            + [pl.BlockSpec(memory_space=ANYM)] * 16,
            out_specs=[
                whole((n, 1024)),
                whole((n, 1024)),
                spec_in(index),
                spec_in(index),
                spec_out(index),
                spec_out(index),
                bias_spec(8),
            ],
            scratch_shapes=[
                VM((2, 1024, 2048), BF),
                VM((2, 1024, 2048), BF),
                VM((n, 1024), F32),
                VM((n, FFB), BF),
                VM((n, FFB), BF),
                VM((256, FFB), BF),
                pltpu.SemaphoreType.DMA((2, 2)),
            ],
        ),
        out_shape=[
            jax.ShapeDtypeStruct((n, 1024), BF),
            jax.ShapeDtypeStruct((n, 1024), F32),
            shape_in,
            shape_in,
            shape_out,
            shape_out,
            jax.ShapeDtypeStruct((8, 4096), F32),
        ],
        compiler_params=params_of(60),
        cost_estimate=cost(51.5e9, 60e6, 4e6),
        name="feedforward",
    )(info, par, bias, normed, normed_t, grad, grad_t, hidden, *pieces_in, *pieces_out)


def back_three_kernel(info, par, dn_ref, h_ref, g_ref, *rest):
    pieces, rest = rest[:8], rest[8:]
    dh_ref, do_ref, gt_ref, sum_ref, wo, sems = rest
    step = pl.program_id(0)

    @pl.when(step == 0)
    def _():
        start_weight(info, pieces, "zxy", 2048, 512, wo, sems)
        sum_ref[...] = jnp.zeros(sum_ref.shape, F32)

    back_rows(par, 2, dn_ref[...], h_ref[...], g_ref[...].astype(F32), dh_ref, gt_ref, sum_ref, do_ref, wo, sems)


def back_rows(par, index, dn, hidden, residual, dh_ref, gt_ref, sum_ref, do_ref, wo, sems):
    unit, inverse = ln_parts(hidden)
    grad = residual + ln_back(dn, par[index : index + 1, :], unit, inverse)
    dh_ref[...] = grad
    sum_ref[0:1, :] += row_sum(dn * unit)
    sum_ref[1:2, :] += row_sum(dn)
    sum_ref[2:3, :] += row_sum(grad)
    rounded = grad.astype(BF)
    gt_ref[...] = transposed(rounded)
    for slab in range(2):

        @pl.when(pl.program_id(0) == 0)
        def _():
            wait_weight(wo, sems, slab)

        do_ref[:, slab * 512 : slab * 512 + 512] = mm(rounded, wo[slab]).astype(BF)


def call_back_three(info, par, dn, h, g, pieces):
    n = h.shape[0]
    rows = pl.BlockSpec((ROWS, 1024), lambda i, s: (i, 0))
    return pl.pallas_call(
        back_three_kernel,
        grid_spec=pltpu.PrefetchScalarGridSpec(
            num_scalar_prefetch=1,
            grid=(n // ROWS,),
            in_specs=[pl.BlockSpec((24, 1024), lambda i, s: (0, 0)), rows, rows, rows]
            + [pl.BlockSpec(memory_space=ANYM)] * 8,
            out_specs=[
                rows,
                rows,
                pl.BlockSpec((1024, ROWS), lambda i, s: (0, i)),
                pl.BlockSpec((8, 1024), lambda i, s: (0, 0)),
            ],
            scratch_shapes=[VM((2, 1024, 512), BF), pltpu.SemaphoreType.DMA((2,))],
        ),
        out_shape=[
            jax.ShapeDtypeStruct((n, 1024), F32),
            jax.ShapeDtypeStruct((n, 1024), BF),
            jax.ShapeDtypeStruct((1024, n), BF),
            jax.ShapeDtypeStruct((8, 1024), F32),
        ],
        compiler_params=params_of(48),
        cost_estimate=cost(2.2e9, 20e6),
        name="back_three",
    )(info, par, dn, h, g, *pieces)


def back_two_kernel(info, par, dq_ref, h_ref, dh2_ref, *rest):
    pieces, rest = rest[:8], rest[8:]
    dh_ref, do_ref, gt_ref, sum_ref, wq, wo, sems = rest
    step = pl.program_id(0)

    @pl.when(step == 0)
    def _():
        start_weight(info, pieces, "zxy", 1536, 512, wq, sems.at[0])
        start_weight(info, pieces, "zxy", 1024, 512, wo, sems.at[1])
        sum_ref[...] = jnp.zeros(sum_ref.shape, F32)

    dn = None
    for slab in range(2):

        @pl.when(step == 0)
        def _():
            wait_weight(wq, sems.at[0], slab)

        term = mm_nt(dq_ref[:, slab * 512 : slab * 512 + 512], wq[slab])
        dn = term if dn is None else dn + term
    back_rows(par, 1, dn, h_ref[...], dh2_ref[...], dh_ref, gt_ref, sum_ref, do_ref, wo, sems.at[1])


def call_back_two(info, par, dq, h, dh2, pieces):
    n = h.shape[0]
    rows = pl.BlockSpec((ROWS, 1024), lambda i, s: (i, 0))
    return pl.pallas_call(
        back_two_kernel,
        grid_spec=pltpu.PrefetchScalarGridSpec(
            num_scalar_prefetch=1,
            grid=(n // ROWS,),
            in_specs=[pl.BlockSpec((24, 1024), lambda i, s: (0, 0)), rows, rows, rows]
            + [pl.BlockSpec(memory_space=ANYM)] * 8,
            out_specs=[
                rows,
                rows,
                pl.BlockSpec((1024, ROWS), lambda i, s: (0, i)),
                pl.BlockSpec((8, 1024), lambda i, s: (0, 0)),
            ],
            scratch_shapes=[VM((2, 1024, 512), BF)] * 2 + [pltpu.SemaphoreType.DMA((2, 2))],
        ),
        out_shape=[
            jax.ShapeDtypeStruct((n, 1024), F32),
            jax.ShapeDtypeStruct((n, 1024), BF),
            jax.ShapeDtypeStruct((1024, n), BF),
            jax.ShapeDtypeStruct((8, 1024), F32),
        ],
        compiler_params=params_of(48),
        cost_estimate=cost(4.3e9, 24e6),
        name="back_two",
    )(info, par, dq, h, dh2, *pieces)


def memory_back_kernel(info, dk_ref, dv_ref, *rest):
    pieces, rest = rest[:8], rest[8:]
    out_ref, wk, wv, sems = rest

    @pl.when(pl.program_id(0) == 0)
    def _():
        start_weight(info, pieces, "zxy", 0, 512, wk, sems.at[0])
        start_weight(info, pieces, "zxy", 512, 512, wv, sems.at[1])

    total = None
    for t, (ref, weight) in enumerate(((dk_ref, wk), (dv_ref, wv))):
        for slab in range(2):

            @pl.when(pl.program_id(0) == 0)
            def _():
                wait_weight(weight, sems.at[t], slab)

            term = mm_nt(ref[:, slab * 512 : slab * 512 + 512], weight[slab])
            total = term if total is None else total + term
    out_ref[...] = total.astype(BF)


def call_memory_back(info, dk, dv, pieces):
    n = dk.shape[0]
    rows = pl.BlockSpec((ROWS, 1024), lambda i, s: (i, 0))
    return pl.pallas_call(
        memory_back_kernel,
        grid_spec=pltpu.PrefetchScalarGridSpec(
            num_scalar_prefetch=1,
            grid=(n // ROWS,),
            in_specs=[rows, rows] + [pl.BlockSpec(memory_space=ANYM)] * 8,
            out_specs=rows,
            scratch_shapes=[VM((2, 1024, 512), BF)] * 2 + [pltpu.SemaphoreType.DMA((2, 2))],
        ),
        out_shape=jax.ShapeDtypeStruct((n, 1024), BF),
        compiler_params=params_of(48),
        cost_estimate=cost(4.3e9, 12e6),
        name="memory_back",
    )(info, dk, dv, *pieces)


def back_one_kernel(info, par, dq_ref, dk_ref, dv_ref, x_ref, dh1_ref, *rest):
    pieces, rest = rest[:24], rest[24:]
    out_ref, sum_ref, wq, wk, wv, sems = rest
    weights = (wq, wk, wv)
    step = pl.program_id(0)

    @pl.when(step == 0)
    def _():
        for t in range(3):
            start_weight(info, pieces[8 * t : 8 * t + 8], KINDS[t], 0, 512, weights[t], sems.at[t])
        sum_ref[...] = jnp.zeros(sum_ref.shape, F32)

    dn = None
    for t, ref in enumerate((dq_ref, dk_ref, dv_ref)):
        for slab in range(2):

            @pl.when(step == 0)
            def _():
                wait_weight(weights[t], sems.at[t], slab)

            term = mm_nt(ref[:, slab * 512 : slab * 512 + 512], weights[t][slab])
            dn = term if dn is None else dn + term
    unit, inverse = ln_parts(x_ref[...].astype(F32))
    grad = dh1_ref[...] + ln_back(dn, par[0:1, :], unit, inverse)
    out_ref[...] = grad.astype(BF)
    sum_ref[0:1, :] += row_sum(dn * unit)
    sum_ref[1:2, :] += row_sum(dn)


def call_back_one(info, par, dq, dk, dv, x, dh1, pieces):
    n = x.shape[0]
    rows = pl.BlockSpec((ROWS, 1024), lambda i, s: (i, 0))
    return pl.pallas_call(
        back_one_kernel,
        grid_spec=pltpu.PrefetchScalarGridSpec(
            num_scalar_prefetch=1,
            grid=(n // ROWS,),
            in_specs=[pl.BlockSpec((24, 1024), lambda i, s: (0, 0)), rows, rows, rows, rows, rows]
            + [pl.BlockSpec(memory_space=ANYM)] * 24,
            out_specs=[rows, pl.BlockSpec((8, 1024), lambda i, s: (0, 0))],
            scratch_shapes=[VM((2, 1024, 512), BF)] * 3 + [pltpu.SemaphoreType.DMA((3, 2))],
        ),
        out_shape=[jax.ShapeDtypeStruct((n, 1024), BF), jax.ShapeDtypeStruct((8, 1024), F32)],
        compiler_params=params_of(48),
        cost_estimate=cost(6.4e9, 20e6),
        name="back_one",
    )(info, par, dq, dk, dv, x, dh1, *pieces)


def weight_grad_kernel(kind, picks, count, info, *refs):
    lefts, rights = refs[:count], refs[count : count + len(picks)]
    send_ref, keep_ref, temp = refs[count + len(picks) :]
    for t, pick in enumerate(picks):

        @pl.when(pl.program_id(1) == t)
        def _():
            for zrel in range(4):
                zz = lax.rem(info[0] + zrel, 4)
                rows = pl.ds(pl.multiple_of(zz * 256, 256), 256)
                temp[...] = mm(lefts[pick][rows, :], rights[t][...]).astype(BF)
                store_blocks(info, temp, send_ref, keep_ref, zrel, kind, 512)


def call_weight_grad(info, kind, lefts, rights, picks, name):
    n = rights[0].shape[0]
    shape, spec = block_out(kind, 512, 512 * len(rights))
    index = lambda f: (lambda x, t, s: f(x, t))
    return pl.pallas_call(
        partial(weight_grad_kernel, kind, picks, len(lefts)),
        grid_spec=pltpu.PrefetchScalarGridSpec(
            num_scalar_prefetch=1,
            grid=(2, len(rights)),
            in_specs=[pl.BlockSpec((1024, n), lambda x, t, s: (0, 0))] * len(lefts)
            + [pl.BlockSpec((n, 512), lambda x, t, s: (0, lax.rem(x + s[3], 2)))] * len(rights),
            out_specs=[spec(index), spec(index)],
            scratch_shapes=[VM((256, 512), BF)],
        ),
        out_shape=[shape, shape],
        compiler_params=params_of(48),
        cost_estimate=cost(2.15e9 * len(rights), 4e6 * len(rights) + 2e6 * len(lefts)),
        name=name,
    )(info, *lefts, *rights)


def along(axis_bit):
    return [(i, i ^ axis_bit) for i in range(16)]


RING = [(i, (i + 4) % 16) for i in range(16)]


def swap_x(value):
    return lax.ppermute(value, "mp", [(0, 1), (1, 0)])


def swap_y(value):
    return lax.ppermute(value, "dp", along(2))


def swap_core(value):
    return lax.ppermute(value, "dp", along(1))


def next_z(value):
    return lax.ppermute(value, "dp", RING)


def gather_flow(shard, kind):
    if kind == "zxy":
        one = next_z(shard)
        two = next_z(one)
        three = next_z(two)
        base = jnp.stack([shard, one, two, three])
        over_x = swap_x(base)
        quads = [base, over_x, swap_y(base), swap_y(over_x)]
    else:
        over_x = swap_x(shard)
        base = jnp.stack([shard, over_x, swap_y(shard), swap_y(over_x)])
        one = next_z(base)
        two = next_z(one)
        quads = [base, one, two, next_z(two)]
    return quads + [swap_core(quad) for quad in quads]


def join(kept, received):
    return (kept.astype(F32) + received.astype(F32)).astype(kept.dtype)


def reduce_ring(parts):
    moving = next_z(parts[3])
    moving = next_z(join(parts[2], moving))
    moving = next_z(join(parts[1], moving))
    return (parts[0], moving)


def reduce_flow(send, keep, kind):
    received = swap_core(send)
    if kind == "zxy":
        arrived = swap_y(join(keep[1], received[1]))
        kept = join(keep[0], received[0])
        across = swap_x(join(kept[1], arrived[1]))
        kept = join(kept[0], arrived[0])
        parts = [join(kept[k], across[k]) for k in range(4)]
        last, moving = reduce_ring(parts)
        return last.astype(F32) + moving.astype(F32)
    parts = [join(keep[k], received[k]) for k in range(4)]
    last, moving = reduce_ring(parts)
    whole = join(last, moving)
    arrived = swap_y(whole[1])
    kept = join(whole[0], arrived)
    return kept[0].astype(F32) + swap_x(kept[1]).astype(F32)


def join_halves(mine, other, me):
    return jnp.where(me == 0, jnp.concatenate([mine, other], 0), jnp.concatenate([other, mine], 0))


def whole_sequence(local, me):
    mine = lax.dynamic_index_in_dim(local, me, 1, keepdims=False)
    theirs = lax.dynamic_index_in_dim(local, 1 - me, 1, keepdims=False)
    return join_halves(mine, swap_x(theirs), me)


def both_sequences(whole, me):
    half = whole.shape[0] // 2
    mine = lax.dynamic_slice_in_dim(whole, me * half, half, 0)
    theirs = lax.dynamic_slice_in_dim(whole, (1 - me) * half, half, 0)
    other = swap_x(theirs)
    return jnp.where(me == 0, jnp.stack([mine, other], 1), jnp.stack([other, mine], 1))


def own_first(values, dp, me):
    rest = values.shape[2:]
    v = values.reshape((4, 2, 2, 2) + rest)
    z, y, c = dp // 4, (dp // 2) % 2, dp % 2
    v = lax.dynamic_slice_in_dim(jnp.concatenate([v, v], 0), z, 4, 0)
    v = jnp.where(y == 1, v[:, ::-1], v)
    v = jnp.where(c == 1, v[:, :, ::-1], v)
    v = jnp.where(me == 1, v[:, :, :, ::-1], v)
    return jnp.transpose(v, (2, 1, 3, 0) + tuple(range(4, v.ndim)))


def one_sequence_body(
    tokens,
    memory,
    cotangent,
    lengths,
    memory_lengths,
    pair_ids,
    pair_counts,
    self_in,
    self_out,
    cross_in,
    cross_out,
    fc_in,
    fc_out,
    head_biases,
    inner_bias,
    norm_gains,
    feature_biases,
):
    dp, me = lax.axis_index("dp"), lax.axis_index("mp")
    own_length = lax.dynamic_index_in_dim(lengths, me, 0, keepdims=False)
    own_memory = lax.dynamic_index_in_dim(memory_lengths, me, 0, keepdims=False)
    info = jnp.stack([dp // 4, (dp // 2) % 2, dp % 2, me, own_memory, own_length, dp, dp]).astype(jnp.int32)
    counts = pair_counts.astype(F32)
    matches = (pair_ids[:, None] == jnp.arange(counts.shape[0], dtype=jnp.int32)[None, :]).astype(F32)
    scales = jnp.mean(counts) / jnp.sum(matches * counts[None, :], -1)
    scale = jnp.broadcast_to(lax.dynamic_index_in_dim(scales, me, 0, keepdims=False), (8, 128))

    small = jnp.concatenate(
        [
            norm_gains.reshape(-1),
            feature_biases.reshape(-1),
            head_biases.astype(F32).reshape(-1),
            inner_bias.astype(F32).reshape(-1),
        ]
    )
    small = lax.all_gather(small, ("dp", "mp"), axis=0, tiled=False)
    gains = small[:, :96].reshape(32, 3, 32).transpose(1, 0, 2).reshape(3, 1024)
    shifts = small[:, 96:288].reshape(32, 6, 32).transpose(1, 0, 2).reshape(6, 1024)
    heads = small[:, 288:416].reshape(16, 2, 4, 8, 4).transpose(2, 1, 3, 0, 4).reshape(4, 1024)
    inner = small[:, 416:544].reshape(16, 2, 8, 16).transpose(1, 2, 0, 3).reshape(1, 4096)
    par = jnp.concatenate([gains, shifts, heads, jnp.zeros((11, 1024), F32)], 0)
    inner = jnp.broadcast_to(inner, (8, 4096))

    x = whole_sequence(tokens, me)
    w_self = [gather_flow(self_in[t], KINDS[t]) for t in range(3)]
    pieces_self = [piece for flow in w_self for piece in flow]
    mixed_shard = jnp.concatenate([cross_in[1], cross_in[2], self_out.T, cross_in[0], cross_out.T], 1)
    w_mid = gather_flow(mixed_shard, "zxy")
    mem = whole_sequence(memory, me)
    w_in = gather_flow(fc_in, "zxy")
    w_out = gather_flow(fc_out.T, "xyz")
    cot = whole_sequence(cotangent, me)

    q1, k1, v1, n1_t = call_qkv(info, par, x, pieces_self)
    o1, lse1 = call_attend(info, q1, k1, v1, True)
    k2, v2, mem_t = call_kv(info, par, mem, w_mid)
    h1, q2, n2_t = call_after_self(info, par, x, o1, w_mid)
    o2, lse2 = call_attend(info, q2, k2, v2, False)
    h2, n3, n3_t, g3, g3_t, g_sum = call_after_cross(info, par, scale, h1, o2, cot, w_mid)
    out, dn3, send_in, keep_in, send_out, keep_out, d_inner = call_ffn(
        info, par, inner, n3, n3_t, g3, g3_t, h2, w_in, w_out
    )
    output = both_sequences(out, me)
    sum_fc_in = reduce_flow(send_in, keep_in, "zxy")
    sum_fc_out = reduce_flow(send_out, keep_out, "xyz")
    dh2, do2, g2_t, sums3 = call_back_three(info, par, dn3, h2, g3, w_mid)
    dq2, dk2, dv2, bias2 = call_attend_back(info, q2, k2, v2, o2, do2, lse2, False)
    grad_memory = both_sequences(call_memory_back(info, dk2, dv2, w_mid), me).astype(F32)
    cross_grads = call_weight_grad(
        info, "zxy", [mem_t, n2_t, g2_t], [dk2, dv2, dq2, o2], (0, 0, 1, 2), "weight_grad_cross"
    )
    sum_cross = reduce_flow(*cross_grads, "zxy")
    dh1, do1, g1_t, sums2 = call_back_two(info, par, dq2, h1, dh2, w_mid)
    dq1, dk1, dv1, bias1 = call_attend_back(info, q1, k1, v1, o1, do1, lse1, True)
    self_grads = call_weight_grad(info, "zxy", [n1_t, g1_t], [dq1, dk1, dv1, o1], (0, 0, 0, 1), "weight_grad_self")
    sum_self = reduce_flow(*self_grads, "zxy")
    grad_x, sums1 = call_back_one(info, par, dq1, dk1, dv1, x, dh1, pieces_self)
    grad_tokens = both_sequences(grad_x, me).astype(F32)

    d_gains = jnp.stack([sums1[0], sums2[0], sums3[0]])
    d_shifts = jnp.stack([sums1[1], sums2[1], sums3[1], sums2[2], sums3[2], g_sum[0]])
    d_heads = jnp.concatenate([bias1[:2], bias2[:2]], 0)
    d_small = jnp.concatenate(
        [
            d_gains.reshape(3, 32, 32).transpose(1, 0, 2).reshape(32, 96),
            d_shifts.reshape(6, 32, 32).transpose(1, 0, 2).reshape(32, 192),
            d_heads.reshape(4, 2, 8, 16, 4).transpose(3, 1, 0, 2, 4).reshape(32, 128),
            d_inner[0].reshape(2, 8, 16, 16).transpose(2, 0, 1, 3).reshape(32, 128),
        ],
        1,
    )
    d_small = own_first(d_small.reshape(16, 2, 544), dp, me)
    total = reduce_flow(d_small[1], d_small[0], "zxy")
    return (
        output,
        grad_tokens,
        grad_memory,
        jnp.stack([sum_self[:, :512], sum_self[:, 512:1024], sum_self[:, 1024:1536]]),
        sum_self[:, 1536:].T,
        jnp.stack([sum_cross[:, 1024:1536], sum_cross[:, :512], sum_cross[:, 512:1024]]),
        sum_cross[:, 1536:].T,
        sum_fc_in,
        sum_fc_out.T,
        total[288:416].reshape(4, 8, 4),
        total[416:].reshape(8, 16),
        total[:96].reshape(3, 32),
        total[96:288].reshape(6, 32),
    )


def solution(mesh):
    in_specs = (
        P("mp", "dp", None),
        P("mp", "dp", None),
        P("mp", "dp", None),
        P("dp"),
        P("dp"),
        P("dp"),
        P(),
        P(None, "dp", "mp"),
        P("mp", "dp"),
        P(None, "dp", "mp"),
        P("mp", "dp"),
        P("dp", "mp"),
        P("mp", "dp"),
        P(None, "mp", "dp"),
        P("mp", "dp"),
        P(None, ("dp", "mp")),
        P(None, ("dp", "mp")),
    )
    out_specs = (
        P("mp", "dp", None),
        P("mp", "dp", None),
        P("mp", "dp", None),
        P(None, "dp", "mp"),
        P("mp", "dp"),
        P(None, "dp", "mp"),
        P("mp", "dp"),
        P("dp", "mp"),
        P("mp", "dp"),
        P(None, "mp", "dp"),
        P("mp", "dp"),
        P(None, ("dp", "mp")),
        P(None, ("dp", "mp")),
    )
    sizes = dict(mesh.shape)
    chosen = one_sequence_body if (sizes["dp"], sizes["mp"]) == (16, 2) else body
    return jax.shard_map(chosen, mesh=mesh, in_specs=in_specs, out_specs=out_specs, check_vma=False)
```

```python
from functools import partial

import jax
import jax.numpy as jnp
from jax import lax
from jax.experimental import pallas as pl
from jax.experimental.pallas import tpu as pltpu
from jax.sharding import PartitionSpec as P

eps = 1e-05
floor_score = -1e30


def smooth_unit(values):
    return jax.nn.gelu(values, approximate=True)


def normalize(hidden, gain, shift):
    average = jnp.mean(hidden, -1, keepdims=True)
    centred = hidden - average
    inverse = lax.rsqrt(jnp.mean(centred * centred, -1, keepdims=True) + eps)
    unit = centred * inverse
    return (unit * gain + shift, unit, inverse)


def normalize_back(grad_normed, gain, unit, inverse):
    grad_unit = grad_normed * gain
    grad_hidden = inverse * (
        grad_unit
        - jnp.mean(grad_unit, -1, keepdims=True)
        - unit * jnp.mean(grad_unit * unit, -1, keepdims=True)
    )
    return (grad_hidden, jnp.sum(grad_normed * unit, (0, 1)), jnp.sum(grad_normed, (0, 1)))


def masked_scores(rows, keys, first, limit, causal):
    scores = jnp.einsum("qhd,khd->hqk", rows, keys, preferred_element_type=jnp.float32)
    key_place = jnp.arange(keys.shape[0], dtype=jnp.int32)[None, :]
    if causal:
        allowed = key_place <= first + jnp.arange(rows.shape[0], dtype=jnp.int32)[:, None]
    else:
        allowed = key_place < limit
    return jnp.where(allowed[None], scores, floor_score)


def attend_forward(queries, keys, values, limit, causal):
    length = queries.shape[0]
    block = min(512, length)
    outputs = []
    totals = []
    for first in range(0, length, block):
        span = first + block if causal else keys.shape[0]
        scores = masked_scores(queries[first : first + block], keys[:span], first, limit, causal)
        highest = jnp.max(scores, -1, keepdims=True)
        raised = jnp.exp(scores - highest)
        total = jnp.sum(raised, -1, keepdims=True)
        probs = (raised / total).astype(jnp.bfloat16)
        outputs.append(
            jnp.einsum("hqk,khd->qhd", probs, values[:span], preferred_element_type=jnp.float32)
        )
        totals.append((highest + jnp.log(total))[:, :, 0])
    return (jnp.concatenate(outputs, 0), jnp.concatenate(totals, 1))


def attend_backward(queries, keys, values, totals, grad_mixed, limit, causal):
    length = queries.shape[0]
    block = min(512, length)
    key_grads = jnp.zeros(keys.shape, jnp.float32)
    value_grads = jnp.zeros(values.shape, jnp.float32)
    query_grads = []
    for first in range(0, length, block):
        span = first + block if causal else keys.shape[0]
        rows = queries[first : first + block]
        grad_piece = grad_mixed[first : first + block]
        scores = masked_scores(rows, keys[:span], first, limit, causal)
        probs = jnp.exp(scores - totals[:, first : first + block, None])
        grad_probs = jnp.einsum(
            "qhd,khd->hqk", grad_piece, values[:span], preferred_element_type=jnp.float32
        )
        inner_sum = jnp.sum(probs * grad_probs, -1, keepdims=True)
        grad_scores = (probs * (grad_probs - inner_sum)).astype(jnp.bfloat16)
        query_grads.append(
            jnp.einsum("hqk,khd->qhd", grad_scores, keys[:span], preferred_element_type=jnp.float32)
        )
        key_grads = key_grads.at[:span].add(
            jnp.einsum("hqk,qhd->khd", grad_scores, rows, preferred_element_type=jnp.float32)
        )
        value_grads = value_grads.at[:span].add(
            jnp.einsum(
                "hqk,qhd->khd",
                probs.astype(jnp.bfloat16),
                grad_piece,
                preferred_element_type=jnp.float32,
            )
        )
    return (jnp.concatenate(query_grads, 0), key_grads, value_grads)


def run_forward(operands, causal):
    return attend_forward(operands[0], operands[1], operands[2], operands[3], causal)


def run_backward(operands, causal):
    return attend_backward(
        operands[0], operands[1], operands[2], operands[3], operands[4], operands[5], causal
    )


def gather_rows(normed):
    return lax.all_gather(normed, "mp", axis=0, tiled=True)


def spread_rows(term_fn, rows):
    return lax.psum_scatter(
        term_fn(jnp.int32(0), lax.axis_size("mp") * rows).astype(jnp.bfloat16),
        "mp",
        scatter_dimension=0,
        tiled=True,
    ).astype(jnp.float32)


def whole_rows(term_fn, local, start_row):
    full_rows = local.shape[0] * lax.axis_size("mp")
    term = term_fn(0, full_rows)
    placed = lax.dynamic_update_slice_in_dim(jnp.zeros_like(term), local, start_row, 0)
    return lax.psum((term + placed).astype(jnp.bfloat16), "mp").astype(jnp.float32)


def gather_grads(grad_branch):
    return lax.all_gather(grad_branch, "mp", axis=0, tiled=True)


def reduce_inputs(term_fn, rows):
    return lax.psum_scatter(
        term_fn(jnp.int32(0), lax.axis_size("mp") * rows).astype(jnp.bfloat16),
        "mp",
        scatter_dimension=0,
        tiled=True,
    ).astype(jnp.float32)


def body(
    tokens,
    memory,
    cotangent,
    lengths,
    memory_lengths,
    pair_ids,
    pair_counts,
    self_in,
    self_out,
    cross_in,
    cross_out,
    fc_in,
    fc_out,
    head_biases,
    inner_bias,
    norm_gains,
    feature_biases,
):
    shards = (self_in, self_out, cross_in, cross_out, fc_in, fc_out, head_biases, inner_bias)
    gathered = (
        lax.all_gather(shards[0], "dp", axis=1, tiled=True),
        lax.all_gather(shards[1], "dp", axis=1, tiled=True),
        lax.all_gather(shards[2], "dp", axis=1, tiled=True),
        lax.all_gather(shards[3], "dp", axis=1, tiled=True),
        lax.all_gather(shards[4], "dp", axis=0, tiled=True),
        lax.all_gather(shards[5], "dp", axis=1, tiled=True),
        lax.all_gather(shards[6], "dp", axis=2, tiled=True),
        lax.all_gather(shards[7], "dp", axis=1, tiled=True),
    )
    gains, shifts = (
        lax.all_gather(norm_gains, ("dp", "mp"), axis=1, tiled=True),
        lax.all_gather(feature_biases, ("dp", "mp"), axis=1, tiled=True),
    )
    local_rows, seq_count, width = tokens.shape
    memory_local = memory.shape[0]
    heads_here = head_biases.shape[1]
    head_size = gathered[6].shape[2]
    local_width = heads_here * head_size
    length = local_rows * lax.axis_size("mp")
    memory_length = memory_local * lax.axis_size("mp")
    shape_heads = (seq_count, length, heads_here, head_size)
    shape_memory = (seq_count, memory_length, heads_here, head_size)
    start_row = lax.axis_index("mp") * local_rows
    (
        w_self_in,
        w_self_out,
        w_cross_in,
        w_cross_out,
        feedforward_input_weight,
        feedforward_output_weight,
        w_heads,
        w_inner,
    ) = gathered
    bias_heads = w_heads.astype(jnp.float32).reshape(4, local_width)
    bias_inner = w_inner.astype(jnp.float32).reshape(-1)
    hidden_in = tokens.astype(jnp.float32)
    normed_one, unit_one, inverse_one = normalize(hidden_in, gains[0], shifts[0])
    rows_one = gather_rows(normed_one.astype(jnp.bfloat16))
    project = jnp.einsum("lsd,kde->ksle", rows_one, w_self_in, preferred_element_type=jnp.float32)
    queries_self = ((project[0] + bias_heads[0]) * 0.125).astype(jnp.bfloat16).reshape(shape_heads)
    keys_self = project[1].astype(jnp.bfloat16).reshape(shape_heads)
    values_self = (project[2] + bias_heads[1]).astype(jnp.bfloat16).reshape(shape_heads)
    mixed_self, totals_self = lax.map(
        partial(run_forward, causal=True), (queries_self, keys_self, values_self, lengths)
    )
    mixed_self = mixed_self.astype(jnp.bfloat16).reshape(seq_count, length, local_width)

    def self_term(start, count):
        slice_part = lax.dynamic_slice_in_dim(mixed_self, start, count, 1)
        return jnp.einsum("sle,ed->lsd", slice_part, w_self_out, preferred_element_type=jnp.float32)

    whole_one = whole_rows(self_term, hidden_in, start_row) + shifts[3]
    hidden_one = lax.dynamic_slice_in_dim(whole_one, start_row, local_rows, 0)
    normed_two, unit_two, inverse_two = normalize(hidden_one, gains[1], shifts[1])
    rows_two = normalize(whole_one, gains[1], shifts[1])[0].astype(jnp.bfloat16)
    memory_all = lax.all_gather(memory, "mp", axis=0, tiled=True)
    queries_cross = (
        (
            (
                jnp.einsum(
                    "lsd,de->sle", rows_two, w_cross_in[0], preferred_element_type=jnp.float32
                )
                + bias_heads[2]
            )
            * 0.125
        )
        .astype(jnp.bfloat16)
        .reshape(shape_heads)
    )
    memory_project = jnp.einsum(
        "msd,kde->ksme", memory_all, w_cross_in[1:], preferred_element_type=jnp.float32
    )
    keys_cross = memory_project[0].astype(jnp.bfloat16).reshape(shape_memory)
    values_cross = (memory_project[1] + bias_heads[3]).astype(jnp.bfloat16).reshape(shape_memory)
    mixed_cross, totals_cross = lax.map(
        partial(run_forward, causal=False),
        (queries_cross, keys_cross, values_cross, memory_lengths),
    )
    mixed_cross = mixed_cross.astype(jnp.bfloat16).reshape(seq_count, length, local_width)

    def cross_term(start, count):
        slice_part = lax.dynamic_slice_in_dim(mixed_cross, start, count, 1)
        return jnp.einsum(
            "sle,ed->lsd", slice_part, w_cross_out, preferred_element_type=jnp.float32
        )

    whole_two = whole_rows(cross_term, hidden_one, start_row) + shifts[4]
    hidden_two = lax.dynamic_slice_in_dim(whole_two, start_row, local_rows, 0)
    normed_three, unit_three, inverse_three = normalize(hidden_two, gains[2], shifts[2])
    third_rows = normalize(whole_two, gains[2], shifts[2])[0].astype(jnp.bfloat16)
    inner = (
        jnp.einsum(
            "wri,ix->wrx", third_rows, feedforward_input_weight, preferred_element_type=jnp.float32
        )
        + bias_inner
    )
    smooth_value, smooth_pull = jax.vjp(smooth_unit, inner)
    active_units = smooth_value.astype(jnp.bfloat16)

    def ffn_term(start, count):
        slice_part = lax.dynamic_slice_in_dim(active_units, start, count, 0)
        return jnp.einsum(
            "crx,xp->crp", slice_part, feedforward_output_weight, preferred_element_type=jnp.float32
        )

    output = (hidden_two + spread_rows(ffn_term, local_rows) + shifts[5]).astype(jnp.bfloat16)
    again = (
        lax.all_gather(shards[0], "dp", axis=1, tiled=True),
        lax.all_gather(shards[1], "dp", axis=1, tiled=True),
        lax.all_gather(shards[2], "dp", axis=1, tiled=True),
        lax.all_gather(shards[3], "dp", axis=1, tiled=True),
        lax.all_gather(shards[4], "dp", axis=0, tiled=True),
        lax.all_gather(shards[5], "dp", axis=1, tiled=True),
        lax.all_gather(shards[6], "dp", axis=2, tiled=True),
        lax.all_gather(shards[7], "dp", axis=1, tiled=True),
    )
    (
        w_self_in,
        w_self_out,
        w_cross_in,
        w_cross_out,
        feedforward_input_weight,
        feedforward_output_weight,
        w_heads,
        w_inner,
    ) = again
    counts = pair_counts.astype(jnp.float32)
    matches = (pair_ids[:, None] == jnp.arange(counts.shape[0], dtype=jnp.int32)[None, :]).astype(
        jnp.float32
    )
    own_count = jnp.sum(matches * counts[None, :], -1)
    scale = jnp.mean(counts) / own_count
    positions = start_row + jnp.arange(local_rows, dtype=jnp.int32)
    valid = (positions[:, None] < lengths[None, :]).astype(jnp.float32)
    grad_out = cotangent.astype(jnp.float32) * (valid * scale[None, :])[:, :, None]
    gradient_rows3 = gather_grads(grad_out.astype(jnp.bfloat16))
    gradient_feedforward_output = jnp.einsum(
        "ytb,yth->bh", active_units, gradient_rows3, preferred_element_type=jnp.float32
    )
    grad_active = jnp.einsum(
        "vmr,yr->vmy", gradient_rows3, feedforward_output_weight, preferred_element_type=jnp.float32
    )
    gradient_inner_hidden = smooth_pull(grad_active)[0].astype(jnp.bfloat16)
    grad_fc_in = jnp.einsum(
        "eoc,eoi->ci", third_rows, gradient_inner_hidden, preferred_element_type=jnp.float32
    )
    grad_inner_bias = jnp.sum(gradient_inner_hidden.astype(jnp.float32), (0, 1)).reshape(
        w_inner.shape
    )

    def ffn_back(start, count):
        slice_part = lax.dynamic_slice_in_dim(gradient_inner_hidden, start, count, 0)
        return jnp.einsum(
            "mou,tu->mot", slice_part, feedforward_input_weight, preferred_element_type=jnp.float32
        )

    grad_normed3 = reduce_inputs(ffn_back, local_rows)
    back_three, gain_three, shift_three = normalize_back(
        grad_normed3, gains[2], unit_three, inverse_three
    )
    grad_hidden2 = grad_out + back_three
    grad_rows2 = gather_grads(grad_hidden2.astype(jnp.bfloat16))
    grad_cross_out = jnp.einsum(
        "sle,lsd->ed", mixed_cross, grad_rows2, preferred_element_type=jnp.float32
    )
    grad_mixed = (
        jnp.einsum("lsd,ed->sle", grad_rows2, w_cross_out, preferred_element_type=jnp.float32)
        .astype(jnp.bfloat16)
        .reshape(shape_heads)
    )
    grad_query, grad_key, grad_value = lax.map(
        partial(run_backward, causal=False),
        (queries_cross, keys_cross, values_cross, totals_cross, grad_mixed, memory_lengths),
    )
    grad_query = (grad_query.astype(jnp.bfloat16) * 0.125).reshape(seq_count, length, local_width)
    memory_stack = jnp.stack(
        [
            grad_key.astype(jnp.bfloat16).reshape(seq_count, memory_length, local_width),
            grad_value.astype(jnp.bfloat16).reshape(seq_count, memory_length, local_width),
        ]
    )
    grad_cross_query = jnp.einsum(
        "lsd,sle->de", rows_two, grad_query, preferred_element_type=jnp.float32
    )
    grad_cross_pair = jnp.einsum(
        "msd,ksme->kde", memory_all, memory_stack, preferred_element_type=jnp.float32
    )
    grad_cross_in = jnp.concatenate([grad_cross_query[None], grad_cross_pair], 0)
    bias_query_cross = jnp.sum(grad_query.astype(jnp.float32), (0, 1))
    bias_value_cross = jnp.sum(memory_stack[1].astype(jnp.float32), (0, 1))

    def memory_back(start, count):
        return jnp.einsum(
            "ksme,kde->msd", memory_stack, w_cross_in[1:], preferred_element_type=jnp.float32
        )

    grad_memory = reduce_inputs(memory_back, memory_local)

    def cross_back(start, count):
        slice_part = lax.dynamic_slice_in_dim(grad_query, start, count, 1)
        return jnp.einsum(
            "sle,de->lsd", slice_part, w_cross_in[0], preferred_element_type=jnp.float32
        )

    grad_normed2 = reduce_inputs(cross_back, local_rows)
    back_two, gain_two, shift_two = normalize_back(grad_normed2, gains[1], unit_two, inverse_two)
    grad_hidden1 = grad_hidden2 + back_two
    grad_rows1 = gather_grads(grad_hidden1.astype(jnp.bfloat16))
    grad_self_out = jnp.einsum(
        "sle,lsd->ed", mixed_self, grad_rows1, preferred_element_type=jnp.float32
    )
    grad_mixed = (
        jnp.einsum("lsd,ed->sle", grad_rows1, w_self_out, preferred_element_type=jnp.float32)
        .astype(jnp.bfloat16)
        .reshape(shape_heads)
    )
    grad_query, grad_key, grad_value = lax.map(
        partial(run_backward, causal=True),
        (queries_self, keys_self, values_self, totals_self, grad_mixed, lengths),
    )
    flat_shape = (seq_count, length, local_width)
    self_stack = jnp.stack(
        [
            (grad_query.astype(jnp.bfloat16) * 0.125).reshape(flat_shape),
            grad_key.astype(jnp.bfloat16).reshape(flat_shape),
            grad_value.astype(jnp.bfloat16).reshape(flat_shape),
        ]
    )
    grad_self_in = jnp.einsum(
        "lsd,ksle->kde", rows_one, self_stack, preferred_element_type=jnp.float32
    )
    bias_query_self = jnp.sum(self_stack[0].astype(jnp.float32), (0, 1))
    bias_value_self = jnp.sum(self_stack[2].astype(jnp.float32), (0, 1))

    def self_back(start, count):
        slice_part = lax.dynamic_slice_in_dim(self_stack, start, count, 2)
        return jnp.einsum(
            "ksle,kde->lsd", slice_part, w_self_in, preferred_element_type=jnp.float32
        )

    grad_normed1 = reduce_inputs(self_back, local_rows)
    back_one, gain_one, shift_one = normalize_back(grad_normed1, gains[0], unit_one, inverse_one)
    grad_tokens = grad_hidden1 + back_one
    grad_heads = jnp.stack(
        [bias_query_self, bias_value_self, bias_query_cross, bias_value_cross]
    ).reshape(w_heads.shape)
    gain_grads = jnp.stack([gain_one, gain_two, gain_three])
    shift_grads = jnp.stack(
        [
            shift_one,
            shift_two,
            shift_three,
            jnp.sum(grad_hidden1, (0, 1)),
            jnp.sum(grad_hidden2, (0, 1)),
            jnp.sum(grad_out, (0, 1)),
        ]
    )
    grad_gains, grad_shifts = (
        lax.psum_scatter(gain_grads, ("dp", "mp"), scatter_dimension=1, tiled=True),
        lax.psum_scatter(shift_grads, ("dp", "mp"), scatter_dimension=1, tiled=True),
    )
    all_sums = (
        lax.psum_scatter(
            grad_self_in.astype(jnp.bfloat16), "dp", scatter_dimension=1, tiled=True
        ).astype(jnp.float32),
        lax.psum_scatter(
            grad_self_out.astype(jnp.bfloat16), "dp", scatter_dimension=1, tiled=True
        ).astype(jnp.float32),
        lax.psum_scatter(
            grad_cross_in.astype(jnp.bfloat16), "dp", scatter_dimension=1, tiled=True
        ).astype(jnp.float32),
        lax.psum_scatter(
            grad_cross_out.astype(jnp.bfloat16), "dp", scatter_dimension=1, tiled=True
        ).astype(jnp.float32),
        lax.psum_scatter(
            grad_fc_in.astype(jnp.bfloat16), "dp", scatter_dimension=0, tiled=True
        ).astype(jnp.float32),
        lax.psum_scatter(
            gradient_feedforward_output.astype(jnp.bfloat16), "dp", scatter_dimension=1, tiled=True
        ).astype(jnp.float32),
        lax.psum_scatter(
            grad_heads.astype(jnp.bfloat16), "dp", scatter_dimension=2, tiled=True
        ).astype(jnp.float32),
        lax.psum_scatter(
            grad_inner_bias.astype(jnp.bfloat16), "dp", scatter_dimension=1, tiled=True
        ).astype(jnp.float32),
    )
    (
        sum_self_in,
        sum_self_out,
        sum_cross_in,
        sum_cross_out,
        sum_fc_in,
        sum_fc_out,
        sum_heads,
        sum_inner,
    ) = all_sums
    return (
        output,
        grad_tokens,
        grad_memory,
        sum_self_in,
        sum_self_out,
        sum_cross_in,
        sum_cross_out,
        sum_fc_in,
        sum_fc_out,
        sum_heads,
        sum_inner,
        grad_gains,
        grad_shifts,
    )


LOG2E = 1.4426950408889634
LN2 = 0.6931471805599453
VM = pltpu.VMEM
ANYM = pltpu.HBM
F32 = jnp.float32
BF = jnp.bfloat16
NT_DIMS = (((1,), (1,)), ((), ()))
TN_DIMS = (((0,), (0,)), ((), ()))


def mm(a, b):
    return jnp.dot(a, b, preferred_element_type=F32)


def mm_nt(a, b):
    return lax.dot_general(a, b, NT_DIMS, preferred_element_type=F32)


def mm_tn(a, b):
    return lax.dot_general(a, b, TN_DIMS, preferred_element_type=F32)


def params_of(limit_mib, **more):
    return pltpu.CompilerParams(vmem_limit_bytes=limit_mib * 1024 * 1024, **more)


def cost(flops, data, exps=0):
    return pl.CostEstimate(flops=int(flops), bytes_accessed=int(data), transcendentals=int(exps))


def gated_call(after, kernel, *, grid_spec, out_shape, through=(), input_output_aliases=None, **settings):
    scalars, reads = grid_spec["num_scalar_prefetch"], len(grid_spec["in_specs"])
    used = scalars + reads
    after, through = values_of(after), list(through)
    single = not isinstance(out_shape, list)
    shapes = [out_shape] if single else out_shape
    out_specs = [grid_spec["out_specs"]] if single else list(grid_spec["out_specs"])
    outs, waits = len(shapes), len(after) + len(through)

    def body_of(*refs):
        kernel(*refs[:used], *refs[used + waits : used + waits + outs], *refs[used + waits + outs + len(through) :])

    anywhere = pl.BlockSpec(memory_space=ANYM)
    spec = dict(
        grid_spec,
        in_specs=list(grid_spec["in_specs"]) + [anywhere] * waits,
        out_specs=out_specs + [anywhere] * len(through),
    )
    aliases = dict(input_output_aliases or {})
    aliases.update({used + len(after) + i: outs + i for i in range(len(through))})
    passed = values_of(through)
    call = pl.pallas_call(body_of,
        grid_spec=pltpu.PrefetchScalarGridSpec(**spec),
        out_shape=list(shapes) + [jax.ShapeDtypeStruct(value.shape, value.dtype) for value in passed],
        input_output_aliases=aliases,
        **settings,
    )

    def run(*operands):
        results = call(*values_of(operands), *after, *passed)
        for cell, value in zip(through, results[outs:]):
            cell.value = value
        return results[0] if single else results[:outs]

    return run


def flow_meta(kind):
    corners = [(0, 0), (1, 0), (0, 1), (1, 1)]
    if kind == "zxy":
        near = [[(k, y, 0, x) for k in range(4)] for (x, y) in corners]
    else:
        near = [[(k, y, 0, x) for (x, y) in corners] for k in range(4)]
    return near + [[(k, y, 1, x) for quad in near for (k, y, _, x) in quad]]


def place_of(info, meta):
    k, y, c, x = meta
    slab = info[3] if x == 0 else 1 - info[3]
    zz = lax.rem(info[0] - k + 4, 4)
    yy = info[1] if y == 0 else 1 - info[1]
    cc = info[2] if c == 0 else 1 - info[2]
    return (slab, pl.multiple_of(zz * 256 + yy * 128 + cc * 64, 64))


def start_weight(info, pieces, kind, first, width, buffer, sems):
    for ref, metas in zip(pieces, flow_meta(kind)):
        for j, meta in enumerate(metas):
            slab, row = place_of(info, meta)
            pltpu.make_async_copy(
                ref.at[j, :, pl.ds(first, width)],
                buffer.at[slab, pl.ds(row, 64), :],
                sems.at[slab],
            ).start()


def start_all(pieces, first, width, buffer, sems):
    (ref,) = pieces
    for device in range(32):
        pltpu.make_async_copy(
            ref.at[device, :, pl.ds(first, width)],
            buffer.at[device % 2, pl.ds(device // 2 * 64, 64), :],
            sems.at[device % 2],
        ).start()


def wait_weight(buffer, sems, slab):
    pltpu.make_async_copy(buffer.at[slab], buffer.at[slab], sems.at[slab]).wait()


def ln_parts(hidden):
    average = jnp.mean(hidden, -1, keepdims=True)
    centred = hidden - average
    inverse = lax.rsqrt(jnp.mean(centred * centred, -1, keepdims=True) + eps)
    return (centred * inverse, inverse)


def ln_back(grad_normed, gain, unit, inverse):
    grad_unit = grad_normed * gain
    return inverse * (
        grad_unit
        - jnp.mean(grad_unit, -1, keepdims=True)
        - unit * jnp.mean(grad_unit * unit, -1, keepdims=True)
    )


def row_sum(values):
    return jnp.sum(values, 0, keepdims=True)


def transposed(values):
    return values.T


ROWS = 256
QB = 256


def qkv_kernel(info, par, x_ref, *rest):
    pieces, rest = rest[:10], rest[10:]
    q_ref, k_ref, v_ref, nt_ref, wq, wk, wv, sems = rest
    weights = (wq, wk, wv)

    @pl.when(pl.program_id(0) == 0)
    def _():
        start_self(info, pieces, weights, sems)
        for t in range(3):
            for slab in range(2):
                wait_weight(weights[t], sems.at[t], slab)

    unit, _ = ln_parts(x_ref[...].astype(F32))
    normed = (unit * par[0:1, :] + par[3:4, :]).astype(BF)
    nt_ref[...] = transposed(normed)
    for t in range(3):
        for slab in range(2):


            cols = slice(slab * 512, slab * 512 + 512)
            value = mm(normed, weights[t][slab])
            if t == 0:
                value = (value + par[9:10, cols]) * (0.125 * LOG2E)
            if t == 2:
                value = value + par[10:11, cols]
            (q_ref, k_ref, v_ref)[t][:, cols] = value.astype(BF)


def start_self(info, pieces, weights, sems):
    start_weight(info, pieces[:5], "zxy", 0, 512, weights[0], sems.at[0])
    start_weight(info, pieces[5:], "xyz", 0, 512, weights[1], sems.at[1])
    start_weight(info, pieces[:5], "zxy", 512, 512, weights[2], sems.at[2])


def call_qkv(info, par, x, pieces, after=(), through=()):
    n = x.shape[0]
    out = jax.ShapeDtypeStruct((n, 1024), BF)
    rows = pl.BlockSpec((ROWS, 1024), lambda i, s: (i, 0))
    return gated_call(
        after,
        qkv_kernel,
        grid_spec=dict(
            num_scalar_prefetch=1,
            grid=(n // ROWS,),
            in_specs=[pl.BlockSpec((24, 1024), lambda i, s: (0, 0)), rows]
            + [pl.BlockSpec(memory_space=ANYM)] * 10,
            out_specs=[rows, rows, rows, pl.BlockSpec((1024, ROWS), lambda i, s: (0, i))],
            scratch_shapes=[VM((2, 1024, 512), BF)] * 3 + [pltpu.SemaphoreType.DMA((3, 2))],
        ),
        out_shape=[out, out, out, jax.ShapeDtypeStruct((1024, n), BF)],
        compiler_params=params_of(60),
        cost_estimate=cost(6.4e9, 16e6),
        through=through,
        name="project_self",
    )(info, par, x, *pieces)


def kv_kernel(info, par, x_ref, *rest):
    pieces, rest = rest[:1], rest[1:]
    k_ref, v_ref, nt_ref, wk, wv, sems = rest
    weights = (wk, wv)

    @pl.when(pl.program_id(0) == 0)
    def _():
        for t in range(2):
            start_all(pieces, t * 512, 512, weights[t], sems.at[t])
        for t in range(2):
            for slab in range(2):
                wait_weight(weights[t], sems.at[t], slab)

    rows = x_ref[...]
    nt_ref[...] = transposed(rows)
    for t in range(2):
        for slab in range(2):


            cols = slice(slab * 512, slab * 512 + 512)
            value = mm(rows, weights[t][slab])
            if t == 1:
                value = value + par[12:13, cols]
            (k_ref, v_ref)[t][:, cols] = value.astype(BF)


def call_kv(info, par, x, pieces, after=(), through=()):
    n = x.shape[0]
    out = jax.ShapeDtypeStruct((n, 1024), BF)
    rows = pl.BlockSpec((ROWS, 1024), lambda i, s: (i, 0))
    return gated_call(
        after,
        kv_kernel,
        grid_spec=dict(
            num_scalar_prefetch=1,
            grid=(n // ROWS,),
            in_specs=[pl.BlockSpec((24, 1024), lambda i, s: (0, 0)), rows]
            + [pl.BlockSpec(memory_space=ANYM)],
            out_specs=[rows, rows, pl.BlockSpec((1024, ROWS), lambda i, s: (0, i))],
            scratch_shapes=[VM((2, 1024, 512), BF)] * 2 + [pltpu.SemaphoreType.DMA((2, 2))],
        ),
        out_shape=[out, out, jax.ShapeDtypeStruct((1024, n), BF)],
        compiler_params=params_of(60),
        cost_estimate=cost(4.3e9, 12e6),
        through=through,
        name="project_memory",
    )(info, par, x, *pieces)


def lane_ids(rows):
    return lax.broadcasted_iota(jnp.int32, (rows, 128), 1)


def split3(column):
    high = column.astype(BF)
    rest = column - high.astype(F32)
    middle = rest.astype(BF)
    return (high, middle, (rest - middle.astype(F32)).astype(BF))


def attend_kernel(causal, info, q_ref, k_ref, v_ref, *rest):
    o_ref, lse_ref = rest[-2:]
    lse_ref = lse_ref.at[0]
    n, nk = q_ref.shape[0], k_ref.shape[0]
    lanes_k, lanes_q = lane_ids(nk), lane_ids(QB)
    lane_all = lane_ids(n)

    one = jnp.ones((), BF)
    zero = jnp.zeros((), BF)
    k_aug, v_aug = [], []
    for head in range(2):
        own = (lanes_k >= 64) if head else (lanes_k < 64)
        spare = 0 if head else 64
        keys = jnp.where(own, k_ref[...], zero)
        if not causal:
            place = lax.broadcasted_iota(jnp.int32, (nk, 128), 0)
            shut = jnp.where(place < info[4], 0.0, floor_score).astype(BF)
            keys = jnp.where(lanes_k == spare, shut, keys)
        k_aug.append(keys)
        v_aug.append(jnp.where(own, v_ref[...], jnp.where(lanes_k == spare, one, zero)))
    items = [(first, head) for first in range(0, n, QB) for head in range(2)]

    def scores_of(first, head):
        span = first + QB if causal else nk
        block = q_ref[first : first + QB, :]
        query = block if causal else jnp.where(lanes_q == (0 if head else 64), one, block)
        scores = mm_nt(query, k_aug[head][:span])
        if causal:
            row = lax.broadcasted_iota(jnp.int32, (QB, QB), 0)
            col = lax.broadcasted_iota(jnp.int32, (QB, QB), 1)
            last = jnp.where(col <= row, scores[:, first:], floor_score)
            scores = jnp.concatenate([scores[:, :first], last], 1) if first else last
        return scores

    ahead = scores_of(*items[0])
    for index, (first, head) in enumerate(items):
        scores = ahead
        if index + 1 < len(items):
            ahead = scores_of(*items[index + 1])
        span = first + QB if causal else nk
        highest = jnp.max(scores, -1, keepdims=True)
        raised = jnp.exp2(scores - highest).astype(BF)
        mixed = mm(raised, v_aug[head][:span])
        total = jnp.sum(jnp.where(lanes_q == (0 if head else 64), mixed, 0.0), -1, keepdims=True)
        out, lse = mixed * (1.0 / total), highest + jnp.log2(total)
        if head == 0:
            out_a, lse_a = out, lse
        else:
            o_ref[first : first + QB, :] = jnp.where(lanes_q < 64, out_a, out).astype(BF)
            lse_ref[first : first + QB, :] = jnp.where(lanes_q < 64, lse, lse_a)


def call_attend(info, q, k, v, causal, first, count, earlier=None, after=(), through=()):
    n, nk = q.shape[0], k.shape[0]
    part = (0.625 if causal else 1.0) * count / 8
    heads = lambda rows: pl.BlockSpec((rows, 128), lambda i, s: (0, i + first))
    held = () if earlier is None else tuple(earlier)
    return gated_call(
        after,
        partial(attend_kernel, causal),
        grid_spec=dict(
            num_scalar_prefetch=1,
            grid=(count,),
            in_specs=[heads(n), heads(nk), heads(nk)] + [pl.BlockSpec(memory_space=ANYM)] * len(held),
            out_specs=[heads(n), pl.BlockSpec((1, n, 128), lambda i, s: (i + first, 0, 0))],
        ),
        out_shape=[jax.ShapeDtypeStruct((n, 1024), BF), jax.ShapeDtypeStruct((8, n, 128), F32)],
        input_output_aliases={4: 0, 5: 1} if held else {},
        compiler_params=params_of(60),
        cost_estimate=cost(110.4e9 * part, 1e6),
        name="attend_self" if causal else "attend_cross",
    )(info, q, k, v, *held)


def attend_back_kernel(causal, info, q_ref, k_ref, v_ref, o_ref, g_ref, lse_ref, *rest):
    dq_ref, dk_ref, dv_ref, bias_ref, acc = rest[-5:]
    lse_ref = lse_ref.at[0]
    n, nk = q_ref.shape[0], k_ref.shape[0]
    lanes_k, lanes_q = lane_ids(nk), lane_ids(n)
    one = jnp.ones((), BF)
    zero = jnp.zeros((), BF)
    block_rows = 256 if causal else 512
    q_all, g_all = q_ref[...], g_ref[...]
    k_turned = k_ref[...].T
    product = g_all.astype(F32) * o_ref[...].astype(F32)
    row = lax.broadcasted_iota(jnp.int32, (128, 128), 0)
    col = lax.broadcasted_iota(jnp.int32, (128, 128), 1)
    crossing = jnp.where((row < 64) != (col < 64), one, zero)
    inner = sum(mm(part, crossing) for part in split3(product))
    slot_q, slot_k = lanes_q % 64, lanes_k % 64

    def in_slots(column):
        first, second, third = split3(-column)
        rest = jnp.where(slot_q == 2, third, jnp.where(slot_q == 3, one, zero))
        return jnp.where(slot_q == 0, first, jnp.where(slot_q == 1, second, rest))

    spare_q, spare_g = in_slots(lse_ref[...]), in_slots(inner)
    spare_v = jnp.where(slot_k < 3, one, zero)
    spare_k = spare_v
    if not causal:
        place = lax.broadcasted_iota(jnp.int32, (nk, 128), 0)
        shut = jnp.where(place < info[4], 0.0, floor_score).astype(BF)
        spare_k = jnp.where(slot_k == 3, shut, spare_k)
    k_all, v_all = k_ref[...], v_ref[...]
    sets = []
    for head in range(2):
        own_k = (lanes_k >= 64) if head else (lanes_k < 64)
        own_q = (lanes_q >= 64) if head else (lanes_q < 64)
        sets.append(
            (
                jnp.where(own_q, q_all, zero),
                jnp.where(own_q, g_all, zero),
                jnp.where(own_q, q_all, spare_q),
                jnp.where(own_q, g_all, spare_g),
                jnp.where(own_k, k_all, spare_k),
                jnp.where(own_k, v_all, spare_v),
            )
        )
    items = [(first, head) for first in range(0, nk, block_rows) for head in range(2)]

    def scores_of(first, head):
        from_q = first if causal else 0
        q_own, g_own, q_aug, g_aug, k_aug, v_aug = sets[head]
        keys = slice(first, first + block_rows)
        scores = mm_nt(k_aug[keys], q_aug[from_q:])
        if causal:
            row = lax.broadcasted_iota(jnp.int32, (block_rows, block_rows), 0)
            col = lax.broadcasted_iota(jnp.int32, (block_rows, block_rows), 1)
            head_part = jnp.where(col >= row, scores[:, :block_rows], floor_score)
            if first + block_rows < n:
                scores = jnp.concatenate([head_part, scores[:, block_rows:]], 1)
            else:
                scores = head_part
        return (scores, mm_nt(v_aug[keys], g_aug[from_q:]))

    ahead = scores_of(*items[0])
    acc[...] = jnp.zeros(acc.shape, F32)
    bias = None
    for index, (first, head) in enumerate(items):
        scores, grad_probs = ahead
        if index + 1 < len(items):
            ahead = scores_of(*items[index + 1])
        from_q = first if causal else 0
        q_own, g_own, q_aug, g_aug, k_aug, v_aug = sets[head]
        keys = slice(first, first + block_rows)
        probs = jnp.exp2(scores)
        grad_scores = (probs * grad_probs).astype(BF)
        add_v = mm(probs.astype(BF), g_own[from_q:])
        add_k = mm(grad_scores, q_own[from_q:])
        own = slice(64 * head, 64 * head + 64)
        acc[own, from_q:] += mm(k_turned[own, keys], grad_scores)
        if head == 0:
            dv, dk = add_v, add_k
        else:
            dv = (dv + add_v).astype(BF)
            dv_ref[keys, :] = dv
            dk_ref[keys, :] = ((dk + add_k) * LN2).astype(BF)
            sums = row_sum(dv.astype(F32))
            bias = sums if bias is None else bias + sums
    bias_ref[1:2, :] = bias
    dq = acc[...].T.astype(BF) * jnp.asarray(0.125, BF)
    dq_ref[...] = dq
    bias_ref[0:1, :] = row_sum(dq.astype(F32))


def own_or_other(info, other):
    return 1 - info[3] if other else info[3]


def call_attend_back(info, q, k, v, o, g, lse, causal, first, count, earlier=None, other=None, after=(), through=()):
    n, nk = q.shape[0], k.shape[0]
    part = (0.625 if causal else 1.0) * count / 8
    place = lambda i, s: i + first if other is None else i + first + 4 * own_or_other(s, other)
    heads = lambda rows: pl.BlockSpec((rows, 128), lambda i, s: (0, place(i, s)))
    out = lambda rows: jax.ShapeDtypeStruct((rows, 1024), BF)
    held = () if earlier is None else tuple(earlier)
    return gated_call(
        after,
        partial(attend_back_kernel, causal),
        grid_spec=dict(
            num_scalar_prefetch=1,
            grid=(count,),
            in_specs=[heads(n), heads(nk), heads(nk), heads(n), heads(n)]
            + [pl.BlockSpec((1, n, 128), lambda i, s: (place(i, s), 0, 0))]
            + [pl.BlockSpec(memory_space=ANYM)] * len(held),
            out_specs=[heads(n), heads(nk), heads(nk), heads(8)],
            scratch_shapes=[VM((128, n), F32)],
        ),
        out_shape=[out(n), out(nk), out(nk), jax.ShapeDtypeStruct((8, 1024), F32)],
        input_output_aliases={7: 0, 8: 1, 9: 2, 10: 3} if held else {},
        compiler_params=params_of(60),
        cost_estimate=cost(142.6e9 * part, 1e6),
        name="attend_back_self" if causal else "attend_back_cross",
    )(info, q, k, v, o, g, lse, *held)


def after_self_kernel(info, par, x_ref, o_ref, *rest):
    pieces, rest = rest[:1], rest[1:]
    h_ref, q_ref, nt_ref, wo, wq, sems = rest

    @pl.when(pl.program_id(0) == 0)
    def _():
        start_all(pieces, 1024, 512, wo, sems.at[0])
        start_all(pieces, 1536, 512, wq, sems.at[1])
        for slab in range(2):
            wait_weight(wo, sems.at[0], slab)
        for slab in range(2):
            wait_weight(wq, sems.at[1], slab)

    total = x_ref[...].astype(F32) + par[6:7, :]
    for slab in range(2):


        total = total + mm_nt(o_ref[:, slab * 512 : slab * 512 + 512], wo[slab])
    h_ref[...] = total
    unit, _ = ln_parts(total)
    normed = (unit * par[1:2, :] + par[4:5, :]).astype(BF)
    nt_ref[...] = transposed(normed)
    for slab in range(2):


        cols = slice(slab * 512, slab * 512 + 512)
        value = (mm(normed, wq[slab]) + par[11:12, cols]) * (0.125 * LOG2E)
        q_ref[:, cols] = value.astype(BF)


def call_after_self(info, par, x, o, pieces, after=(), through=()):
    n = x.shape[0]
    rows = pl.BlockSpec((ROWS, 1024), lambda i, s: (i, 0))
    return gated_call(
        after,
        after_self_kernel,
        grid_spec=dict(
            num_scalar_prefetch=1,
            grid=(n // ROWS,),
            in_specs=[pl.BlockSpec((24, 1024), lambda i, s: (0, 0)), rows, rows]
            + [pl.BlockSpec(memory_space=ANYM)],
            out_specs=[rows, rows, pl.BlockSpec((1024, ROWS), lambda i, s: (0, i))],
            scratch_shapes=[VM((2, 1024, 512), BF)] * 2 + [pltpu.SemaphoreType.DMA((2, 2))],
        ),
        out_shape=[
            jax.ShapeDtypeStruct((n, 1024), F32),
            jax.ShapeDtypeStruct((n, 1024), BF),
            jax.ShapeDtypeStruct((1024, n), BF),
        ],
        compiler_params=params_of(60),
        cost_estimate=cost(4.3e9, 16e6),
        through=through,
        name="after_self",
    )(info, par, x, o, *pieces)


def after_cross_kernel(info, par, scale, h_in, o_ref, cot_ref, *rest):
    pieces, rest = rest[:1], rest[1:]
    h_ref, n_ref, nt_ref, g_ref, gt_ref, gsum_ref, wo, sems = rest
    step = pl.program_id(0)

    @pl.when(step == 0)
    def _():
        start_all(pieces, 4096, 512, wo, sems)
        for slab in range(2):
            wait_weight(wo, sems, slab)

    place = step * ROWS + lax.broadcasted_iota(jnp.int32, (ROWS, 1), 0)
    weight = jnp.where(place < info[5], scale[0, 0], 0.0)
    grad = cot_ref[...].astype(F32) * weight
    rounded = grad.astype(BF)
    g_ref[...] = rounded
    gt_ref[...] = transposed(rounded)
    sums = row_sum(grad)

    @pl.when(step == 0)
    def _():
        gsum_ref[...] = jnp.zeros(gsum_ref.shape, F32)

    gsum_ref[0:1, :] += sums
    total = h_in[...] + par[7:8, :]
    for slab in range(2):


        total = total + mm_nt(o_ref[:, slab * 512 : slab * 512 + 512], wo[slab])
    h_ref[...] = total
    unit, _ = ln_parts(total)
    normed = (unit * par[2:3, :] + par[5:6, :]).astype(BF)
    n_ref[...] = normed
    nt_ref[...] = transposed(normed)


def call_after_cross(info, par, scale, h, o, cot, pieces, after=(), through=()):
    n = h.shape[0]
    rows = pl.BlockSpec((ROWS, 1024), lambda i, s: (i, 0))
    turned = pl.BlockSpec((1024, ROWS), lambda i, s: (0, i))
    act = jax.ShapeDtypeStruct((n, 1024), BF)
    act_t = jax.ShapeDtypeStruct((1024, n), BF)
    return gated_call(
        after,
        after_cross_kernel,
        grid_spec=dict(
            num_scalar_prefetch=1,
            grid=(n // ROWS,),
            in_specs=[
                pl.BlockSpec((24, 1024), lambda i, s: (0, 0)),
                pl.BlockSpec((8, 128), lambda i, s: (0, 0)),
                rows,
                rows,
                rows,
            ]
            + [pl.BlockSpec(memory_space=ANYM)],
            out_specs=[rows, rows, turned, rows, turned, pl.BlockSpec((8, 1024), lambda i, s: (0, 0))],
            scratch_shapes=[VM((2, 1024, 512), BF), pltpu.SemaphoreType.DMA((2,))],
        ),
        out_shape=[
            jax.ShapeDtypeStruct((n, 1024), F32),
            act,
            act_t,
            act,
            act_t,
            jax.ShapeDtypeStruct((8, 1024), F32),
        ],
        compiler_params=params_of(60),
        cost_estimate=cost(2.2e9, 26e6),
        through=through,
        name="after_cross",
    )(info, par, scale, h, o, cot, *pieces)


GELU_A = 0.7978845608028654
GELU_B = 0.044715


def store_blocks(info, temp, send_ref, keep_ref, zrel, kind, width):
    for yrel in range(2):
        yy = info[1] if yrel == 0 else 1 - info[1]
        for crel in range(2):
            cc = info[2] if crel == 0 else 1 - info[2]
            row = pl.multiple_of(yy * 128 + cc * 64, 64)
            block = temp[pl.ds(row, 64), :]
            target = send_ref if crel else keep_ref
            if kind == "zxy":
                target[yrel, 0, zrel, :, :] = block
            else:
                target[zrel, yrel, 0, :, :] = block


FFB = 512


def ffn_kernel(info, par, bias_ref, n_ref, nt_ref, g_ref, gt_ref, h_ref, *rest):
    pieces, rest = rest[:1], rest[1:]
    (out_ref, dn_ref, send_ref, keep_ref, dbias_ref, w_in, w_out, acc, active, du, temp, sems) = rest
    half, part = pl.program_id(0), pl.program_id(1)
    parts = pl.num_programs(1)
    n = n_ref.shape[0]
    slab = lax.rem(half + info[3], 2)
    first_step = (half == 0) & (part == 0)

    @pl.when(first_step)
    def _():
        start_all(pieces, 0, 2048, w_in, sems.at[0])
        start_all(pieces, 2048, 2048, w_out, sems.at[1])
        acc[...] = jnp.zeros(acc.shape, F32)
        dn_ref[...] = jnp.zeros(dn_ref.shape, F32)

    @pl.when(part == 0)
    def _():
        wait_weight(w_in, sems.at[0], slab)
        wait_weight(w_out, sems.at[1], slab)

    cols = pl.ds(pl.multiple_of(part * FFB, FFB), FFB)
    first = w_in.at[slab, :, cols]
    second = w_out.at[slab, :, cols]
    total_bias = None
    for chunk in range(n // ROWS):
        rows = slice(chunk * ROWS, chunk * ROWS + ROWS)
        u = mm(n_ref[rows, :], first[...]) + bias_ref[0:1, :]
        square = u * u
        bend = jnp.tanh(u * (GELU_A + GELU_A * GELU_B * square))
        half_up = 0.5 + 0.5 * bend
        r = (u * half_up).astype(BF)
        active[rows, :] = r
        slope = half_up + 0.5 * u * (1.0 - bend * bend) * (GELU_A + 3.0 * GELU_A * GELU_B * square)
        dr = mm(g_ref[rows, :], second[...])
        d = (dr * slope).astype(BF)
        du[rows, :] = d
        sums = row_sum(d.astype(F32))
        total_bias = sums if total_bias is None else total_bias + sums
        up = mm_nt(r, second[...])
        down = mm_nt(d, first[...])

        acc[rows, :] += up
        dn_ref[rows, :] += down

    dbias_ref[0:1, :] = total_bias
    for zrel in range(4):
        zz = lax.rem(info[0] + zrel, 4)
        rows = pl.ds(pl.multiple_of(zz * 256, 256), 256)
        temp[zrel % 2, :, :FFB] = mm(nt_ref[rows, :], du[...]).astype(BF)
        temp[zrel % 2, :, FFB:] = mm(gt_ref[rows, :], active[...]).astype(BF)
        store_blocks(info, temp.at[zrel % 2], send_ref, keep_ref, zrel, "zxy", 2 * FFB)

    @pl.when((half == 1) & (part == parts - 1))
    def _():
        for chunk in range(n // ROWS):
            start = lax.rem(info[3] * (n // 2) + chunk * ROWS, n)
            rows = pl.ds(pl.multiple_of(start, ROWS), ROWS)
            value = h_ref[rows, :] + acc[rows, :] + par[8:9, :]
            out_ref[chunk * ROWS : chunk * ROWS + ROWS, :] = value.astype(BF)


def call_ffn(info, par, bias, normed, normed_t, grad, grad_t, hidden, pieces, after=(), through=()):
    n = normed.shape[0]
    parts = 2048 // FFB
    whole = lambda shape: pl.BlockSpec(shape, lambda x, t, s: (0, 0))
    blocks = pl.BlockSpec((2, 1, 4, 64, 2 * FFB), lambda x, t, s: (0, x, 0, 0, t))
    bias_spec = lambda rows: pl.BlockSpec((rows, FFB), lambda x, t, s: (0, lax.rem(x + s[3], 2) * parts + t))
    return gated_call(
        after,
        ffn_kernel,
        grid_spec=dict(
            num_scalar_prefetch=1,
            grid=(2, parts),
            in_specs=[
                whole((24, 1024)),
                bias_spec(8),
                whole((n, 1024)),
                whole((1024, n)),
                whole((n, 1024)),
                whole((1024, n)),
                whole((n, 1024)),
            ]
            + [pl.BlockSpec(memory_space=ANYM)],
            out_specs=[
                whole((n, 1024)),
                whole((n, 1024)),
                blocks,
                blocks,
                bias_spec(8),
            ],
            scratch_shapes=[
                VM((2, 1024, 2048), BF),
                VM((2, 1024, 2048), BF),
                VM((n, 1024), F32),
                VM((n, FFB), BF),
                VM((n, FFB), BF),
                VM((2, 256, 2 * FFB), BF),
                pltpu.SemaphoreType.DMA((2, 2)),
            ],
        ),
        out_shape=[
            jax.ShapeDtypeStruct((n, 1024), BF),
            jax.ShapeDtypeStruct((n, 1024), F32),
            jax.ShapeDtypeStruct((2, 2, 4, 64, 4096), BF),
            jax.ShapeDtypeStruct((2, 2, 4, 64, 4096), BF),
            jax.ShapeDtypeStruct((8, 4096), F32),
        ],
        compiler_params=params_of(60),
        cost_estimate=cost(51.5e9, 60e6, 4e6),
        through=through,
        name="feedforward",
    )(info, par, bias, normed, normed_t, grad, grad_t, hidden, *pieces)


def back_three_kernel(info, par, dn_ref, h_ref, g_ref, *rest):
    pieces, rest = rest[:1], rest[1:]
    dh_ref, do_ref, gt_ref, sum_ref, wo, sems = rest
    step = pl.program_id(0)

    @pl.when(step == 0)
    def _():
        start_all(pieces, 4096, 512, wo, sems)
        sum_ref[...] = jnp.zeros(sum_ref.shape, F32)
        for slab in range(2):
            wait_weight(wo, sems, slab)

    back_rows(par, 2, dn_ref[...], h_ref[...], g_ref[...].astype(F32), dh_ref, gt_ref, sum_ref, do_ref, wo, sems)


def back_rows(par, index, dn, hidden, residual, dh_ref, gt_ref, sum_ref, do_ref, wo, sems):
    unit, inverse = ln_parts(hidden)
    grad = residual + ln_back(dn, par[index : index + 1, :], unit, inverse)
    dh_ref[...] = grad
    sum_ref[0:1, :] += row_sum(dn * unit)
    sum_ref[1:2, :] += row_sum(dn)
    sum_ref[2:3, :] += row_sum(grad)
    rounded = grad.astype(BF)
    gt_ref[...] = transposed(rounded)
    for slab in range(2):


        do_ref[:, slab * 512 : slab * 512 + 512] = mm(rounded, wo[slab]).astype(BF)


def call_back_three(info, par, dn, h, g, pieces, after=(), through=()):
    n = h.shape[0]
    rows = pl.BlockSpec((ROWS, 1024), lambda i, s: (i, 0))
    return gated_call(
        after,
        back_three_kernel,
        grid_spec=dict(
            num_scalar_prefetch=1,
            grid=(n // ROWS,),
            in_specs=[pl.BlockSpec((24, 1024), lambda i, s: (0, 0)), rows, rows, rows]
            + [pl.BlockSpec(memory_space=ANYM)],
            out_specs=[
                rows,
                rows,
                pl.BlockSpec((1024, ROWS), lambda i, s: (0, i)),
                pl.BlockSpec((8, 1024), lambda i, s: (0, 0)),
            ],
            scratch_shapes=[VM((2, 1024, 512), BF), pltpu.SemaphoreType.DMA((2,))],
        ),
        out_shape=[
            jax.ShapeDtypeStruct((n, 1024), F32),
            jax.ShapeDtypeStruct((n, 1024), BF),
            jax.ShapeDtypeStruct((1024, n), BF),
            jax.ShapeDtypeStruct((8, 1024), F32),
        ],
        compiler_params=params_of(60),
        cost_estimate=cost(2.2e9, 20e6),
        through=through,
        name="back_three",
    )(info, par, dn, h, g, *pieces)


def back_two_kernel(info, par, dq_ref, h_ref, dh2_ref, *rest):
    pieces, rest = rest[:1], rest[1:]
    dh_ref, do_ref, gt_ref, sum_ref, wq, wo, sems = rest
    step = pl.program_id(0)

    @pl.when(step == 0)
    def _():
        start_all(pieces, 1536, 512, wq, sems.at[0])
        start_all(pieces, 1024, 512, wo, sems.at[1])
        sum_ref[...] = jnp.zeros(sum_ref.shape, F32)
        for slab in range(2):
            wait_weight(wq, sems.at[0], slab)
        for slab in range(2):
            wait_weight(wo, sems.at[1], slab)

    dn = None
    for slab in range(2):


        term = mm_nt(dq_ref[:, slab * 512 : slab * 512 + 512], wq[slab])
        dn = term if dn is None else dn + term
    back_rows(par, 1, dn, h_ref[...], dh2_ref[...], dh_ref, gt_ref, sum_ref, do_ref, wo, sems.at[1])


def call_back_two(info, par, dq, h, dh2, pieces, after=(), through=()):
    n = h.shape[0]
    rows = pl.BlockSpec((ROWS, 1024), lambda i, s: (i, 0))
    return gated_call(
        after,
        back_two_kernel,
        grid_spec=dict(
            num_scalar_prefetch=1,
            grid=(n // ROWS,),
            in_specs=[pl.BlockSpec((24, 1024), lambda i, s: (0, 0)), rows, rows, rows]
            + [pl.BlockSpec(memory_space=ANYM)],
            out_specs=[
                rows,
                rows,
                pl.BlockSpec((1024, ROWS), lambda i, s: (0, i)),
                pl.BlockSpec((8, 1024), lambda i, s: (0, 0)),
            ],
            scratch_shapes=[VM((2, 1024, 512), BF)] * 2 + [pltpu.SemaphoreType.DMA((2, 2))],
        ),
        out_shape=[
            jax.ShapeDtypeStruct((n, 1024), F32),
            jax.ShapeDtypeStruct((n, 1024), BF),
            jax.ShapeDtypeStruct((1024, n), BF),
            jax.ShapeDtypeStruct((8, 1024), F32),
        ],
        compiler_params=params_of(60),
        cost_estimate=cost(4.3e9, 24e6),
        through=through,
        name="back_two",
    )(info, par, dq, h, dh2, *pieces)


def memory_back_kernel(info, dk_ref, dv_ref, *rest):
    pieces, rest = rest[:1], rest[1:]
    out_ref, wk, wv, sems = rest

    @pl.when(pl.program_id(0) == 0)
    def _():
        start_all(pieces, 0, 512, wk, sems.at[0])
        start_all(pieces, 512, 512, wv, sems.at[1])
        for slab in range(2):
            wait_weight(wk, sems.at[0], slab)
        for slab in range(2):
            wait_weight(wv, sems.at[1], slab)

    total = None
    for t, (ref, weight) in enumerate(((dk_ref, wk), (dv_ref, wv))):
        for slab in range(2):


            term = mm_nt(ref[:, slab * 512 : slab * 512 + 512], weight[slab])
            total = term if total is None else total + term
    out_ref[...] = total.astype(BF)


def call_memory_back(info, dk, dv, pieces, after=(), through=()):
    n = dk.shape[0]
    steps = n // 2 // ROWS
    rows = pl.BlockSpec((ROWS, 1024), lambda i, s: (lax.rem(i + steps * s[3], 2 * steps), 0))
    return gated_call(
        after,
        memory_back_kernel,
        grid_spec=dict(
            num_scalar_prefetch=1,
            grid=(n // ROWS,),
            in_specs=[rows, rows] + [pl.BlockSpec(memory_space=ANYM)],
            out_specs=pl.BlockSpec((ROWS, 1024), lambda i, s: (i, 0)),
            scratch_shapes=[VM((2, 1024, 512), BF)] * 2 + [pltpu.SemaphoreType.DMA((2, 2))],
        ),
        out_shape=jax.ShapeDtypeStruct((n, 1024), BF),
        compiler_params=params_of(60),
        cost_estimate=cost(4.3e9, 12e6),
        through=through,
        name="memory_back",
    )(info, dk, dv, *pieces)


def back_one_kernel(info, par, dq_ref, dk_ref, dv_ref, x_ref, dh1_ref, *rest):
    pieces, rest = rest[:10], rest[10:]
    out_ref, sum_ref, wq, wk, wv, sems = rest
    weights = (wq, wk, wv)
    step = pl.program_id(0)

    @pl.when(step == 0)
    def _():
        start_self(info, pieces, weights, sems)
        sum_ref[...] = jnp.zeros(sum_ref.shape, F32)
        for t in range(3):
            for slab in range(2):
                wait_weight(weights[t], sems.at[t], slab)

    dn = None
    for t, ref in enumerate((dq_ref, dk_ref, dv_ref)):
        for slab in range(2):


            term = mm_nt(ref[:, slab * 512 : slab * 512 + 512], weights[t][slab])
            dn = term if dn is None else dn + term
    unit, inverse = ln_parts(x_ref[...].astype(F32))
    grad = dh1_ref[...] + ln_back(dn, par[0:1, :], unit, inverse)
    out_ref[...] = grad.astype(BF)
    sum_ref[0:1, :] += row_sum(dn * unit)
    sum_ref[1:2, :] += row_sum(dn)


def call_back_one(info, par, dq, dk, dv, x, dh1, pieces, other, after=(), through=()):
    n = x.shape[0]
    steps = n // 2 // ROWS
    rows = pl.BlockSpec((ROWS, 1024), lambda i, s: (i + steps * own_or_other(s, other), 0))
    return gated_call(
        after,
        back_one_kernel,
        grid_spec=dict(
            num_scalar_prefetch=1,
            grid=(steps,),
            in_specs=[pl.BlockSpec((24, 1024), lambda i, s: (0, 0)), rows, rows, rows, rows, rows]
            + [pl.BlockSpec(memory_space=ANYM)] * 10,
            out_specs=[pl.BlockSpec((ROWS, 1024), lambda i, s: (i, 0)), pl.BlockSpec((8, 1024), lambda i, s: (0, 0))],
            scratch_shapes=[VM((2, 1024, 512), BF)] * 3 + [pltpu.SemaphoreType.DMA((3, 2))],
        ),
        out_shape=[jax.ShapeDtypeStruct((n // 2, 1024), BF), jax.ShapeDtypeStruct((8, 1024), F32)],
        compiler_params=params_of(60),
        cost_estimate=cost(6.4e9, 20e6),
        through=through,
        name="back_one",
    )(info, par, dq, dk, dv, x, dh1, *pieces)


def block_out(kind, width, total):
    if kind == "zxy":
        shape, block = (2, 2, 4, 64, total), (2, 1, 4, 64, width)
        spec = lambda index: pl.BlockSpec(block, index(lambda x, t: (0, x, 0, 0, t)))
    else:
        shape, block = (4, 2, 2, 64, total), (4, 2, 1, 64, width)
        spec = lambda index: pl.BlockSpec(block, index(lambda x, t: (0, 0, x, 0, t)))
    return (jax.ShapeDtypeStruct(shape, BF), spec)


def weight_grad_kernel(kind, picks, count, info, *refs):
    lefts, rights = refs[:count], refs[count : count + len(picks)]
    send_ref, keep_ref, temp = refs[count + len(picks) :]
    for t, pick in enumerate(picks):

        @pl.when(pl.program_id(1) == t)
        def _():
            for zrel in range(4):
                zz = lax.rem(info[0] + zrel, 4)
                rows = pl.ds(pl.multiple_of(zz * 256, 256), 256)
                temp[...] = mm(lefts[pick][rows, :], rights[t][...]).astype(BF)
                store_blocks(info, temp, send_ref, keep_ref, zrel, kind, 512)


def call_weight_grad(info, kind, lefts, rights, picks, name, after=(), through=()):
    n = rights[0].shape[0]
    shape, spec = block_out(kind, 512, 512 * len(rights))
    index = lambda f: (lambda x, t, s: f(x, t))
    return gated_call(
        after,
        partial(weight_grad_kernel, kind, picks, len(lefts)),
        grid_spec=dict(
            num_scalar_prefetch=1,
            grid=(2, len(rights)),
            in_specs=[pl.BlockSpec((1024, n), lambda x, t, s: (0, 0))] * len(lefts)
            + [pl.BlockSpec((n, 512), lambda x, t, s: (0, lax.rem(x + s[3], 2)))] * len(rights),
            out_specs=[spec(index), spec(index)],
            scratch_shapes=[VM((256, 512), BF)],
        ),
        out_shape=[shape, shape],
        compiler_params=params_of(60),
        cost_estimate=cost(10.3e9 * len(rights), 1e6),
        through=through,
        name=name,
    )(info, *lefts, *rights)


def half_grad_kernel(picks, count, info, *refs):
    lefts, rights = refs[:count], refs[count : count + len(picks)]
    send_ref, keep_ref, temp = refs[count + len(picks) :]
    for t, pick in enumerate(picks):

        @pl.when(pl.program_id(0) == t)
        def _():
            for zrel in range(4):
                zz = lax.rem(info[0] + zrel, 4)
                rows = pl.ds(pl.multiple_of(zz * 256, 256), 256)
                temp[...] = mm(lefts[pick][rows, :], rights[t][...]).astype(BF)
                for yrel in range(2):
                    yy = info[1] if yrel == 0 else 1 - info[1]
                    for crel, target in enumerate((keep_ref, send_ref)):
                        cc = info[2] if crel == 0 else 1 - info[2]
                        row = pl.multiple_of(yy * 128 + cc * 64, 64)
                        target[yrel, zrel, :, :] = temp[pl.ds(row, 64), :]


def call_half_grad(info, other, lefts, rights, picks, name, after=(), through=()):
    n = rights[0].shape[0]
    shape = jax.ShapeDtypeStruct((2, 4, 64, 512 * len(rights)), BF)
    spec = pl.BlockSpec((2, 4, 64, 512), lambda t, s: (0, 0, 0, t))
    return gated_call(
        after,
        partial(half_grad_kernel, picks, len(lefts)),
        grid_spec=dict(
            num_scalar_prefetch=1,
            grid=(len(rights),),
            in_specs=[pl.BlockSpec((1024, n), lambda t, s: (0, 0))] * len(lefts)
            + [pl.BlockSpec((n, 512), lambda t, s: (0, own_or_other(s, other)))] * len(rights),
            out_specs=[spec, spec],
            scratch_shapes=[VM((256, 512), BF)],
        ),
        out_shape=[shape, shape],
        compiler_params=params_of(60),
        cost_estimate=cost(10e9, 1e6),
        through=through,
        name=name,
    )(info, *lefts, *rights)


def pack_kernel(one_a, one_b, two, three, cot, own, cross, inner, out_ref):
    out_ref[...] = jnp.zeros(out_ref.shape, F32)
    out_ref[0:1, :] = one_a[0:1, :] + one_b[0:1, :]
    out_ref[3:4, :] = one_a[1:2, :] + one_b[1:2, :]
    for k, ref in ((1, two), (2, three)):
        out_ref[k : k + 1, :] = ref[0:1, :]
        out_ref[3 + k : 4 + k, :] = ref[1:2, :]
        out_ref[5 + k : 6 + k, :] = ref[2:3, :]
    out_ref[8:9, :] = cot[0:1, :]
    out_ref[9:11, :] = own[0:2, :]
    out_ref[11:13, :] = cross[0:2, :]
    for k in range(4):
        out_ref[13 + k : 14 + k, :] = inner[0:1, k * 1024 : k * 1024 + 1024]


def call_pack(*sums):
    return pl.pallas_call(
        pack_kernel,
        out_shape=jax.ShapeDtypeStruct((24, 1024), F32),
        compiler_params=params_of(60),
        name="pack_sums",
    )(*sums)


def along(axis_bit):
    return [(i, i ^ axis_bit) for i in range(16)]


NEAR_Z = [(i, i ^ 4) for i in range(16)]
FAR_Z = [(i, i ^ 8) for i in range(16)]
RING = [(i, (i + 4) % 16) for i in range(16)]


def swap_x(value):
    return lax.ppermute(value, "mp", [(0, 1), (1, 0)])


def swap_y(value):
    return lax.ppermute(value, "dp", along(2))


def swap_core(value):
    return lax.ppermute(value, "dp", along(1))


def next_z(value):
    return lax.ppermute(value, "dp", RING)


class Cell:
    def __init__(self, value):
        self.value = value


def values_of(items):
    return [item.value if isinstance(item, Cell) else item for item in items]


class GatherZXY:
    def __init__(self, shard):
        self.steps = [Cell(shard)]

    def z(self):
        self.steps.append(Cell(next_z(self.steps[-1].value)))
        return self.steps[-1]

    def x(self):
        self.base = Cell(jnp.stack(values_of(self.steps)))
        self.over_x = Cell(swap_x(self.base.value))
        return self.over_x

    def y(self):
        self.over_y = Cell(swap_y(self.base.value))
        return self.over_y

    def xy(self):
        self.over_xy = Cell(swap_y(self.over_x.value))
        return self.over_xy

    def core(self):
        self.quads = [self.base, self.over_x, self.over_y, self.over_xy]
        self.other = Cell(swap_core(jnp.concatenate(values_of(self.quads), 0)))
        return self.other

    def pieces(self):
        return values_of(self.quads + [self.other])


class GatherXYZ:
    def __init__(self, shard):
        self.shard = Cell(shard)

    def x(self):
        self.pair = Cell(jnp.stack([self.shard.value, swap_x(self.shard.value)]))
        return self.pair

    def y(self):
        over_y = swap_y(self.pair.value)
        self.quads = [Cell(jnp.concatenate([self.pair.value, over_y], 0))]
        return self.quads[0]

    def z(self):
        self.quads.append(Cell(next_z(self.quads[-1].value)))
        return self.quads[-1]

    def core(self):
        self.other = Cell(swap_core(jnp.concatenate(values_of(self.quads), 0)))
        return self.other

    def pieces(self):
        return values_of(self.quads + [self.other])


def hold(cells, after):
    def kernel(*refs):
        pass

    gated_call(
        after,
        kernel,
        through=cells,
        grid_spec=dict(num_scalar_prefetch=0, grid=(), in_specs=[], out_specs=[]),
        out_shape=[],
        compiler_params=params_of(60),
        name="hold",
    )()


def sum_small(value):
    value = value + swap_core(value)
    value = value + swap_x(value)
    value = value + swap_y(value)
    value = value + lax.ppermute(value, "dp", NEAR_Z)
    return value + lax.ppermute(value, "dp", FAR_Z)


def join(kept, received):
    return (kept.astype(F32) + received.astype(F32)).astype(kept.dtype)


class ReduceZXY:
    def __init__(self, send, keep):
        self.send, self.keep, self.moving = Cell(send), keep, None

    def core(self):
        self.received = Cell(swap_core(self.send.value))

    def y(self):
        got = self.received.value
        arrived = swap_y(join(self.keep[1], got[1]))
        self.keep, self.also = join(self.keep[0], got[0]), None
        self.received = Cell(arrived)

    def x(self):
        got = self.received.value
        arrived = swap_x(join(self.keep[1], got[1]))
        self.keep, self.also = self.keep[0], got[0]
        self.received = Cell(arrived)
        self.left = 4

    def z(self):
        self.moving = Cell(next_z(self.total(BF)))

    def total(self, kind):
        self.left -= 1
        k = self.left
        value = self.keep[k].astype(F32) + self.also[k].astype(F32) + self.received.value[k].astype(F32)
        if self.moving is not None:
            value = value + self.moving.value.astype(F32)
        return value.astype(kind)

    def result(self):
        return self.total(F32)


class ReduceXYZ:
    def __init__(self, send, keep):
        self.send, self.keep, self.moving = Cell(send), keep, None

    def core(self):
        self.received = Cell(swap_core(self.send.value))
        self.left = 4

    def z(self):
        self.left -= 1
        self.moving = Cell(next_z(self.total(BF, ())))

    def total(self, kind, index):
        k = self.left
        value = self.keep[k][index].astype(F32) + self.received.value[k][index].astype(F32)
        if self.moving is not None:
            value = value + self.moving.value[index].astype(F32)
        return value.astype(kind)

    def y(self):
        self.left -= 1
        self.arrived = Cell(swap_y(self.total(BF, 1)))

    def x(self):
        self.across = Cell(swap_x((self.total(F32, (0, 1)) + self.arrived.value[1].astype(F32)).astype(BF)))

    def result(self):
        return self.total(F32, (0, 0)) + self.arrived.value[0].astype(F32) + self.across.value.astype(F32)


def join_halves(mine, other, me):
    return jnp.where(me == 0, jnp.concatenate([mine, other], 0), jnp.concatenate([other, mine], 0))


class Exchange:
    def __init__(self, local, me):
        self.me = me
        self.mine = jnp.where(me == 0, local[:, 0], local[:, 1])
        self.theirs = Cell(jnp.where(me == 0, local[:, 1], local[:, 0]))

    def go(self):
        self.other = swap_x(self.theirs.value)

    def whole(self):
        return join_halves(self.mine, self.other, self.me)


def both_sequences(mine, other, me):
    return jnp.where(me == 0, jnp.stack([mine, other], 1), jnp.stack([other, mine], 1))


class ReduceHalves:
    def __init__(self, send, keep):
        self.send, self.keep, self.across = Cell(send), keep, None

    def core(self):
        self.received = Cell(swap_core(self.send.value))

    def y(self):
        self.arrived = Cell(swap_y(join(self.keep[1], self.received.value[1])))

    def sum(self, k):
        terms = (self.keep[0], self.received.value[0], self.arrived.value)
        if self.across is not None:
            terms += (self.across.value,)
        return sum(term[k].astype(F32) for term in terms)

    def x(self):
        return Cell(swap_x(self.sum(slice(None)).astype(BF)))

    def z(self, moving=None):
        k = 3 if moving is None else moving[0] - 1
        value = self.sum(k) if moving is None else self.sum(k) + moving[1].astype(F32)
        return (k, next_z(value.astype(BF)))


SMALL = 17 * 1024


def place_small(norm_gains, feature_biases, head_biases, inner_bias, dp, me):
    column = 32 * (2 * dp + me)
    put = lax.dynamic_update_slice
    gains = put(jnp.zeros((3, 1024), F32), norm_gains, (0, column))
    shifts = put(jnp.zeros((6, 1024), F32), feature_biases, (0, column))
    heads = put(jnp.zeros((4, 16, 64), F32), head_biases.astype(F32), (0, me * 8, dp * 4))
    inner = put(jnp.zeros((16, 256), F32), inner_bias.astype(F32), (me * 8, dp * 16))
    return jnp.concatenate([gains, shifts, heads.reshape(4, 1024), inner.reshape(4, 1024)], 0)


def one_sequence_body(
    tokens,
    memory,
    cotangent,
    lengths,
    memory_lengths,
    pair_ids,
    pair_counts,
    self_in,
    self_out,
    cross_in,
    cross_out,
    fc_in,
    fc_out,
    head_biases,
    inner_bias,
    norm_gains,
    feature_biases,
):
    dp, me = lax.axis_index("dp"), lax.axis_index("mp")
    own_length = lax.dynamic_index_in_dim(lengths, me, 0, keepdims=False)
    own_memory = lax.dynamic_index_in_dim(memory_lengths, me, 0, keepdims=False)
    info = jnp.stack([dp // 4, (dp // 2) % 2, dp % 2, me, own_memory, own_length, dp, dp]).astype(jnp.int32)
    counts = pair_counts.astype(F32)
    matches = (pair_ids[:, None] == jnp.arange(counts.shape[0], dtype=jnp.int32)[None, :]).astype(F32)
    scales = jnp.mean(counts) / jnp.sum(matches * counts[None, :], -1)
    scale = jnp.broadcast_to(lax.dynamic_index_in_dim(scales, me, 0, keepdims=False), (8, 128))

    small = place_small(norm_gains, feature_biases, head_biases, inner_bias, dp, me)
    info = Cell(info)
    x = Exchange(tokens, me)
    own_k = GatherXYZ(self_in[1])
    own_qv = GatherZXY(jnp.concatenate([self_in[0], self_in[2]], 1))
    middle = jnp.concatenate([cross_in[1], cross_in[2], self_out.T, cross_in[0]], 1)
    w_mid = [lax.all_gather(middle, ("dp", "mp"), axis=0, tiled=False)]
    outer = jnp.concatenate([fc_in, fc_out.T, cross_out.T], 1)
    w_out = [lax.all_gather(outer, ("dp", "mp"), axis=0, tiled=False)]
    mem, cot = Exchange(memory, me), Exchange(cotangent, me)
    own_k.x(), own_qv.z(), x.go()
    small = small + swap_core(small)
    own_k.y(), own_qv.z()
    small = small + swap_x(small)
    own_k.z(), own_qv.z()
    small = small + swap_y(small)
    own_k.z(), own_qv.x(), own_qv.y()
    small = Cell(small + lax.ppermute(small, "dp", NEAR_Z))
    hold([mem.theirs, own_k.quads[2], own_qv.over_x, small], [])
    own_k.z(), own_qv.xy()
    small = small.value + lax.ppermute(small.value, "dp", FAR_Z)
    own_k.core(), own_qv.core()
    par = jnp.concatenate([small[:13], jnp.zeros((11, 1024), F32)], 0)
    inner = jnp.broadcast_to(small[13:17].reshape(1, 4096), (8, 4096))
    x = x.whole()
    hold([info, mem.theirs], [own_k.other, own_qv.other, x])
    w_self = own_qv.pieces() + own_k.pieces()
    mem.go()
    q1, k1, v1, n1_t = call_qkv(info, par, x, w_self)
    attended = call_attend(info, q1, k1, v1, True, 0, 4)
    o1, lse1 = call_attend(info, q1, k1, v1, True, 4, 4, attended)
    h1, q2, n2_t = call_after_self(info, par, x, o1, w_mid)
    mem = mem.whole()
    hold([info, cot.theirs], [h1, mem])
    cot.go()
    k2, v2, mem_t = call_kv(info, par, mem, w_mid)
    o2, lse2 = call_attend(info, q2, k2, v2, False, 0, 8)
    h2, n3, n3_t, g3, g3_t, g_sum = call_after_cross(info, par, scale, h1, o2, cot.whole(), w_out)
    out, dn3, send_fc, keep_fc, d_inner = call_ffn(info, par, inner, n3, n3_t, g3, g3_t, h2, w_out)

    half = out.shape[0] // 2
    sum_f = ReduceZXY(send_fc, keep_fc)
    sum_f.core()
    out_other = swap_x(out[half:])
    dh2, do2, g2_t, sums3 = call_back_three(info, par, dn3, h2, g3, w_out)
    hold([info, sum_f.received], [do2])
    sum_f.y()
    dq2, dk2, dv2, bias2 = call_attend_back(info, q2, k2, v2, o2, do2, lse2, False, 0, 8)
    dh1, do1, g1_t, sums2 = call_back_two(info, par, dq2, h1, dh2, w_mid)
    cross = call_weight_grad(
        info, "zxy", [mem_t, n2_t, g2_t, g1_t], [dk2, dv2, dq2, o2, o1], (0, 0, 1, 2, 3), "weight_grad_cross", after=[do1]
    )
    sum_c = ReduceZXY(*cross)
    hold([info, sum_c.send, sum_f.received], [out_other, sum_c.keep])
    sum_c.core(), sum_f.x()
    grad_mem = Cell(call_memory_back(info, dk2, dv2, w_mid))
    hold([info, sum_c.received, grad_mem], [])
    sum_c.y()
    memory_other = swap_x(grad_mem.value[half:])
    back = call_attend_back(info, q1, k1, v1, o1, do1, lse1, True, 0, 4, other=True)
    hold([info, sum_f.received], [back[0], memory_other])
    sum_f.z()
    sum_s1 = ReduceHalves(*call_half_grad(info, True, [n1_t], back[:3], (0, 0, 0), "weight_grad_self_1"))
    hold([info, sum_s1.send, sum_f.moving], [sum_s1.keep])
    sum_s1.core(), sum_f.z()
    back = call_attend_back(info, q1, k1, v1, o1, do1, lse1, True, 0, 2, back, other=False)
    hold([info, sum_s1.received, sum_c.received, sum_f.moving], [back[0]])
    sum_s1.y(), sum_c.x(), sum_f.z()
    dq1, dk1, dv1, bias1 = call_attend_back(info, q1, k1, v1, o1, do1, lse1, True, 2, 2, back, other=False)
    hold([info, sum_s1.arrived], [bias1, sum_f.moving])
    across = sum_s1.x()
    sum_s0 = ReduceHalves(*call_half_grad(info, False, [n1_t], [dq1, dk1, dv1], (0, 0, 0), "weight_grad_self_0"))
    hold([info, sum_s0.send, sum_c.received], [sum_s0.keep])
    sum_s0.core(), sum_c.z()
    grad_other, sums1a = call_back_one(info, par, dq1, dk1, dv1, x, dh1, w_self, True)
    grad_other = Cell(grad_other)
    hold([info, sum_s0.received, sum_c.moving, grad_other, across], [])
    sum_s0.y(), sum_c.z()
    tokens_other = swap_x(grad_other.value)
    grad_own, sums1b = call_back_one(info, par, dq1, dk1, dv1, x, dh1, w_self, False)
    d_small = Cell(call_pack(sums1a, sums1b, sums2, sums3, g_sum, bias1, bias2, d_inner))
    hold([sum_s0.arrived, sum_c.moving, d_small], [tokens_other])
    sum_s0.across = across
    moving = sum_s0.z()
    d_small = sum_small(d_small.value)
    moving = sum_s0.z(moving)
    sum_c.z()
    moving = sum_s0.z(moving)
    output = both_sequences(out[:half], out_other, me)
    grad_tokens = both_sequences(grad_own, tokens_other, me).astype(F32)
    grad_memory = both_sequences(grad_mem.value[:half], memory_other, me).astype(F32)
    fc = sum_f.result().reshape(64, 4, 2, 512)
    self_all = sum_s0.sum(0) + moving[1].astype(F32)
    column = 32 * (2 * dp + me)
    take = lax.dynamic_slice
    crossed = sum_c.result()
    return (
        output,
        grad_tokens,
        grad_memory,
        jnp.stack([self_all[:, :512], self_all[:, 512:1024], self_all[:, 1024:]]),
        crossed[:, 2048:].T,
        jnp.stack([crossed[:, 1024:1536], crossed[:, :512], crossed[:, 512:1024]]),
        crossed[:, 1536:2048].T,
        fc[:, :, 0].reshape(64, 2048),
        fc[:, :, 1].reshape(64, 2048).T,
        take(d_small[9:13].reshape(4, 16, 64), (0, me * 8, dp * 4), (4, 8, 4)),
        take(d_small[13:17].reshape(16, 256), (me * 8, dp * 16), (8, 16)),
        take(d_small[:3], (0, column), (3, 32)),
        take(d_small[3:9], (0, column), (6, 32)),
    )


def solution(mesh):
    in_specs = (
        P("mp", "dp", None),
        P("mp", "dp", None),
        P("mp", "dp", None),
        P("dp"),
        P("dp"),
        P("dp"),
        P(),
        P(None, "dp", "mp"),
        P("mp", "dp"),
        P(None, "dp", "mp"),
        P("mp", "dp"),
        P("dp", "mp"),
        P("mp", "dp"),
        P(None, "mp", "dp"),
        P("mp", "dp"),
        P(None, ("dp", "mp")),
        P(None, ("dp", "mp")),
    )
    out_specs = (
        P("mp", "dp", None),
        P("mp", "dp", None),
        P("mp", "dp", None),
        P(None, "dp", "mp"),
        P("mp", "dp"),
        P(None, "dp", "mp"),
        P("mp", "dp"),
        P("dp", "mp"),
        P("mp", "dp"),
        P(None, "mp", "dp"),
        P("mp", "dp"),
        P(None, ("dp", "mp")),
        P(None, ("dp", "mp")),
    )
    sizes = dict(mesh.shape)
    chosen = one_sequence_body if (sizes["dp"], sizes["mp"]) == (16, 2) else body
    return jax.shard_map(chosen, mesh=mesh, in_specs=in_specs, out_specs=out_specs, check_vma=False)
```

```python
from functools import partial

import jax
import jax.numpy as jnp
from jax import lax
from jax.experimental import pallas as pl
from jax.experimental.pallas import tpu as pltpu
from jax.sharding import PartitionSpec as P

eps = 1e-05
floor_score = -1e30


def smooth_unit(values):
    return jax.nn.gelu(values, approximate=True)


def normalize(hidden, gain, shift):
    average = jnp.mean(hidden, -1, keepdims=True)
    centred = hidden - average
    inverse = lax.rsqrt(jnp.mean(centred * centred, -1, keepdims=True) + eps)
    unit = centred * inverse
    return (unit * gain + shift, unit, inverse)


def normalize_back(grad_normed, gain, unit, inverse):
    grad_unit = grad_normed * gain
    grad_hidden = inverse * (
        grad_unit
        - jnp.mean(grad_unit, -1, keepdims=True)
        - unit * jnp.mean(grad_unit * unit, -1, keepdims=True)
    )
    return (grad_hidden, jnp.sum(grad_normed * unit, (0, 1)), jnp.sum(grad_normed, (0, 1)))


def masked_scores(rows, keys, first, limit, causal):
    scores = jnp.einsum("qhd,khd->hqk", rows, keys, preferred_element_type=jnp.float32)
    key_place = jnp.arange(keys.shape[0], dtype=jnp.int32)[None, :]
    if causal:
        allowed = key_place <= first + jnp.arange(rows.shape[0], dtype=jnp.int32)[:, None]
    else:
        allowed = key_place < limit
    return jnp.where(allowed[None], scores, floor_score)


def attend_forward(queries, keys, values, limit, causal):
    length = queries.shape[0]
    block = min(512, length)
    outputs = []
    totals = []
    for first in range(0, length, block):
        span = first + block if causal else keys.shape[0]
        scores = masked_scores(queries[first : first + block], keys[:span], first, limit, causal)
        highest = jnp.max(scores, -1, keepdims=True)
        raised = jnp.exp(scores - highest)
        total = jnp.sum(raised, -1, keepdims=True)
        probs = (raised / total).astype(jnp.bfloat16)
        outputs.append(
            jnp.einsum("hqk,khd->qhd", probs, values[:span], preferred_element_type=jnp.float32)
        )
        totals.append((highest + jnp.log(total))[:, :, 0])
    return (jnp.concatenate(outputs, 0), jnp.concatenate(totals, 1))


def attend_backward(queries, keys, values, totals, grad_mixed, limit, causal):
    length = queries.shape[0]
    block = min(512, length)
    key_grads = jnp.zeros(keys.shape, jnp.float32)
    value_grads = jnp.zeros(values.shape, jnp.float32)
    query_grads = []
    for first in range(0, length, block):
        span = first + block if causal else keys.shape[0]
        rows = queries[first : first + block]
        grad_piece = grad_mixed[first : first + block]
        scores = masked_scores(rows, keys[:span], first, limit, causal)
        probs = jnp.exp(scores - totals[:, first : first + block, None])
        grad_probs = jnp.einsum(
            "qhd,khd->hqk", grad_piece, values[:span], preferred_element_type=jnp.float32
        )
        inner_sum = jnp.sum(probs * grad_probs, -1, keepdims=True)
        grad_scores = (probs * (grad_probs - inner_sum)).astype(jnp.bfloat16)
        query_grads.append(
            jnp.einsum("hqk,khd->qhd", grad_scores, keys[:span], preferred_element_type=jnp.float32)
        )
        key_grads = key_grads.at[:span].add(
            jnp.einsum("hqk,qhd->khd", grad_scores, rows, preferred_element_type=jnp.float32)
        )
        value_grads = value_grads.at[:span].add(
            jnp.einsum(
                "hqk,qhd->khd",
                probs.astype(jnp.bfloat16),
                grad_piece,
                preferred_element_type=jnp.float32,
            )
        )
    return (jnp.concatenate(query_grads, 0), key_grads, value_grads)


def run_forward(operands, causal):
    return attend_forward(operands[0], operands[1], operands[2], operands[3], causal)


def run_backward(operands, causal):
    return attend_backward(
        operands[0], operands[1], operands[2], operands[3], operands[4], operands[5], causal
    )


def gather_rows(normed):
    return lax.all_gather(normed, "mp", axis=0, tiled=True)


def spread_rows(term_fn, rows):
    return lax.psum_scatter(
        term_fn(jnp.int32(0), lax.axis_size("mp") * rows).astype(jnp.bfloat16),
        "mp",
        scatter_dimension=0,
        tiled=True,
    ).astype(jnp.float32)


def whole_rows(term_fn, local, start_row):
    full_rows = local.shape[0] * lax.axis_size("mp")
    term = term_fn(0, full_rows)
    placed = lax.dynamic_update_slice_in_dim(jnp.zeros_like(term), local, start_row, 0)
    return lax.psum((term + placed).astype(jnp.bfloat16), "mp").astype(jnp.float32)


def gather_grads(grad_branch):
    return lax.all_gather(grad_branch, "mp", axis=0, tiled=True)


def reduce_inputs(term_fn, rows):
    return lax.psum_scatter(
        term_fn(jnp.int32(0), lax.axis_size("mp") * rows).astype(jnp.bfloat16),
        "mp",
        scatter_dimension=0,
        tiled=True,
    ).astype(jnp.float32)


def body(
    tokens,
    memory,
    cotangent,
    lengths,
    memory_lengths,
    pair_ids,
    pair_counts,
    self_in,
    self_out,
    cross_in,
    cross_out,
    fc_in,
    fc_out,
    head_biases,
    inner_bias,
    norm_gains,
    feature_biases,
):
    shards = (self_in, self_out, cross_in, cross_out, fc_in, fc_out, head_biases, inner_bias)
    gathered = (
        lax.all_gather(shards[0], "dp", axis=1, tiled=True),
        lax.all_gather(shards[1], "dp", axis=1, tiled=True),
        lax.all_gather(shards[2], "dp", axis=1, tiled=True),
        lax.all_gather(shards[3], "dp", axis=1, tiled=True),
        lax.all_gather(shards[4], "dp", axis=0, tiled=True),
        lax.all_gather(shards[5], "dp", axis=1, tiled=True),
        lax.all_gather(shards[6], "dp", axis=2, tiled=True),
        lax.all_gather(shards[7], "dp", axis=1, tiled=True),
    )
    gains, shifts = (
        lax.all_gather(norm_gains, ("dp", "mp"), axis=1, tiled=True),
        lax.all_gather(feature_biases, ("dp", "mp"), axis=1, tiled=True),
    )
    local_rows, seq_count, width = tokens.shape
    memory_local = memory.shape[0]
    heads_here = head_biases.shape[1]
    head_size = gathered[6].shape[2]
    local_width = heads_here * head_size
    length = local_rows * lax.axis_size("mp")
    memory_length = memory_local * lax.axis_size("mp")
    shape_heads = (seq_count, length, heads_here, head_size)
    shape_memory = (seq_count, memory_length, heads_here, head_size)
    start_row = lax.axis_index("mp") * local_rows
    (
        w_self_in,
        w_self_out,
        w_cross_in,
        w_cross_out,
        feedforward_input_weight,
        feedforward_output_weight,
        w_heads,
        w_inner,
    ) = gathered
    bias_heads = w_heads.astype(jnp.float32).reshape(4, local_width)
    bias_inner = w_inner.astype(jnp.float32).reshape(-1)
    hidden_in = tokens.astype(jnp.float32)
    normed_one, unit_one, inverse_one = normalize(hidden_in, gains[0], shifts[0])
    rows_one = gather_rows(normed_one.astype(jnp.bfloat16))
    project = jnp.einsum("lsd,kde->ksle", rows_one, w_self_in, preferred_element_type=jnp.float32)
    queries_self = ((project[0] + bias_heads[0]) * 0.125).astype(jnp.bfloat16).reshape(shape_heads)
    keys_self = project[1].astype(jnp.bfloat16).reshape(shape_heads)
    values_self = (project[2] + bias_heads[1]).astype(jnp.bfloat16).reshape(shape_heads)
    mixed_self, totals_self = lax.map(
        partial(run_forward, causal=True), (queries_self, keys_self, values_self, lengths)
    )
    mixed_self = mixed_self.astype(jnp.bfloat16).reshape(seq_count, length, local_width)

    def self_term(start, count):
        slice_part = lax.dynamic_slice_in_dim(mixed_self, start, count, 1)
        return jnp.einsum("sle,ed->lsd", slice_part, w_self_out, preferred_element_type=jnp.float32)

    whole_one = whole_rows(self_term, hidden_in, start_row) + shifts[3]
    hidden_one = lax.dynamic_slice_in_dim(whole_one, start_row, local_rows, 0)
    normed_two, unit_two, inverse_two = normalize(hidden_one, gains[1], shifts[1])
    rows_two = normalize(whole_one, gains[1], shifts[1])[0].astype(jnp.bfloat16)
    memory_all = lax.all_gather(memory, "mp", axis=0, tiled=True)
    queries_cross = (
        (
            (
                jnp.einsum(
                    "lsd,de->sle", rows_two, w_cross_in[0], preferred_element_type=jnp.float32
                )
                + bias_heads[2]
            )
            * 0.125
        )
        .astype(jnp.bfloat16)
        .reshape(shape_heads)
    )
    memory_project = jnp.einsum(
        "msd,kde->ksme", memory_all, w_cross_in[1:], preferred_element_type=jnp.float32
    )
    keys_cross = memory_project[0].astype(jnp.bfloat16).reshape(shape_memory)
    values_cross = (memory_project[1] + bias_heads[3]).astype(jnp.bfloat16).reshape(shape_memory)
    mixed_cross, totals_cross = lax.map(
        partial(run_forward, causal=False),
        (queries_cross, keys_cross, values_cross, memory_lengths),
    )
    mixed_cross = mixed_cross.astype(jnp.bfloat16).reshape(seq_count, length, local_width)

    def cross_term(start, count):
        slice_part = lax.dynamic_slice_in_dim(mixed_cross, start, count, 1)
        return jnp.einsum(
            "sle,ed->lsd", slice_part, w_cross_out, preferred_element_type=jnp.float32
        )

    whole_two = whole_rows(cross_term, hidden_one, start_row) + shifts[4]
    hidden_two = lax.dynamic_slice_in_dim(whole_two, start_row, local_rows, 0)
    normed_three, unit_three, inverse_three = normalize(hidden_two, gains[2], shifts[2])
    third_rows = normalize(whole_two, gains[2], shifts[2])[0].astype(jnp.bfloat16)
    inner = (
        jnp.einsum(
            "wri,ix->wrx", third_rows, feedforward_input_weight, preferred_element_type=jnp.float32
        )
        + bias_inner
    )
    smooth_value, smooth_pull = jax.vjp(smooth_unit, inner)
    active_units = smooth_value.astype(jnp.bfloat16)

    def ffn_term(start, count):
        slice_part = lax.dynamic_slice_in_dim(active_units, start, count, 0)
        return jnp.einsum(
            "crx,xp->crp", slice_part, feedforward_output_weight, preferred_element_type=jnp.float32
        )

    output = (hidden_two + spread_rows(ffn_term, local_rows) + shifts[5]).astype(jnp.bfloat16)
    again = (
        lax.all_gather(shards[0], "dp", axis=1, tiled=True),
        lax.all_gather(shards[1], "dp", axis=1, tiled=True),
        lax.all_gather(shards[2], "dp", axis=1, tiled=True),
        lax.all_gather(shards[3], "dp", axis=1, tiled=True),
        lax.all_gather(shards[4], "dp", axis=0, tiled=True),
        lax.all_gather(shards[5], "dp", axis=1, tiled=True),
        lax.all_gather(shards[6], "dp", axis=2, tiled=True),
        lax.all_gather(shards[7], "dp", axis=1, tiled=True),
    )
    (
        w_self_in,
        w_self_out,
        w_cross_in,
        w_cross_out,
        feedforward_input_weight,
        feedforward_output_weight,
        w_heads,
        w_inner,
    ) = again
    counts = pair_counts.astype(jnp.float32)
    matches = (pair_ids[:, None] == jnp.arange(counts.shape[0], dtype=jnp.int32)[None, :]).astype(
        jnp.float32
    )
    own_count = jnp.sum(matches * counts[None, :], -1)
    scale = jnp.mean(counts) / own_count
    positions = start_row + jnp.arange(local_rows, dtype=jnp.int32)
    valid = (positions[:, None] < lengths[None, :]).astype(jnp.float32)
    grad_out = cotangent.astype(jnp.float32) * (valid * scale[None, :])[:, :, None]
    gradient_rows3 = gather_grads(grad_out.astype(jnp.bfloat16))
    gradient_feedforward_output = jnp.einsum(
        "ytb,yth->bh", active_units, gradient_rows3, preferred_element_type=jnp.float32
    )
    grad_active = jnp.einsum(
        "vmr,yr->vmy", gradient_rows3, feedforward_output_weight, preferred_element_type=jnp.float32
    )
    gradient_inner_hidden = smooth_pull(grad_active)[0].astype(jnp.bfloat16)
    grad_fc_in = jnp.einsum(
        "eoc,eoi->ci", third_rows, gradient_inner_hidden, preferred_element_type=jnp.float32
    )
    grad_inner_bias = jnp.sum(gradient_inner_hidden.astype(jnp.float32), (0, 1)).reshape(
        w_inner.shape
    )

    def ffn_back(start, count):
        slice_part = lax.dynamic_slice_in_dim(gradient_inner_hidden, start, count, 0)
        return jnp.einsum(
            "mou,tu->mot", slice_part, feedforward_input_weight, preferred_element_type=jnp.float32
        )

    grad_normed3 = reduce_inputs(ffn_back, local_rows)
    back_three, gain_three, shift_three = normalize_back(
        grad_normed3, gains[2], unit_three, inverse_three
    )
    grad_hidden2 = grad_out + back_three
    grad_rows2 = gather_grads(grad_hidden2.astype(jnp.bfloat16))
    grad_cross_out = jnp.einsum(
        "sle,lsd->ed", mixed_cross, grad_rows2, preferred_element_type=jnp.float32
    )
    grad_mixed = (
        jnp.einsum("lsd,ed->sle", grad_rows2, w_cross_out, preferred_element_type=jnp.float32)
        .astype(jnp.bfloat16)
        .reshape(shape_heads)
    )
    grad_query, grad_key, grad_value = lax.map(
        partial(run_backward, causal=False),
        (queries_cross, keys_cross, values_cross, totals_cross, grad_mixed, memory_lengths),
    )
    grad_query = (grad_query.astype(jnp.bfloat16) * 0.125).reshape(seq_count, length, local_width)
    memory_stack = jnp.stack(
        [
            grad_key.astype(jnp.bfloat16).reshape(seq_count, memory_length, local_width),
            grad_value.astype(jnp.bfloat16).reshape(seq_count, memory_length, local_width),
        ]
    )
    grad_cross_query = jnp.einsum(
        "lsd,sle->de", rows_two, grad_query, preferred_element_type=jnp.float32
    )
    grad_cross_pair = jnp.einsum(
        "msd,ksme->kde", memory_all, memory_stack, preferred_element_type=jnp.float32
    )
    grad_cross_in = jnp.concatenate([grad_cross_query[None], grad_cross_pair], 0)
    bias_query_cross = jnp.sum(grad_query.astype(jnp.float32), (0, 1))
    bias_value_cross = jnp.sum(memory_stack[1].astype(jnp.float32), (0, 1))

    def memory_back(start, count):
        return jnp.einsum(
            "ksme,kde->msd", memory_stack, w_cross_in[1:], preferred_element_type=jnp.float32
        )

    grad_memory = reduce_inputs(memory_back, memory_local)

    def cross_back(start, count):
        slice_part = lax.dynamic_slice_in_dim(grad_query, start, count, 1)
        return jnp.einsum(
            "sle,de->lsd", slice_part, w_cross_in[0], preferred_element_type=jnp.float32
        )

    grad_normed2 = reduce_inputs(cross_back, local_rows)
    back_two, gain_two, shift_two = normalize_back(grad_normed2, gains[1], unit_two, inverse_two)
    grad_hidden1 = grad_hidden2 + back_two
    grad_rows1 = gather_grads(grad_hidden1.astype(jnp.bfloat16))
    grad_self_out = jnp.einsum(
        "sle,lsd->ed", mixed_self, grad_rows1, preferred_element_type=jnp.float32
    )
    grad_mixed = (
        jnp.einsum("lsd,ed->sle", grad_rows1, w_self_out, preferred_element_type=jnp.float32)
        .astype(jnp.bfloat16)
        .reshape(shape_heads)
    )
    grad_query, grad_key, grad_value = lax.map(
        partial(run_backward, causal=True),
        (queries_self, keys_self, values_self, totals_self, grad_mixed, lengths),
    )
    flat_shape = (seq_count, length, local_width)
    self_stack = jnp.stack(
        [
            (grad_query.astype(jnp.bfloat16) * 0.125).reshape(flat_shape),
            grad_key.astype(jnp.bfloat16).reshape(flat_shape),
            grad_value.astype(jnp.bfloat16).reshape(flat_shape),
        ]
    )
    grad_self_in = jnp.einsum(
        "lsd,ksle->kde", rows_one, self_stack, preferred_element_type=jnp.float32
    )
    bias_query_self = jnp.sum(self_stack[0].astype(jnp.float32), (0, 1))
    bias_value_self = jnp.sum(self_stack[2].astype(jnp.float32), (0, 1))

    def self_back(start, count):
        slice_part = lax.dynamic_slice_in_dim(self_stack, start, count, 2)
        return jnp.einsum(
            "ksle,kde->lsd", slice_part, w_self_in, preferred_element_type=jnp.float32
        )

    grad_normed1 = reduce_inputs(self_back, local_rows)
    back_one, gain_one, shift_one = normalize_back(grad_normed1, gains[0], unit_one, inverse_one)
    grad_tokens = grad_hidden1 + back_one
    grad_heads = jnp.stack(
        [bias_query_self, bias_value_self, bias_query_cross, bias_value_cross]
    ).reshape(w_heads.shape)
    gain_grads = jnp.stack([gain_one, gain_two, gain_three])
    shift_grads = jnp.stack(
        [
            shift_one,
            shift_two,
            shift_three,
            jnp.sum(grad_hidden1, (0, 1)),
            jnp.sum(grad_hidden2, (0, 1)),
            jnp.sum(grad_out, (0, 1)),
        ]
    )
    grad_gains, grad_shifts = (
        lax.psum_scatter(gain_grads, ("dp", "mp"), scatter_dimension=1, tiled=True),
        lax.psum_scatter(shift_grads, ("dp", "mp"), scatter_dimension=1, tiled=True),
    )
    all_sums = (
        lax.psum_scatter(
            grad_self_in.astype(jnp.bfloat16), "dp", scatter_dimension=1, tiled=True
        ).astype(jnp.float32),
        lax.psum_scatter(
            grad_self_out.astype(jnp.bfloat16), "dp", scatter_dimension=1, tiled=True
        ).astype(jnp.float32),
        lax.psum_scatter(
            grad_cross_in.astype(jnp.bfloat16), "dp", scatter_dimension=1, tiled=True
        ).astype(jnp.float32),
        lax.psum_scatter(
            grad_cross_out.astype(jnp.bfloat16), "dp", scatter_dimension=1, tiled=True
        ).astype(jnp.float32),
        lax.psum_scatter(
            grad_fc_in.astype(jnp.bfloat16), "dp", scatter_dimension=0, tiled=True
        ).astype(jnp.float32),
        lax.psum_scatter(
            gradient_feedforward_output.astype(jnp.bfloat16), "dp", scatter_dimension=1, tiled=True
        ).astype(jnp.float32),
        lax.psum_scatter(
            grad_heads.astype(jnp.bfloat16), "dp", scatter_dimension=2, tiled=True
        ).astype(jnp.float32),
        lax.psum_scatter(
            grad_inner_bias.astype(jnp.bfloat16), "dp", scatter_dimension=1, tiled=True
        ).astype(jnp.float32),
    )
    (
        sum_self_in,
        sum_self_out,
        sum_cross_in,
        sum_cross_out,
        sum_fc_in,
        sum_fc_out,
        sum_heads,
        sum_inner,
    ) = all_sums
    return (
        output,
        grad_tokens,
        grad_memory,
        sum_self_in,
        sum_self_out,
        sum_cross_in,
        sum_cross_out,
        sum_fc_in,
        sum_fc_out,
        sum_heads,
        sum_inner,
        grad_gains,
        grad_shifts,
    )


LOG2E = 1.4426950408889634
LN2 = 0.6931471805599453
VM = pltpu.VMEM
ANYM = pltpu.HBM
F32 = jnp.float32
BF = jnp.bfloat16
NT_DIMS = (((1,), (1,)), ((), ()))
TN_DIMS = (((0,), (0,)), ((), ()))


def mm(a, b):
    return jnp.dot(a, b, preferred_element_type=F32)


def mm_nt(a, b):
    return lax.dot_general(a, b, NT_DIMS, preferred_element_type=F32)


def mm_tn(a, b):
    return lax.dot_general(a, b, TN_DIMS, preferred_element_type=F32)


def params_of(limit_mib, **more):
    return pltpu.CompilerParams(vmem_limit_bytes=limit_mib * 1024 * 1024, **more)


def cost(flops, data, exps=0):
    return pl.CostEstimate(flops=int(flops), bytes_accessed=int(data), transcendentals=int(exps))


def gated_call(after, kernel, *, grid_spec, out_shape, through=(), input_output_aliases=None, **settings):
    scalars, reads = grid_spec["num_scalar_prefetch"], len(grid_spec["in_specs"])
    used = scalars + reads
    after, through = values_of(after), list(through)
    single = not isinstance(out_shape, list)
    shapes = [out_shape] if single else out_shape
    out_specs = [grid_spec["out_specs"]] if single else list(grid_spec["out_specs"])
    outs, waits = len(shapes), len(after) + len(through)

    def body_of(*refs):
        kernel(*refs[:used], *refs[used + waits : used + waits + outs], *refs[used + waits + outs + len(through) :])

    anywhere = pl.BlockSpec(memory_space=ANYM)
    spec = dict(
        grid_spec,
        in_specs=list(grid_spec["in_specs"]) + [anywhere] * waits,
        out_specs=out_specs + [anywhere] * len(through),
    )
    aliases = dict(input_output_aliases or {})
    aliases.update({used + len(after) + i: outs + i for i in range(len(through))})
    passed = values_of(through)
    call = pl.pallas_call(body_of,
        grid_spec=pltpu.PrefetchScalarGridSpec(**spec),
        out_shape=list(shapes) + [jax.ShapeDtypeStruct(value.shape, value.dtype) for value in passed],
        input_output_aliases=aliases,
        **settings,
    )

    def run(*operands):
        results = call(*values_of(operands), *after, *passed)
        for cell, value in zip(through, results[outs:]):
            cell.value = value
        return results[0] if single else results[:outs]

    return run


def flow_meta(kind):
    corners = [(0, 0), (1, 0), (0, 1), (1, 1)]
    if kind == "zxy":
        near = [[(k, y, 0, x) for k in range(4)] for (x, y) in corners]
    else:
        near = [[(k, y, 0, x) for (x, y) in corners] for k in range(4)]
    return near + [[(k, y, 1, x) for quad in near for (k, y, _, x) in quad]]


def place_of(info, meta):
    k, y, c, x = meta
    slab = info[3] if x == 0 else 1 - info[3]
    zz = lax.rem(info[0] - k + 4, 4)
    yy = info[1] if y == 0 else 1 - info[1]
    cc = info[2] if c == 0 else 1 - info[2]
    return (slab, pl.multiple_of(zz * 256 + yy * 128 + cc * 64, 64))


def start_weight(info, pieces, kind, first, width, buffer, sems):
    for ref, metas in zip(pieces, flow_meta(kind)):
        for j, meta in enumerate(metas):
            slab, row = place_of(info, meta)
            pltpu.make_async_copy(
                ref.at[j, :, pl.ds(first, width)],
                buffer.at[slab, pl.ds(row, 64), :],
                sems.at[slab],
            ).start()


def start_all(pieces, first, width, buffer, sems):
    (ref,) = pieces
    for device in range(32):
        pltpu.make_async_copy(
            ref.at[device, :, pl.ds(first, width)],
            buffer.at[device % 2, pl.ds(device // 2 * 64, 64), :],
            sems.at[device % 2],
        ).start()


def wait_weight(buffer, sems, slab):
    pltpu.make_async_copy(buffer.at[slab], buffer.at[slab], sems.at[slab]).wait()


def ln_parts(hidden):
    average = jnp.mean(hidden, -1, keepdims=True)
    centred = hidden - average
    inverse = lax.rsqrt(jnp.mean(centred * centred, -1, keepdims=True) + eps)
    return (centred * inverse, inverse)


def ln_back(grad_normed, gain, unit, inverse):
    grad_unit = grad_normed * gain
    return inverse * (
        grad_unit
        - jnp.mean(grad_unit, -1, keepdims=True)
        - unit * jnp.mean(grad_unit * unit, -1, keepdims=True)
    )


def row_sum(values):
    return jnp.sum(values, 0, keepdims=True)


def transposed(values):
    return values.T


ROWS = 256
QB = 256


def qkv_kernel(info, par, x_ref, *rest):
    pieces, rest = rest[:10], rest[10:]
    q_ref, k_ref, v_ref, nt_ref, wq, wk, wv, sems = rest
    weights = (wq, wk, wv)

    @pl.when(pl.program_id(0) == 0)
    def _():
        start_self(info, pieces, weights, sems)
        for t in range(3):
            for slab in range(2):
                wait_weight(weights[t], sems.at[t], slab)

    unit, _ = ln_parts(x_ref[...].astype(F32))
    normed = (unit * par[0:1, :] + par[3:4, :]).astype(BF)
    nt_ref[...] = transposed(normed)
    for t in range(3):
        for slab in range(2):


            cols = slice(slab * 512, slab * 512 + 512)
            value = mm(normed, weights[t][slab])
            if t == 0:
                value = (value + par[9:10, cols]) * (0.125 * LOG2E)
            if t == 2:
                value = value + par[10:11, cols]
            (q_ref, k_ref, v_ref)[t][:, cols] = value.astype(BF)


def start_self(info, pieces, weights, sems):
    start_weight(info, pieces[:5], "zxy", 0, 512, weights[0], sems.at[0])
    start_weight(info, pieces[5:], "xyz", 0, 512, weights[1], sems.at[1])
    start_weight(info, pieces[:5], "zxy", 512, 512, weights[2], sems.at[2])


def call_qkv(info, par, x, pieces, after=(), through=()):
    n = x.shape[0]
    out = jax.ShapeDtypeStruct((n, 1024), BF)
    rows = pl.BlockSpec((ROWS, 1024), lambda i, s: (i, 0))
    return gated_call(
        after,
        qkv_kernel,
        grid_spec=dict(
            num_scalar_prefetch=1,
            grid=(n // ROWS,),
            in_specs=[pl.BlockSpec((24, 1024), lambda i, s: (0, 0)), rows]
            + [pl.BlockSpec(memory_space=ANYM)] * 10,
            out_specs=[rows, rows, rows, pl.BlockSpec((1024, ROWS), lambda i, s: (0, i))],
            scratch_shapes=[VM((2, 1024, 512), BF)] * 3 + [pltpu.SemaphoreType.DMA((3, 2))],
        ),
        out_shape=[out, out, out, jax.ShapeDtypeStruct((1024, n), BF)],
        compiler_params=params_of(60),
        cost_estimate=cost(6.4e9, 16e6),
        through=through,
        name="project_self",
    )(info, par, x, *pieces)


def kv_kernel(info, par, x_ref, *rest):
    pieces, rest = rest[:1], rest[1:]
    k_ref, v_ref, nt_ref, wk, wv, sems = rest
    weights = (wk, wv)

    @pl.when(pl.program_id(0) == 0)
    def _():
        for t in range(2):
            start_all(pieces, t * 512, 512, weights[t], sems.at[t])
        for t in range(2):
            for slab in range(2):
                wait_weight(weights[t], sems.at[t], slab)

    rows = x_ref[...]
    nt_ref[...] = transposed(rows)
    for t in range(2):
        for slab in range(2):


            cols = slice(slab * 512, slab * 512 + 512)
            value = mm(rows, weights[t][slab])
            if t == 1:
                value = value + par[12:13, cols]
            (k_ref, v_ref)[t][:, cols] = value.astype(BF)


def call_kv(info, par, x, pieces, after=(), through=()):
    n = x.shape[0]
    out = jax.ShapeDtypeStruct((n, 1024), BF)
    rows = pl.BlockSpec((ROWS, 1024), lambda i, s: (i, 0))
    return gated_call(
        after,
        kv_kernel,
        grid_spec=dict(
            num_scalar_prefetch=1,
            grid=(n // ROWS,),
            in_specs=[pl.BlockSpec((24, 1024), lambda i, s: (0, 0)), rows]
            + [pl.BlockSpec(memory_space=ANYM)],
            out_specs=[rows, rows, pl.BlockSpec((1024, ROWS), lambda i, s: (0, i))],
            scratch_shapes=[VM((2, 1024, 512), BF)] * 2 + [pltpu.SemaphoreType.DMA((2, 2))],
        ),
        out_shape=[out, out, jax.ShapeDtypeStruct((1024, n), BF)],
        compiler_params=params_of(60),
        cost_estimate=cost(4.3e9, 12e6),
        through=through,
        name="project_memory",
    )(info, par, x, *pieces)


def lane_ids(rows):
    return lax.broadcasted_iota(jnp.int32, (rows, 128), 1)


def split3(column):
    high = column.astype(BF)
    rest = column - high.astype(F32)
    middle = rest.astype(BF)
    return (high, middle, (rest - middle.astype(F32)).astype(BF))


def attend_kernel(causal, info, q_ref, k_ref, v_ref, *rest):
    o_ref, lse_ref = rest[-2:]
    lse_ref = lse_ref.at[0]
    n, nk = q_ref.shape[0], k_ref.shape[0]
    lanes_k, lanes_q = lane_ids(nk), lane_ids(QB)
    lane_all = lane_ids(n)

    one = jnp.ones((), BF)
    zero = jnp.zeros((), BF)
    k_aug, v_aug = [], []
    for head in range(2):
        own = (lanes_k >= 64) if head else (lanes_k < 64)
        spare = 0 if head else 64
        keys = jnp.where(own, k_ref[...], zero)
        if not causal:
            place = lax.broadcasted_iota(jnp.int32, (nk, 128), 0)
            shut = jnp.where(place < info[4], 0.0, floor_score).astype(BF)
            keys = jnp.where(lanes_k == spare, shut, keys)
        k_aug.append(keys)
        v_aug.append(jnp.where(own, v_ref[...], jnp.where(lanes_k == spare, one, zero)))
    items = [(first, head) for first in range(0, n, QB) for head in range(2)]

    def scores_of(first, head):
        span = first + QB if causal else nk
        block = q_ref[first : first + QB, :]
        query = block if causal else jnp.where(lanes_q == (0 if head else 64), one, block)
        scores = mm_nt(query, k_aug[head][:span])
        if causal:
            row = lax.broadcasted_iota(jnp.int32, (QB, QB), 0)
            col = lax.broadcasted_iota(jnp.int32, (QB, QB), 1)
            last = jnp.where(col <= row, scores[:, first:], floor_score)
            scores = jnp.concatenate([scores[:, :first], last], 1) if first else last
        return scores

    ahead = scores_of(*items[0])
    for index, (first, head) in enumerate(items):
        scores = ahead
        if index + 1 < len(items):
            ahead = scores_of(*items[index + 1])
        span = first + QB if causal else nk
        highest = jnp.max(scores, -1, keepdims=True)
        raised = jnp.exp2(scores - highest).astype(BF)
        mixed = mm(raised, v_aug[head][:span])
        total = jnp.sum(jnp.where(lanes_q == (0 if head else 64), mixed, 0.0), -1, keepdims=True)
        out, lse = mixed * (1.0 / total), highest + jnp.log2(total)
        if head == 0:
            out_a, lse_a = out, lse
        else:
            o_ref[first : first + QB, :] = jnp.where(lanes_q < 64, out_a, out).astype(BF)
            lse_ref[first : first + QB, :] = jnp.where(lanes_q < 64, lse, lse_a)


def call_attend(info, q, k, v, causal, first, count, earlier=None, after=(), through=()):
    n, nk = q.shape[0], k.shape[0]
    part = (0.625 if causal else 1.0) * count / 8
    heads = lambda rows: pl.BlockSpec((rows, 128), lambda i, s: (0, i + first))
    held = () if earlier is None else tuple(earlier)
    return gated_call(
        after,
        partial(attend_kernel, causal),
        grid_spec=dict(
            num_scalar_prefetch=1,
            grid=(count,),
            in_specs=[heads(n), heads(nk), heads(nk)] + [pl.BlockSpec(memory_space=ANYM)] * len(held),
            out_specs=[heads(n), pl.BlockSpec((1, n, 128), lambda i, s: (i + first, 0, 0))],
        ),
        out_shape=[jax.ShapeDtypeStruct((n, 1024), BF), jax.ShapeDtypeStruct((8, n, 128), F32)],
        input_output_aliases={4: 0, 5: 1} if held else {},
        compiler_params=params_of(60),
        cost_estimate=cost(110.4e9 * part, 1e6),
        name="attend_self" if causal else "attend_cross",
    )(info, q, k, v, *held)


def attend_back_kernel(causal, info, q_ref, k_ref, v_ref, o_ref, g_ref, lse_ref, *rest):
    dq_ref, dk_ref, dv_ref, bias_ref, acc = rest[-5:]
    lse_ref = lse_ref.at[0]
    n, nk = q_ref.shape[0], k_ref.shape[0]
    lanes_k, lanes_q = lane_ids(nk), lane_ids(n)
    one = jnp.ones((), BF)
    zero = jnp.zeros((), BF)
    block_rows = 256 if causal else 512
    q_all, g_all = q_ref[...], g_ref[...]
    k_turned = k_ref[...].T
    product = g_all.astype(F32) * o_ref[...].astype(F32)
    row = lax.broadcasted_iota(jnp.int32, (128, 128), 0)
    col = lax.broadcasted_iota(jnp.int32, (128, 128), 1)
    crossing = jnp.where((row < 64) != (col < 64), one, zero)
    inner = sum(mm(part, crossing) for part in split3(product))
    slot_q, slot_k = lanes_q % 64, lanes_k % 64

    def in_slots(column):
        first, second, third = split3(-column)
        rest = jnp.where(slot_q == 2, third, jnp.where(slot_q == 3, one, zero))
        return jnp.where(slot_q == 0, first, jnp.where(slot_q == 1, second, rest))

    spare_q, spare_g = in_slots(lse_ref[...]), in_slots(inner)
    spare_v = jnp.where(slot_k < 3, one, zero)
    spare_k = spare_v
    if not causal:
        place = lax.broadcasted_iota(jnp.int32, (nk, 128), 0)
        shut = jnp.where(place < info[4], 0.0, floor_score).astype(BF)
        spare_k = jnp.where(slot_k == 3, shut, spare_k)
    k_all, v_all = k_ref[...], v_ref[...]
    sets = []
    for head in range(2):
        own_k = (lanes_k >= 64) if head else (lanes_k < 64)
        own_q = (lanes_q >= 64) if head else (lanes_q < 64)
        sets.append(
            (
                jnp.where(own_q, q_all, zero),
                jnp.where(own_q, g_all, zero),
                jnp.where(own_q, q_all, spare_q),
                jnp.where(own_q, g_all, spare_g),
                jnp.where(own_k, k_all, spare_k),
                jnp.where(own_k, v_all, spare_v),
            )
        )
    items = [(first, head) for first in range(0, nk, block_rows) for head in range(2)]

    def scores_of(first, head):
        from_q = first if causal else 0
        q_own, g_own, q_aug, g_aug, k_aug, v_aug = sets[head]
        keys = slice(first, first + block_rows)
        scores = mm_nt(k_aug[keys], q_aug[from_q:])
        if causal:
            row = lax.broadcasted_iota(jnp.int32, (block_rows, block_rows), 0)
            col = lax.broadcasted_iota(jnp.int32, (block_rows, block_rows), 1)
            head_part = jnp.where(col >= row, scores[:, :block_rows], floor_score)
            if first + block_rows < n:
                scores = jnp.concatenate([head_part, scores[:, block_rows:]], 1)
            else:
                scores = head_part
        return (scores, mm_nt(v_aug[keys], g_aug[from_q:]))

    ahead = scores_of(*items[0])
    acc[...] = jnp.zeros(acc.shape, F32)
    bias = None
    for index, (first, head) in enumerate(items):
        scores, grad_probs = ahead
        if index + 1 < len(items):
            ahead = scores_of(*items[index + 1])
        from_q = first if causal else 0
        q_own, g_own, q_aug, g_aug, k_aug, v_aug = sets[head]
        keys = slice(first, first + block_rows)
        probs = jnp.exp2(scores)
        grad_scores = (probs * grad_probs).astype(BF)
        add_v = mm(probs.astype(BF), g_own[from_q:])
        add_k = mm(grad_scores, q_own[from_q:])
        own = slice(64 * head, 64 * head + 64)
        acc[own, from_q:] += mm(k_turned[own, keys], grad_scores)
        if head == 0:
            dv, dk = add_v, add_k
        else:
            dv = (dv + add_v).astype(BF)
            dv_ref[keys, :] = dv
            dk_ref[keys, :] = ((dk + add_k) * LN2).astype(BF)
            sums = row_sum(dv.astype(F32))
            bias = sums if bias is None else bias + sums
    bias_ref[1:2, :] = bias
    dq = acc[...].T.astype(BF) * jnp.asarray(0.125, BF)
    dq_ref[...] = dq
    bias_ref[0:1, :] = row_sum(dq.astype(F32))


def own_or_other(info, other):
    return 1 - info[3] if other else info[3]


def call_attend_back(info, q, k, v, o, g, lse, causal, first, count, earlier=None, other=None, after=(), through=()):
    n, nk = q.shape[0], k.shape[0]
    part = (0.625 if causal else 1.0) * count / 8
    place = lambda i, s: i + first if other is None else i + first + 4 * own_or_other(s, other)
    heads = lambda rows: pl.BlockSpec((rows, 128), lambda i, s: (0, place(i, s)))
    out = lambda rows: jax.ShapeDtypeStruct((rows, 1024), BF)
    held = () if earlier is None else tuple(earlier)
    return gated_call(
        after,
        partial(attend_back_kernel, causal),
        grid_spec=dict(
            num_scalar_prefetch=1,
            grid=(count,),
            in_specs=[heads(n), heads(nk), heads(nk), heads(n), heads(n)]
            + [pl.BlockSpec((1, n, 128), lambda i, s: (place(i, s), 0, 0))]
            + [pl.BlockSpec(memory_space=ANYM)] * len(held),
            out_specs=[heads(n), heads(nk), heads(nk), heads(8)],
            scratch_shapes=[VM((128, n), F32)],
        ),
        out_shape=[out(n), out(nk), out(nk), jax.ShapeDtypeStruct((8, 1024), F32)],
        input_output_aliases={7: 0, 8: 1, 9: 2, 10: 3} if held else {},
        compiler_params=params_of(60),
        cost_estimate=cost(142.6e9 * part, 1e6),
        name="attend_back_self" if causal else "attend_back_cross",
    )(info, q, k, v, o, g, lse, *held)


def after_self_kernel(info, par, x_ref, o_ref, *rest):
    pieces, rest = rest[:1], rest[1:]
    h_ref, q_ref, nt_ref, wo, wq, sems = rest

    @pl.when(pl.program_id(0) == 0)
    def _():
        start_all(pieces, 1024, 512, wo, sems.at[0])
        start_all(pieces, 1536, 512, wq, sems.at[1])
        for slab in range(2):
            wait_weight(wo, sems.at[0], slab)
        for slab in range(2):
            wait_weight(wq, sems.at[1], slab)

    total = x_ref[...].astype(F32) + par[6:7, :]
    for slab in range(2):


        total = total + mm_nt(o_ref[:, slab * 512 : slab * 512 + 512], wo[slab])
    h_ref[...] = total
    unit, _ = ln_parts(total)
    normed = (unit * par[1:2, :] + par[4:5, :]).astype(BF)
    nt_ref[...] = transposed(normed)
    for slab in range(2):


        cols = slice(slab * 512, slab * 512 + 512)
        value = (mm(normed, wq[slab]) + par[11:12, cols]) * (0.125 * LOG2E)
        q_ref[:, cols] = value.astype(BF)


def call_after_self(info, par, x, o, pieces, after=(), through=()):
    n = x.shape[0]
    rows = pl.BlockSpec((ROWS, 1024), lambda i, s: (i, 0))
    return gated_call(
        after,
        after_self_kernel,
        grid_spec=dict(
            num_scalar_prefetch=1,
            grid=(n // ROWS,),
            in_specs=[pl.BlockSpec((24, 1024), lambda i, s: (0, 0)), rows, rows]
            + [pl.BlockSpec(memory_space=ANYM)],
            out_specs=[rows, rows, pl.BlockSpec((1024, ROWS), lambda i, s: (0, i))],
            scratch_shapes=[VM((2, 1024, 512), BF)] * 2 + [pltpu.SemaphoreType.DMA((2, 2))],
        ),
        out_shape=[
            jax.ShapeDtypeStruct((n, 1024), F32),
            jax.ShapeDtypeStruct((n, 1024), BF),
            jax.ShapeDtypeStruct((1024, n), BF),
        ],
        compiler_params=params_of(60),
        cost_estimate=cost(4.3e9, 16e6),
        through=through,
        name="after_self",
    )(info, par, x, o, *pieces)


def after_cross_kernel(info, par, scale, h_in, o_ref, cot_ref, *rest):
    pieces, rest = rest[:1], rest[1:]
    h_ref, n_ref, nt_ref, g_ref, gt_ref, gsum_ref, wo, sems = rest
    step = pl.program_id(0)

    @pl.when(step == 0)
    def _():
        start_all(pieces, 4096, 512, wo, sems)
        for slab in range(2):
            wait_weight(wo, sems, slab)

    place = step * ROWS + lax.broadcasted_iota(jnp.int32, (ROWS, 1), 0)
    weight = jnp.where(place < info[5], scale[0, 0], 0.0)
    grad = cot_ref[...].astype(F32) * weight
    rounded = grad.astype(BF)
    g_ref[...] = rounded
    gt_ref[...] = transposed(rounded)
    sums = row_sum(grad)

    @pl.when(step == 0)
    def _():
        gsum_ref[...] = jnp.zeros(gsum_ref.shape, F32)

    gsum_ref[0:1, :] += sums
    total = h_in[...] + par[7:8, :]
    for slab in range(2):


        total = total + mm_nt(o_ref[:, slab * 512 : slab * 512 + 512], wo[slab])
    h_ref[...] = total
    unit, _ = ln_parts(total)
    normed = (unit * par[2:3, :] + par[5:6, :]).astype(BF)
    n_ref[...] = normed
    nt_ref[...] = transposed(normed)


def call_after_cross(info, par, scale, h, o, cot, pieces, after=(), through=()):
    n = h.shape[0]
    rows = pl.BlockSpec((ROWS, 1024), lambda i, s: (i, 0))
    turned = pl.BlockSpec((1024, ROWS), lambda i, s: (0, i))
    act = jax.ShapeDtypeStruct((n, 1024), BF)
    act_t = jax.ShapeDtypeStruct((1024, n), BF)
    return gated_call(
        after,
        after_cross_kernel,
        grid_spec=dict(
            num_scalar_prefetch=1,
            grid=(n // ROWS,),
            in_specs=[
                pl.BlockSpec((24, 1024), lambda i, s: (0, 0)),
                pl.BlockSpec((8, 128), lambda i, s: (0, 0)),
                rows,
                rows,
                rows,
            ]
            + [pl.BlockSpec(memory_space=ANYM)],
            out_specs=[rows, rows, turned, rows, turned, pl.BlockSpec((8, 1024), lambda i, s: (0, 0))],
            scratch_shapes=[VM((2, 1024, 512), BF), pltpu.SemaphoreType.DMA((2,))],
        ),
        out_shape=[
            jax.ShapeDtypeStruct((n, 1024), F32),
            act,
            act_t,
            act,
            act_t,
            jax.ShapeDtypeStruct((8, 1024), F32),
        ],
        compiler_params=params_of(60),
        cost_estimate=cost(2.2e9, 26e6),
        through=through,
        name="after_cross",
    )(info, par, scale, h, o, cot, *pieces)


GELU_A = 0.7978845608028654
GELU_B = 0.044715


def store_blocks(info, temp, send_ref, keep_ref, zrel, kind, width):
    for yrel in range(2):
        yy = info[1] if yrel == 0 else 1 - info[1]
        for crel in range(2):
            cc = info[2] if crel == 0 else 1 - info[2]
            row = pl.multiple_of(yy * 128 + cc * 64, 64)
            block = temp[pl.ds(row, 64), :]
            target = send_ref if crel else keep_ref
            if kind == "zxy":
                target[yrel, 0, zrel, :, :] = block
            else:
                target[zrel, yrel, 0, :, :] = block


FFB = 512
FFR = 512


def ffn_kernel(info, par, bias_ref, n_ref, nt_ref, g_ref, gt_ref, h_ref, *rest):
    pieces, rest = rest[:6], rest[6:]
    (out_ref, other_ref, dn_ref, send_ref, keep_ref, dbias_ref, w_in, w_out, acc, active, du, temp, sems) = rest
    half, part = pl.program_id(0), pl.program_id(1)
    parts = pl.num_programs(1)
    n = n_ref.shape[0]
    slab = lax.rem(half + info[3], 2)
    first_step = (half == 0) & (part == 0)

    @pl.when(first_step)
    def _():
        start_all(pieces[:1], 2048, 2048, w_in, sems.at[0])
        start_weight(info, pieces[1:], "xyz", 0, 2048, w_out, sems.at[1])
        acc[...] = jnp.zeros(acc.shape, F32)
        dn_ref[...] = jnp.zeros(dn_ref.shape, F32)

    @pl.when(part == 0)
    def _():
        wait_weight(w_in, sems.at[0], slab)
        wait_weight(w_out, sems.at[1], slab)

    cols = pl.ds(pl.multiple_of(part * FFB, FFB), FFB)
    first = w_in.at[slab, :, cols]
    second = w_out.at[slab, :, cols]
    total_bias = None
    chunks = [slice(start, start + FFR) for start in range(0, n, FFR)]

    def products(rows):
        return (mm(n_ref[rows, :], first[...]) + bias_ref[0:1, :], mm(g_ref[rows, :], second[...]))

    ahead = products(chunks[0])
    for index, rows in enumerate(chunks):
        u, dr = ahead
        if index + 1 < len(chunks):
            ahead = products(chunks[index + 1])
        square = u * u
        bend = jnp.tanh(u * (GELU_A + GELU_A * GELU_B * square))
        half_up = 0.5 + 0.5 * bend
        r = (u * half_up).astype(BF)
        active[rows, :] = r
        slope = half_up + 0.5 * u * (1.0 - bend * bend) * (GELU_A + 3.0 * GELU_A * GELU_B * square)
        d = (dr * slope).astype(BF)
        du[rows, :] = d
        sums = row_sum(d.astype(F32))
        total_bias = sums if total_bias is None else total_bias + sums
        acc[rows, :] += mm_nt(r, second[...])
        dn_ref[rows, :] += mm_nt(d, first[...])

    dbias_ref[0:1, :] = total_bias
    for zrel in range(4):
        zz = lax.rem(info[0] + zrel, 4)
        rows = pl.ds(pl.multiple_of(zz * 256, 256), 256)
        for kind, (left, right) in enumerate(((nt_ref, du), (gt_ref, active))):
            temp[kind] = mm(left[rows, :], right[...]).astype(BF)
            for yrel in range(2):
                yy = info[1] if yrel == 0 else 1 - info[1]
                for crel, target in enumerate((keep_ref, send_ref)):
                    cc = info[2] if crel == 0 else 1 - info[2]
                    row = pl.multiple_of(yy * 128 + cc * 64, 64)
                    target[yrel, 0, zrel, kind, :, :] = temp[kind, pl.ds(row, 64), :]

    @pl.when((half == 1) & (part == parts - 1))
    def _():
        for chunk in range(n // ROWS):
            start = lax.rem(info[3] * (n // 2) + chunk * ROWS, n)
            rows = pl.ds(pl.multiple_of(start, ROWS), ROWS)
            value = h_ref[rows, :] + acc[rows, :] + par[8:9, :]
            target = out_ref if chunk * ROWS < n // 2 else other_ref
            at = chunk * ROWS % (n // 2)
            target[at : at + ROWS, :] = value.astype(BF)


def call_ffn(info, par, bias, normed, normed_t, grad, grad_t, hidden, pieces, after=(), through=()):
    n = normed.shape[0]
    parts = 2048 // FFB
    whole = lambda shape: pl.BlockSpec(shape, lambda x, t, s: (0, 0))
    blocks = pl.BlockSpec((2, 1, 4, 2, 64, FFB), lambda x, t, s: (0, x, 0, 0, 0, t))
    bias_spec = lambda rows: pl.BlockSpec((rows, FFB), lambda x, t, s: (0, lax.rem(x + s[3], 2) * parts + t))
    return gated_call(
        after,
        ffn_kernel,
        grid_spec=dict(
            num_scalar_prefetch=1,
            grid=(2, parts),
            in_specs=[
                whole((24, 1024)),
                bias_spec(8),
                whole((n, 1024)),
                whole((1024, n)),
                whole((n, 1024)),
                whole((1024, n)),
                whole((n, 1024)),
            ]
            + [pl.BlockSpec(memory_space=ANYM)] * 6,
            out_specs=[
                whole((n // 2, 1024)),
                whole((n // 2, 1024)),
                whole((n, 1024)),
                blocks,
                blocks,
                bias_spec(8),
            ],
            scratch_shapes=[
                VM((2, 1024, 2048), BF),
                VM((2, 1024, 2048), BF),
                VM((n, 1024), F32),
                VM((n, FFB), BF),
                VM((n, FFB), BF),
                VM((2, 256, FFB), BF),
                pltpu.SemaphoreType.DMA((2, 2)),
            ],
        ),
        out_shape=[
            jax.ShapeDtypeStruct((n // 2, 1024), BF),
            jax.ShapeDtypeStruct((n // 2, 1024), BF),
            jax.ShapeDtypeStruct((n, 1024), F32),
            jax.ShapeDtypeStruct((2, 2, 4, 2, 64, 2048), BF),
            jax.ShapeDtypeStruct((2, 2, 4, 2, 64, 2048), BF),
            jax.ShapeDtypeStruct((8, 4096), F32),
        ],
        compiler_params=params_of(60),
        cost_estimate=cost(51.5e9, 60e6, 4e6),
        through=through,
        name="feedforward",
    )(info, par, bias, normed, normed_t, grad, grad_t, hidden, *pieces)


def back_three_kernel(info, par, dn_ref, h_ref, g_ref, *rest):
    pieces, rest = rest[:1], rest[1:]
    dh_ref, do_ref, gt_ref, sum_ref, wo, sems = rest
    step = pl.program_id(0)

    @pl.when(step == 0)
    def _():
        start_all(pieces, 4096, 512, wo, sems)
        sum_ref[...] = jnp.zeros(sum_ref.shape, F32)
        for slab in range(2):
            wait_weight(wo, sems, slab)

    back_rows(par, 2, dn_ref[...], h_ref[...], g_ref[...].astype(F32), dh_ref, gt_ref, sum_ref, do_ref, wo, sems)


def back_rows(par, index, dn, hidden, residual, dh_ref, gt_ref, sum_ref, do_ref, wo, sems):
    unit, inverse = ln_parts(hidden)
    grad = residual + ln_back(dn, par[index : index + 1, :], unit, inverse)
    dh_ref[...] = grad
    sum_ref[0:1, :] += row_sum(dn * unit)
    sum_ref[1:2, :] += row_sum(dn)
    sum_ref[2:3, :] += row_sum(grad)
    rounded = grad.astype(BF)
    gt_ref[...] = transposed(rounded)
    for slab in range(2):


        do_ref[:, slab * 512 : slab * 512 + 512] = mm(rounded, wo[slab]).astype(BF)


def call_back_three(info, par, dn, h, g, pieces, after=(), through=()):
    n = h.shape[0]
    rows = pl.BlockSpec((ROWS, 1024), lambda i, s: (i, 0))
    return gated_call(
        after,
        back_three_kernel,
        grid_spec=dict(
            num_scalar_prefetch=1,
            grid=(n // ROWS,),
            in_specs=[pl.BlockSpec((24, 1024), lambda i, s: (0, 0)), rows, rows, rows]
            + [pl.BlockSpec(memory_space=ANYM)],
            out_specs=[
                rows,
                rows,
                pl.BlockSpec((1024, ROWS), lambda i, s: (0, i)),
                pl.BlockSpec((8, 1024), lambda i, s: (0, 0)),
            ],
            scratch_shapes=[VM((2, 1024, 512), BF), pltpu.SemaphoreType.DMA((2,))],
        ),
        out_shape=[
            jax.ShapeDtypeStruct((n, 1024), F32),
            jax.ShapeDtypeStruct((n, 1024), BF),
            jax.ShapeDtypeStruct((1024, n), BF),
            jax.ShapeDtypeStruct((8, 1024), F32),
        ],
        compiler_params=params_of(60),
        cost_estimate=cost(2.2e9, 20e6),
        through=through,
        name="back_three",
    )(info, par, dn, h, g, *pieces)


def back_two_kernel(info, par, dq_ref, h_ref, dh2_ref, *rest):
    pieces, rest = rest[:1], rest[1:]
    dh_ref, do_ref, gt_ref, sum_ref, wq, wo, sems = rest
    step = pl.program_id(0)

    @pl.when(step == 0)
    def _():
        start_all(pieces, 1536, 512, wq, sems.at[0])
        start_all(pieces, 1024, 512, wo, sems.at[1])
        sum_ref[...] = jnp.zeros(sum_ref.shape, F32)
        for slab in range(2):
            wait_weight(wq, sems.at[0], slab)
        for slab in range(2):
            wait_weight(wo, sems.at[1], slab)

    dn = None
    for slab in range(2):


        term = mm_nt(dq_ref[:, slab * 512 : slab * 512 + 512], wq[slab])
        dn = term if dn is None else dn + term
    back_rows(par, 1, dn, h_ref[...], dh2_ref[...], dh_ref, gt_ref, sum_ref, do_ref, wo, sems.at[1])


def call_back_two(info, par, dq, h, dh2, pieces, after=(), through=()):
    n = h.shape[0]
    rows = pl.BlockSpec((ROWS, 1024), lambda i, s: (i, 0))
    return gated_call(
        after,
        back_two_kernel,
        grid_spec=dict(
            num_scalar_prefetch=1,
            grid=(n // ROWS,),
            in_specs=[pl.BlockSpec((24, 1024), lambda i, s: (0, 0)), rows, rows, rows]
            + [pl.BlockSpec(memory_space=ANYM)],
            out_specs=[
                rows,
                rows,
                pl.BlockSpec((1024, ROWS), lambda i, s: (0, i)),
                pl.BlockSpec((8, 1024), lambda i, s: (0, 0)),
            ],
            scratch_shapes=[VM((2, 1024, 512), BF)] * 2 + [pltpu.SemaphoreType.DMA((2, 2))],
        ),
        out_shape=[
            jax.ShapeDtypeStruct((n, 1024), F32),
            jax.ShapeDtypeStruct((n, 1024), BF),
            jax.ShapeDtypeStruct((1024, n), BF),
            jax.ShapeDtypeStruct((8, 1024), F32),
        ],
        compiler_params=params_of(60),
        cost_estimate=cost(4.3e9, 24e6),
        through=through,
        name="back_two",
    )(info, par, dq, h, dh2, *pieces)


def memory_back_kernel(info, dk_ref, dv_ref, *rest):
    pieces, rest = rest[:1], rest[1:]
    out_ref, other_ref, wk, wv, sems = rest

    @pl.when(pl.program_id(0) == 0)
    def _():
        start_all(pieces, 0, 512, wk, sems.at[0])
        start_all(pieces, 512, 512, wv, sems.at[1])
        for slab in range(2):
            wait_weight(wk, sems.at[0], slab)
        for slab in range(2):
            wait_weight(wv, sems.at[1], slab)

    total = None
    for t, (ref, weight) in enumerate(((dk_ref, wk), (dv_ref, wv))):
        for slab in range(2):


            term = mm_nt(ref[:, slab * 512 : slab * 512 + 512], weight[slab])
            total = term if total is None else total + term
    own = pl.program_id(0) < pl.num_programs(0) // 2

    @pl.when(own)
    def _():
        out_ref[...] = total.astype(BF)

    @pl.when(jnp.logical_not(own))
    def _():
        other_ref[...] = total.astype(BF)


def call_memory_back(info, dk, dv, pieces, after=(), through=()):
    n = dk.shape[0]
    steps = n // 2 // ROWS
    rows = pl.BlockSpec((ROWS, 1024), lambda i, s: (lax.rem(i + steps * s[3], 2 * steps), 0))
    return gated_call(
        after,
        memory_back_kernel,
        grid_spec=dict(
            num_scalar_prefetch=1,
            grid=(n // ROWS,),
            in_specs=[rows, rows] + [pl.BlockSpec(memory_space=ANYM)],
            out_specs=[
                pl.BlockSpec((ROWS, 1024), lambda i, s: (jnp.minimum(i, steps - 1), 0)),
                pl.BlockSpec((ROWS, 1024), lambda i, s: (jnp.maximum(i - steps, 0), 0)),
            ],
            scratch_shapes=[VM((2, 1024, 512), BF)] * 2 + [pltpu.SemaphoreType.DMA((2, 2))],
        ),
        out_shape=[jax.ShapeDtypeStruct((n // 2, 1024), BF)] * 2,
        compiler_params=params_of(60),
        cost_estimate=cost(4.3e9, 12e6),
        through=through,
        name="memory_back",
    )(info, dk, dv, *pieces)


def back_one_kernel(info, par, dq_ref, dk_ref, dv_ref, x_ref, dh1_ref, *rest):
    pieces, rest = rest[:10], rest[10:]
    out_ref, sum_ref, wq, wk, wv, sems = rest
    weights = (wq, wk, wv)
    step = pl.program_id(0)

    @pl.when(step == 0)
    def _():
        start_self(info, pieces, weights, sems)
        sum_ref[...] = jnp.zeros(sum_ref.shape, F32)
        for t in range(3):
            for slab in range(2):
                wait_weight(weights[t], sems.at[t], slab)

    dn = None
    for t, ref in enumerate((dq_ref, dk_ref, dv_ref)):
        for slab in range(2):


            term = mm_nt(ref[:, slab * 512 : slab * 512 + 512], weights[t][slab])
            dn = term if dn is None else dn + term
    unit, inverse = ln_parts(x_ref[...].astype(F32))
    grad = dh1_ref[...] + ln_back(dn, par[0:1, :], unit, inverse)
    out_ref[...] = grad.astype(BF)
    sum_ref[0:1, :] += row_sum(dn * unit)
    sum_ref[1:2, :] += row_sum(dn)


def call_back_one(info, par, dq, dk, dv, x, dh1, pieces, other, after=(), through=()):
    n = x.shape[0]
    steps = n // 2 // ROWS
    rows = pl.BlockSpec((ROWS, 1024), lambda i, s: (i + steps * own_or_other(s, other), 0))
    return gated_call(
        after,
        back_one_kernel,
        grid_spec=dict(
            num_scalar_prefetch=1,
            grid=(steps,),
            in_specs=[pl.BlockSpec((24, 1024), lambda i, s: (0, 0)), rows, rows, rows, rows, rows]
            + [pl.BlockSpec(memory_space=ANYM)] * 10,
            out_specs=[pl.BlockSpec((ROWS, 1024), lambda i, s: (i, 0)), pl.BlockSpec((8, 1024), lambda i, s: (0, 0))],
            scratch_shapes=[VM((2, 1024, 512), BF)] * 3 + [pltpu.SemaphoreType.DMA((3, 2))],
        ),
        out_shape=[jax.ShapeDtypeStruct((n // 2, 1024), BF), jax.ShapeDtypeStruct((8, 1024), F32)],
        compiler_params=params_of(60),
        cost_estimate=cost(6.4e9, 20e6),
        through=through,
        name="back_one",
    )(info, par, dq, dk, dv, x, dh1, *pieces)


def block_out(kind, width, total):
    if kind == "zxy":
        shape, block = (2, 2, 4, 64, total), (2, 1, 4, 64, width)
        spec = lambda index: pl.BlockSpec(block, index(lambda x, t: (0, x, 0, 0, t)))
    else:
        shape, block = (4, 2, 2, 64, total), (4, 2, 1, 64, width)
        spec = lambda index: pl.BlockSpec(block, index(lambda x, t: (0, 0, x, 0, t)))
    return (jax.ShapeDtypeStruct(shape, BF), spec)


def weight_grad_kernel(kind, picks, count, info, *refs):
    lefts, rights = refs[:count], refs[count : count + len(picks)]
    send_ref, keep_ref, temp = refs[count + len(picks) :]
    for t, pick in enumerate(picks):

        @pl.when(pl.program_id(1) == t)
        def _():
            for zrel in range(4):
                zz = lax.rem(info[0] + zrel, 4)
                rows = pl.ds(pl.multiple_of(zz * 256, 256), 256)
                temp[...] = mm(lefts[pick][rows, :], rights[t][...]).astype(BF)
                store_blocks(info, temp, send_ref, keep_ref, zrel, kind, 512)


def call_weight_grad(info, kind, lefts, rights, picks, name, after=(), through=()):
    n = rights[0].shape[0]
    shape, spec = block_out(kind, 512, 512 * len(rights))
    index = lambda f: (lambda x, t, s: f(x, t))
    return gated_call(
        after,
        partial(weight_grad_kernel, kind, picks, len(lefts)),
        grid_spec=dict(
            num_scalar_prefetch=1,
            grid=(2, len(rights)),
            in_specs=[pl.BlockSpec((1024, n), lambda x, t, s: (0, 0))] * len(lefts)
            + [pl.BlockSpec((n, 512), lambda x, t, s: (0, lax.rem(x + s[3], 2)))] * len(rights),
            out_specs=[spec(index), spec(index)],
            scratch_shapes=[VM((256, 512), BF)],
        ),
        out_shape=[shape, shape],
        compiler_params=params_of(60),
        cost_estimate=cost(10.3e9 * len(rights), 1e6),
        through=through,
        name=name,
    )(info, *lefts, *rights)


def half_grad_kernel(picks, count, info, *refs):
    lefts, rights = refs[:count], refs[count : count + len(picks)]
    send_ref, keep_ref, temp = refs[count + len(picks) :]
    for t, pick in enumerate(picks):

        @pl.when(pl.program_id(0) == t)
        def _():
            for zrel in range(4):
                zz = lax.rem(info[0] + zrel, 4)
                rows = pl.ds(pl.multiple_of(zz * 256, 256), 256)
                temp[...] = mm(lefts[pick][rows, :], rights[t][...]).astype(BF)
                for yrel in range(2):
                    yy = info[1] if yrel == 0 else 1 - info[1]
                    for crel, target in enumerate((keep_ref, send_ref)):
                        cc = info[2] if crel == 0 else 1 - info[2]
                        row = pl.multiple_of(yy * 128 + cc * 64, 64)
                        target[yrel, zrel, :, :] = temp[pl.ds(row, 64), :]


def call_half_grad(info, other, lefts, rights, picks, name, after=(), through=()):
    n = rights[0].shape[0]
    shape = jax.ShapeDtypeStruct((2, 4, 64, 512 * len(rights)), BF)
    spec = pl.BlockSpec((2, 4, 64, 512), lambda t, s: (0, 0, 0, t))
    return gated_call(
        after,
        partial(half_grad_kernel, picks, len(lefts)),
        grid_spec=dict(
            num_scalar_prefetch=1,
            grid=(len(rights),),
            in_specs=[pl.BlockSpec((1024, n), lambda t, s: (0, 0))] * len(lefts)
            + [pl.BlockSpec((n, 512), lambda t, s: (0, own_or_other(s, other)))] * len(rights),
            out_specs=[spec, spec],
            scratch_shapes=[VM((256, 512), BF)],
        ),
        out_shape=[shape, shape],
        compiler_params=params_of(60),
        cost_estimate=cost(10e9, 1e6),
        through=through,
        name=name,
    )(info, *lefts, *rights)


def pack_kernel(one_a, one_b, two, three, cot, own, cross, inner, out_ref):
    out_ref[...] = jnp.zeros(out_ref.shape, F32)
    out_ref[0:1, :] = one_a[0:1, :] + one_b[0:1, :]
    out_ref[3:4, :] = one_a[1:2, :] + one_b[1:2, :]
    for k, ref in ((1, two), (2, three)):
        out_ref[k : k + 1, :] = ref[0:1, :]
        out_ref[3 + k : 4 + k, :] = ref[1:2, :]
        out_ref[5 + k : 6 + k, :] = ref[2:3, :]
    out_ref[8:9, :] = cot[0:1, :]
    out_ref[9:11, :] = own[0:2, :]
    out_ref[11:13, :] = cross[0:2, :]
    for k in range(4):
        out_ref[13 + k : 14 + k, :] = inner[0:1, k * 1024 : k * 1024 + 1024]


def call_pack(*sums):
    return pl.pallas_call(
        pack_kernel,
        out_shape=jax.ShapeDtypeStruct((24, 1024), F32),
        compiler_params=params_of(60),
        name="pack_sums",
    )(*sums)


def along(axis_bit):
    return [(i, i ^ axis_bit) for i in range(16)]


RING = [(i, (i + 4) % 16) for i in range(16)]
FAR_Z = [(i, i ^ 8) for i in range(16)]
BACK = [(i, (i + 12) % 16) for i in range(16)]


def swap_x(value):
    return lax.ppermute(value, "mp", [(0, 1), (1, 0)])


def swap_y(value):
    return lax.ppermute(value, "dp", along(2))


def swap_core(value):
    return lax.ppermute(value, "dp", along(1))


def next_z(value):
    return lax.ppermute(value, "dp", RING)


class Cell:
    def __init__(self, value):
        self.value = value


def values_of(items):
    return [item.value if isinstance(item, Cell) else item for item in items]


class GatherZXY:
    def __init__(self, shard):
        self.steps = [Cell(shard)]

    def z(self):
        self.steps.append(Cell(next_z(self.steps[-1].value)))
        return self.steps[-1]

    def x(self):
        self.base = Cell(jnp.stack(values_of(self.steps)))
        self.over_x = Cell(swap_x(self.base.value))
        return self.over_x

    def y(self):
        self.over_y = Cell(swap_y(self.base.value))
        return self.over_y

    def xy(self):
        self.over_xy = Cell(swap_y(self.over_x.value))
        return self.over_xy

    def core(self):
        self.quads = [self.base, self.over_x, self.over_y, self.over_xy]
        self.other = Cell(swap_core(jnp.concatenate(values_of(self.quads), 0)))
        return self.other

    def pieces(self):
        return values_of(self.quads + [self.other])


class GatherXYZ:
    def __init__(self, shard):
        self.shard = Cell(shard)

    def x(self):
        self.pair = Cell(jnp.stack([self.shard.value, swap_x(self.shard.value)]))
        return self.pair

    def y(self):
        over_y = swap_y(self.pair.value)
        self.quads = [Cell(jnp.concatenate([self.pair.value, over_y], 0))]
        return self.quads[0]

    def z(self):
        self.quads.append(Cell(next_z(self.quads[-1].value)))
        return self.quads[-1]

    def core(self):
        self.other = Cell(swap_core(jnp.concatenate(values_of(self.quads), 0)))
        return self.other

    def pieces(self):
        return values_of(self.quads + [self.other])


def hold(cells, after):
    def kernel(*refs):
        pass

    gated_call(
        after,
        kernel,
        through=cells,
        grid_spec=dict(num_scalar_prefetch=0, grid=(), in_specs=[], out_specs=[]),
        out_shape=[],
        compiler_params=params_of(60),
        name="hold",
    )()


def sum_rest(value):
    value = value + swap_core(value)
    value = value + swap_y(value)
    one, two, three = next_z(value), lax.ppermute(value, "dp", FAR_Z), lax.ppermute(value, "dp", BACK)
    return (value + two) + (one + three)


def join(kept, received):
    return (kept.astype(F32) + received.astype(F32)).astype(kept.dtype)


class ReduceZXY:
    def __init__(self, send, keep):
        self.send, self.keep, self.moving = Cell(send), keep, None

    def core(self):
        self.received = Cell(swap_core(self.send.value))

    def y(self):
        got = self.received.value
        arrived = swap_y(join(self.keep[1], got[1]))
        self.keep, self.also = join(self.keep[0], got[0]), None
        self.received = Cell(arrived)

    def x(self):
        got = self.received.value
        arrived = swap_x(join(self.keep[1], got[1]))
        self.keep, self.also = self.keep[0], got[0]
        self.received = Cell(arrived)
        self.left = 4

    def z(self):
        self.moving = Cell(next_z(self.total(BF)))

    def total(self, kind):
        self.left -= 1
        k = self.left
        value = self.keep[k].astype(F32) + self.also[k].astype(F32) + self.received.value[k].astype(F32)
        if self.moving is not None:
            value = value + self.moving.value.astype(F32)
        return value.astype(kind)

    def result(self):
        return self.total(F32)


class ReduceXYZ:
    def __init__(self, send, keep):
        self.send, self.keep, self.moving = Cell(send), keep, None

    def core(self):
        self.received = Cell(swap_core(self.send.value))
        self.left = 4

    def z(self):
        self.left -= 1
        self.moving = Cell(next_z(self.total(BF, ())))

    def total(self, kind, index):
        k = self.left
        value = self.keep[k][index].astype(F32) + self.received.value[k][index].astype(F32)
        if self.moving is not None:
            value = value + self.moving.value[index].astype(F32)
        return value.astype(kind)

    def y(self):
        self.left -= 1
        self.arrived = Cell(swap_y(self.total(BF, 1)))

    def x(self):
        self.across = Cell(swap_x((self.total(F32, (0, 1)) + self.arrived.value[1].astype(F32)).astype(BF)))

    def result(self):
        return self.total(F32, (0, 0)) + self.arrived.value[0].astype(F32) + self.across.value.astype(F32)


def join_halves(mine, other, me):
    return jnp.where(me == 0, jnp.concatenate([mine, other], 0), jnp.concatenate([other, mine], 0))


class Exchange:
    def __init__(self, local, me):
        self.me = me
        self.mine = jnp.where(me == 0, local[:, 0], local[:, 1])
        self.theirs = Cell(jnp.where(me == 0, local[:, 1], local[:, 0]))

    def go(self):
        self.other = swap_x(self.theirs.value)

    def whole(self):
        return join_halves(self.mine, self.other, self.me)


def both_sequences(mine, other, me):
    return jnp.where(me == 0, jnp.stack([mine, other], 1), jnp.stack([other, mine], 1))


class ReduceHalves:
    def __init__(self, send, keep):
        self.send, self.keep, self.across = Cell(send), keep, None

    def core(self):
        self.received = Cell(swap_core(self.send.value))

    def y(self):
        self.arrived = Cell(swap_y(join(self.keep[1], self.received.value[1])))

    def sum(self, k):
        terms = (self.keep[0], self.received.value[0], self.arrived.value)
        if self.across is not None:
            terms += (self.across.value,)
        return sum(term[k].astype(F32) for term in terms)

    def x(self):
        return Cell(swap_x(self.sum(slice(None)).astype(BF)))

    def z(self, moving=None):
        k = 3 if moving is None else moving[0] - 1
        value = self.sum(k) if moving is None else self.sum(k) + moving[1].astype(F32)
        return (k, next_z(value.astype(BF)))


SMALL = 17 * 1024


def place_small(norm_gains, feature_biases, head_biases, inner_bias, dp, me):
    column = 32 * (2 * dp + me)
    put = lax.dynamic_update_slice
    gains = put(jnp.zeros((3, 1024), F32), norm_gains, (0, column))
    shifts = put(jnp.zeros((6, 1024), F32), feature_biases, (0, column))
    heads = put(jnp.zeros((4, 16, 64), F32), head_biases.astype(F32), (0, me * 8, dp * 4))
    inner = put(jnp.zeros((16, 256), F32), inner_bias.astype(F32), (me * 8, dp * 16))
    return jnp.concatenate([gains, shifts, heads.reshape(4, 1024), inner.reshape(4, 1024)], 0)


def one_sequence_body(
    tokens,
    memory,
    cotangent,
    lengths,
    memory_lengths,
    pair_ids,
    pair_counts,
    self_in,
    self_out,
    cross_in,
    cross_out,
    fc_in,
    fc_out,
    head_biases,
    inner_bias,
    norm_gains,
    feature_biases,
):
    dp, me = lax.axis_index("dp"), lax.axis_index("mp")
    own_length = lax.dynamic_index_in_dim(lengths, me, 0, keepdims=False)
    own_memory = lax.dynamic_index_in_dim(memory_lengths, me, 0, keepdims=False)
    info = jnp.stack([dp // 4, (dp // 2) % 2, dp % 2, me, own_memory, own_length, dp, dp]).astype(jnp.int32)
    counts = pair_counts.astype(F32)
    matches = (pair_ids[:, None] == jnp.arange(counts.shape[0], dtype=jnp.int32)[None, :]).astype(F32)
    scales = jnp.mean(counts) / jnp.sum(matches * counts[None, :], -1)
    scale = jnp.broadcast_to(lax.dynamic_index_in_dim(scales, me, 0, keepdims=False), (8, 128))

    small = place_small(norm_gains, feature_biases, head_biases, inner_bias, dp, me)
    info = Cell(info)
    rest = jnp.concatenate([cross_in[1], cross_in[2], self_out.T, cross_in[0], fc_in, cross_out.T], 1)
    w_rest = [lax.all_gather(rest, ("dp", "mp"), axis=0, tiled=False)]
    own_k = GatherXYZ(self_in[1])
    own_qv = GatherZXY(jnp.concatenate([self_in[0], self_in[2]], 1))
    outer = GatherXYZ(fc_out.T)
    x, mem, cot = Exchange(tokens, me), Exchange(memory, me), Exchange(cotangent, me)
    small = Cell(small + swap_x(small))
    own_k.x(), own_qv.z()
    hold([x.theirs, small], [])
    small = sum_rest(small.value)
    own_k.y(), own_qv.z(), x.go()
    own_k.z(), own_qv.z()
    own_k.z(), own_qv.x(), own_qv.y()
    hold([mem.theirs, outer.shard, own_k.quads[2], own_qv.over_x], [x.other])
    own_k.z(), own_qv.xy(), outer.x()
    hold([own_k.quads[3], own_qv.over_xy, outer.pair], [])
    own_k.core(), own_qv.core(), outer.y()
    par = jnp.concatenate([small[:13], jnp.zeros((11, 1024), F32)], 0)
    inner = jnp.broadcast_to(small[13:17].reshape(1, 4096), (8, 4096))
    x = x.whole()
    hold([info, outer.quads[0], mem.theirs], [own_k.other, own_qv.other, x, par, inner])
    outer.z(), mem.go()
    w_self = own_qv.pieces() + own_k.pieces()
    q1, k1, v1, n1_t = call_qkv(info, par, x, w_self)
    o1, lse1 = call_attend(info, q1, k1, v1, True, 0, 8)
    hold([info, outer.quads[1], cot.theirs], [o1, mem.other])
    outer.z(), cot.go()
    h1, q2, n2_t = call_after_self(info, par, x, o1, w_rest)
    mem = mem.whole()
    k2, v2, mem_t = call_kv(info, par, mem, w_rest, after=[q2])
    hold([info, outer.quads[2]], [k2])
    outer.z()
    o2, lse2 = call_attend(info, q2, k2, v2, False, 0, 8)
    hold([info, outer.quads[3]], [o2, cot.other])
    outer.core()
    h2, n3, n3_t, g3, g3_t, g_sum = call_after_cross(info, par, scale, h1, o2, cot.whole(), w_rest)
    w_fc = w_rest + outer.pieces()
    out, out_peer, dn3, send_fc, keep_fc, d_inner = call_ffn(info, par, inner, n3, n3_t, g3, g3_t, h2, w_fc)

    sum_f = ReduceZXY(send_fc, keep_fc)
    sum_f.core()
    out_other = swap_x(out_peer)
    dh2, do2, g2_t, sums3 = call_back_three(info, par, dn3, h2, g3, w_rest)
    hold([info, sum_f.received], [do2])
    sum_f.y()
    dq2, dk2, dv2, bias2 = call_attend_back(info, q2, k2, v2, o2, do2, lse2, False, 0, 8)
    dh1, do1, g1_t, sums2 = call_back_two(info, par, dq2, h1, dh2, w_rest)
    cross = call_weight_grad(
        info, "zxy", [mem_t, n2_t, g2_t, g1_t], [dk2, dv2, dq2, o2, o1], (0, 0, 1, 2, 3), "weight_grad_cross", after=[do1]
    )
    sum_c = ReduceZXY(*cross)
    hold([info, sum_c.send, sum_f.received], [out_other, sum_c.keep])
    sum_c.core(), sum_f.x()
    grad_mem, mem_peer = call_memory_back(info, dk2, dv2, w_rest)
    mem_peer = Cell(mem_peer)
    hold([info, sum_c.received], [grad_mem])
    sum_c.y()
    back = call_attend_back(info, q1, k1, v1, o1, do1, lse1, True, 0, 4, other=True)
    hold([info, sum_f.received, mem_peer], [back[0]])
    sum_f.z()
    memory_other = swap_x(mem_peer.value)
    sum_s1 = ReduceHalves(*call_half_grad(info, True, [n1_t], back[:3], (0, 0, 0), "weight_grad_self_1"))
    hold([info, sum_s1.send, sum_f.moving], [sum_s1.keep])
    sum_s1.core(), sum_f.z()
    back = call_attend_back(info, q1, k1, v1, o1, do1, lse1, True, 0, 2, back, other=False)
    hold([info, sum_s1.received, sum_c.received, sum_f.moving], [back[0], memory_other])
    sum_s1.y(), sum_c.x(), sum_f.z()
    dq1, dk1, dv1, bias1 = call_attend_back(info, q1, k1, v1, o1, do1, lse1, True, 2, 2, back, other=False)
    hold([info, sum_s1.arrived], [bias1, sum_f.moving])
    across = sum_s1.x()
    sum_s0 = ReduceHalves(*call_half_grad(info, False, [n1_t], [dq1, dk1, dv1], (0, 0, 0), "weight_grad_self_0"))
    hold([info, sum_s0.send, sum_c.received], [sum_s0.keep])
    sum_s0.core(), sum_c.z()
    grad_other, sums1a = call_back_one(info, par, dq1, dk1, dv1, x, dh1, w_self, True)
    grad_other = Cell(grad_other)
    hold([info, sum_s0.received, sum_c.moving, grad_other, across], [])
    sum_s0.y(), sum_c.z()
    tokens_other = swap_x(grad_other.value)
    grad_own, sums1b = call_back_one(info, par, dq1, dk1, dv1, x, dh1, w_self, False)
    d_small = Cell(call_pack(sums1a, sums1b, sums2, sums3, g_sum, bias1, bias2, d_inner))
    hold([sum_s0.arrived, sum_c.moving, d_small], [tokens_other])
    sum_s0.across = across
    moving = sum_s0.z()
    d_small = sum_rest(d_small.value)
    d_small = d_small + swap_x(d_small)
    moving = sum_s0.z(moving)
    sum_c.z()
    moving = sum_s0.z(moving)
    output = both_sequences(out, out_other, me)
    grad_tokens = both_sequences(grad_own, tokens_other, me).astype(F32)
    grad_memory = both_sequences(grad_mem, memory_other, me).astype(F32)
    fc = sum_f.result()
    self_all = sum_s0.sum(0) + moving[1].astype(F32)
    column = 32 * (2 * dp + me)
    take = lax.dynamic_slice
    crossed = sum_c.result()
    return (
        output,
        grad_tokens,
        grad_memory,
        jnp.stack([self_all[:, :512], self_all[:, 512:1024], self_all[:, 1024:]]),
        crossed[:, 2048:].T,
        jnp.stack([crossed[:, 1024:1536], crossed[:, :512], crossed[:, 512:1024]]),
        crossed[:, 1536:2048].T,
        fc[0],
        fc[1].T,
        take(d_small[9:13].reshape(4, 16, 64), (0, me * 8, dp * 4), (4, 8, 4)),
        take(d_small[13:17].reshape(16, 256), (me * 8, dp * 16), (8, 16)),
        take(d_small[:3], (0, column), (3, 32)),
        take(d_small[3:9], (0, column), (6, 32)),
    )


def solution(mesh):
    in_specs = (
        P("mp", "dp", None),
        P("mp", "dp", None),
        P("mp", "dp", None),
        P("dp"),
        P("dp"),
        P("dp"),
        P(),
        P(None, "dp", "mp"),
        P("mp", "dp"),
        P(None, "dp", "mp"),
        P("mp", "dp"),
        P("dp", "mp"),
        P("mp", "dp"),
        P(None, "mp", "dp"),
        P("mp", "dp"),
        P(None, ("dp", "mp")),
        P(None, ("dp", "mp")),
    )
    out_specs = (
        P("mp", "dp", None),
        P("mp", "dp", None),
        P("mp", "dp", None),
        P(None, "dp", "mp"),
        P("mp", "dp"),
        P(None, "dp", "mp"),
        P("mp", "dp"),
        P("dp", "mp"),
        P("mp", "dp"),
        P(None, "mp", "dp"),
        P("mp", "dp"),
        P(None, ("dp", "mp")),
        P(None, ("dp", "mp")),
    )
    sizes = dict(mesh.shape)
    chosen = one_sequence_body if (sizes["dp"], sizes["mp"]) == (16, 2) else body
    return jax.shard_map(chosen, mesh=mesh, in_specs=in_specs, out_specs=out_specs, check_vma=False)
```

```python
from functools import partial

import jax
import jax.numpy as jnp
from jax import lax
from jax.experimental import pallas as pl
from jax.experimental.pallas import tpu as pltpu
from jax.sharding import PartitionSpec as P

eps = 1e-05
floor_score = -1e30


def smooth_unit(values):
    return jax.nn.gelu(values, approximate=True)


def normalize(hidden, gain, shift):
    average = jnp.mean(hidden, -1, keepdims=True)
    centred = hidden - average
    inverse = lax.rsqrt(jnp.mean(centred * centred, -1, keepdims=True) + eps)
    unit = centred * inverse
    return (unit * gain + shift, unit, inverse)


def normalize_back(grad_normed, gain, unit, inverse):
    grad_unit = grad_normed * gain
    grad_hidden = inverse * (
        grad_unit
        - jnp.mean(grad_unit, -1, keepdims=True)
        - unit * jnp.mean(grad_unit * unit, -1, keepdims=True)
    )
    return (grad_hidden, jnp.sum(grad_normed * unit, (0, 1)), jnp.sum(grad_normed, (0, 1)))


def masked_scores(rows, keys, first, limit, causal):
    scores = jnp.einsum("qhd,khd->hqk", rows, keys, preferred_element_type=jnp.float32)
    key_place = jnp.arange(keys.shape[0], dtype=jnp.int32)[None, :]
    if causal:
        allowed = key_place <= first + jnp.arange(rows.shape[0], dtype=jnp.int32)[:, None]
    else:
        allowed = key_place < limit
    return jnp.where(allowed[None], scores, floor_score)


def attend_forward(queries, keys, values, limit, causal):
    length = queries.shape[0]
    block = min(512, length)
    outputs = []
    totals = []
    for first in range(0, length, block):
        span = first + block if causal else keys.shape[0]
        scores = masked_scores(queries[first : first + block], keys[:span], first, limit, causal)
        highest = jnp.max(scores, -1, keepdims=True)
        raised = jnp.exp(scores - highest)
        total = jnp.sum(raised, -1, keepdims=True)
        probs = (raised / total).astype(jnp.bfloat16)
        outputs.append(
            jnp.einsum("hqk,khd->qhd", probs, values[:span], preferred_element_type=jnp.float32)
        )
        totals.append((highest + jnp.log(total))[:, :, 0])
    return (jnp.concatenate(outputs, 0), jnp.concatenate(totals, 1))


def attend_backward(queries, keys, values, totals, grad_mixed, limit, causal):
    length = queries.shape[0]
    block = min(512, length)
    key_grads = jnp.zeros(keys.shape, jnp.float32)
    value_grads = jnp.zeros(values.shape, jnp.float32)
    query_grads = []
    for first in range(0, length, block):
        span = first + block if causal else keys.shape[0]
        rows = queries[first : first + block]
        grad_piece = grad_mixed[first : first + block]
        scores = masked_scores(rows, keys[:span], first, limit, causal)
        probs = jnp.exp(scores - totals[:, first : first + block, None])
        grad_probs = jnp.einsum(
            "qhd,khd->hqk", grad_piece, values[:span], preferred_element_type=jnp.float32
        )
        inner_sum = jnp.sum(probs * grad_probs, -1, keepdims=True)
        grad_scores = (probs * (grad_probs - inner_sum)).astype(jnp.bfloat16)
        query_grads.append(
            jnp.einsum("hqk,khd->qhd", grad_scores, keys[:span], preferred_element_type=jnp.float32)
        )
        key_grads = key_grads.at[:span].add(
            jnp.einsum("hqk,qhd->khd", grad_scores, rows, preferred_element_type=jnp.float32)
        )
        value_grads = value_grads.at[:span].add(
            jnp.einsum(
                "hqk,qhd->khd",
                probs.astype(jnp.bfloat16),
                grad_piece,
                preferred_element_type=jnp.float32,
            )
        )
    return (jnp.concatenate(query_grads, 0), key_grads, value_grads)


def run_forward(operands, causal):
    return attend_forward(operands[0], operands[1], operands[2], operands[3], causal)


def run_backward(operands, causal):
    return attend_backward(
        operands[0], operands[1], operands[2], operands[3], operands[4], operands[5], causal
    )


def gather_rows(normed):
    return lax.all_gather(normed, "mp", axis=0, tiled=True)


def spread_rows(term_fn, rows):
    return lax.psum_scatter(
        term_fn(jnp.int32(0), lax.axis_size("mp") * rows).astype(jnp.bfloat16),
        "mp",
        scatter_dimension=0,
        tiled=True,
    ).astype(jnp.float32)


def whole_rows(term_fn, local, start_row):
    full_rows = local.shape[0] * lax.axis_size("mp")
    term = term_fn(0, full_rows)
    placed = lax.dynamic_update_slice_in_dim(jnp.zeros_like(term), local, start_row, 0)
    return lax.psum((term + placed).astype(jnp.bfloat16), "mp").astype(jnp.float32)


def gather_grads(grad_branch):
    return lax.all_gather(grad_branch, "mp", axis=0, tiled=True)


def reduce_inputs(term_fn, rows):
    return lax.psum_scatter(
        term_fn(jnp.int32(0), lax.axis_size("mp") * rows).astype(jnp.bfloat16),
        "mp",
        scatter_dimension=0,
        tiled=True,
    ).astype(jnp.float32)


def body(
    tokens,
    memory,
    cotangent,
    lengths,
    memory_lengths,
    pair_ids,
    pair_counts,
    self_in,
    self_out,
    cross_in,
    cross_out,
    fc_in,
    fc_out,
    head_biases,
    inner_bias,
    norm_gains,
    feature_biases,
):
    shards = (self_in, self_out, cross_in, cross_out, fc_in, fc_out, head_biases, inner_bias)
    gathered = (
        lax.all_gather(shards[0], "dp", axis=1, tiled=True),
        lax.all_gather(shards[1], "dp", axis=1, tiled=True),
        lax.all_gather(shards[2], "dp", axis=1, tiled=True),
        lax.all_gather(shards[3], "dp", axis=1, tiled=True),
        lax.all_gather(shards[4], "dp", axis=0, tiled=True),
        lax.all_gather(shards[5], "dp", axis=1, tiled=True),
        lax.all_gather(shards[6], "dp", axis=2, tiled=True),
        lax.all_gather(shards[7], "dp", axis=1, tiled=True),
    )
    gains, shifts = (
        lax.all_gather(norm_gains, ("dp", "mp"), axis=1, tiled=True),
        lax.all_gather(feature_biases, ("dp", "mp"), axis=1, tiled=True),
    )
    local_rows, seq_count, width = tokens.shape
    memory_local = memory.shape[0]
    heads_here = head_biases.shape[1]
    head_size = gathered[6].shape[2]
    local_width = heads_here * head_size
    length = local_rows * lax.axis_size("mp")
    memory_length = memory_local * lax.axis_size("mp")
    shape_heads = (seq_count, length, heads_here, head_size)
    shape_memory = (seq_count, memory_length, heads_here, head_size)
    start_row = lax.axis_index("mp") * local_rows
    (
        w_self_in,
        w_self_out,
        w_cross_in,
        w_cross_out,
        feedforward_input_weight,
        feedforward_output_weight,
        w_heads,
        w_inner,
    ) = gathered
    bias_heads = w_heads.astype(jnp.float32).reshape(4, local_width)
    bias_inner = w_inner.astype(jnp.float32).reshape(-1)
    hidden_in = tokens.astype(jnp.float32)
    normed_one, unit_one, inverse_one = normalize(hidden_in, gains[0], shifts[0])
    rows_one = gather_rows(normed_one.astype(jnp.bfloat16))
    project = jnp.einsum("lsd,kde->ksle", rows_one, w_self_in, preferred_element_type=jnp.float32)
    queries_self = ((project[0] + bias_heads[0]) * 0.125).astype(jnp.bfloat16).reshape(shape_heads)
    keys_self = project[1].astype(jnp.bfloat16).reshape(shape_heads)
    values_self = (project[2] + bias_heads[1]).astype(jnp.bfloat16).reshape(shape_heads)
    mixed_self, totals_self = lax.map(
        partial(run_forward, causal=True), (queries_self, keys_self, values_self, lengths)
    )
    mixed_self = mixed_self.astype(jnp.bfloat16).reshape(seq_count, length, local_width)

    def self_term(start, count):
        slice_part = lax.dynamic_slice_in_dim(mixed_self, start, count, 1)
        return jnp.einsum("sle,ed->lsd", slice_part, w_self_out, preferred_element_type=jnp.float32)

    whole_one = whole_rows(self_term, hidden_in, start_row) + shifts[3]
    hidden_one = lax.dynamic_slice_in_dim(whole_one, start_row, local_rows, 0)
    normed_two, unit_two, inverse_two = normalize(hidden_one, gains[1], shifts[1])
    rows_two = normalize(whole_one, gains[1], shifts[1])[0].astype(jnp.bfloat16)
    memory_all = lax.all_gather(memory, "mp", axis=0, tiled=True)
    queries_cross = (
        (
            (
                jnp.einsum(
                    "lsd,de->sle", rows_two, w_cross_in[0], preferred_element_type=jnp.float32
                )
                + bias_heads[2]
            )
            * 0.125
        )
        .astype(jnp.bfloat16)
        .reshape(shape_heads)
    )
    memory_project = jnp.einsum(
        "msd,kde->ksme", memory_all, w_cross_in[1:], preferred_element_type=jnp.float32
    )
    keys_cross = memory_project[0].astype(jnp.bfloat16).reshape(shape_memory)
    values_cross = (memory_project[1] + bias_heads[3]).astype(jnp.bfloat16).reshape(shape_memory)
    mixed_cross, totals_cross = lax.map(
        partial(run_forward, causal=False),
        (queries_cross, keys_cross, values_cross, memory_lengths),
    )
    mixed_cross = mixed_cross.astype(jnp.bfloat16).reshape(seq_count, length, local_width)

    def cross_term(start, count):
        slice_part = lax.dynamic_slice_in_dim(mixed_cross, start, count, 1)
        return jnp.einsum(
            "sle,ed->lsd", slice_part, w_cross_out, preferred_element_type=jnp.float32
        )

    whole_two = whole_rows(cross_term, hidden_one, start_row) + shifts[4]
    hidden_two = lax.dynamic_slice_in_dim(whole_two, start_row, local_rows, 0)
    normed_three, unit_three, inverse_three = normalize(hidden_two, gains[2], shifts[2])
    third_rows = normalize(whole_two, gains[2], shifts[2])[0].astype(jnp.bfloat16)
    inner = (
        jnp.einsum(
            "wri,ix->wrx", third_rows, feedforward_input_weight, preferred_element_type=jnp.float32
        )
        + bias_inner
    )
    smooth_value, smooth_pull = jax.vjp(smooth_unit, inner)
    active_units = smooth_value.astype(jnp.bfloat16)

    def ffn_term(start, count):
        slice_part = lax.dynamic_slice_in_dim(active_units, start, count, 0)
        return jnp.einsum(
            "crx,xp->crp", slice_part, feedforward_output_weight, preferred_element_type=jnp.float32
        )

    output = (hidden_two + spread_rows(ffn_term, local_rows) + shifts[5]).astype(jnp.bfloat16)
    again = (
        lax.all_gather(shards[0], "dp", axis=1, tiled=True),
        lax.all_gather(shards[1], "dp", axis=1, tiled=True),
        lax.all_gather(shards[2], "dp", axis=1, tiled=True),
        lax.all_gather(shards[3], "dp", axis=1, tiled=True),
        lax.all_gather(shards[4], "dp", axis=0, tiled=True),
        lax.all_gather(shards[5], "dp", axis=1, tiled=True),
        lax.all_gather(shards[6], "dp", axis=2, tiled=True),
        lax.all_gather(shards[7], "dp", axis=1, tiled=True),
    )
    (
        w_self_in,
        w_self_out,
        w_cross_in,
        w_cross_out,
        feedforward_input_weight,
        feedforward_output_weight,
        w_heads,
        w_inner,
    ) = again
    counts = pair_counts.astype(jnp.float32)
    matches = (pair_ids[:, None] == jnp.arange(counts.shape[0], dtype=jnp.int32)[None, :]).astype(
        jnp.float32
    )
    own_count = jnp.sum(matches * counts[None, :], -1)
    scale = jnp.mean(counts) / own_count
    positions = start_row + jnp.arange(local_rows, dtype=jnp.int32)
    valid = (positions[:, None] < lengths[None, :]).astype(jnp.float32)
    grad_out = cotangent.astype(jnp.float32) * (valid * scale[None, :])[:, :, None]
    gradient_rows3 = gather_grads(grad_out.astype(jnp.bfloat16))
    gradient_feedforward_output = jnp.einsum(
        "ytb,yth->bh", active_units, gradient_rows3, preferred_element_type=jnp.float32
    )
    grad_active = jnp.einsum(
        "vmr,yr->vmy", gradient_rows3, feedforward_output_weight, preferred_element_type=jnp.float32
    )
    gradient_inner_hidden = smooth_pull(grad_active)[0].astype(jnp.bfloat16)
    grad_fc_in = jnp.einsum(
        "eoc,eoi->ci", third_rows, gradient_inner_hidden, preferred_element_type=jnp.float32
    )
    grad_inner_bias = jnp.sum(gradient_inner_hidden.astype(jnp.float32), (0, 1)).reshape(
        w_inner.shape
    )

    def ffn_back(start, count):
        slice_part = lax.dynamic_slice_in_dim(gradient_inner_hidden, start, count, 0)
        return jnp.einsum(
            "mou,tu->mot", slice_part, feedforward_input_weight, preferred_element_type=jnp.float32
        )

    grad_normed3 = reduce_inputs(ffn_back, local_rows)
    back_three, gain_three, shift_three = normalize_back(
        grad_normed3, gains[2], unit_three, inverse_three
    )
    grad_hidden2 = grad_out + back_three
    grad_rows2 = gather_grads(grad_hidden2.astype(jnp.bfloat16))
    grad_cross_out = jnp.einsum(
        "sle,lsd->ed", mixed_cross, grad_rows2, preferred_element_type=jnp.float32
    )
    grad_mixed = (
        jnp.einsum("lsd,ed->sle", grad_rows2, w_cross_out, preferred_element_type=jnp.float32)
        .astype(jnp.bfloat16)
        .reshape(shape_heads)
    )
    grad_query, grad_key, grad_value = lax.map(
        partial(run_backward, causal=False),
        (queries_cross, keys_cross, values_cross, totals_cross, grad_mixed, memory_lengths),
    )
    grad_query = (grad_query.astype(jnp.bfloat16) * 0.125).reshape(seq_count, length, local_width)
    memory_stack = jnp.stack(
        [
            grad_key.astype(jnp.bfloat16).reshape(seq_count, memory_length, local_width),
            grad_value.astype(jnp.bfloat16).reshape(seq_count, memory_length, local_width),
        ]
    )
    grad_cross_query = jnp.einsum(
        "lsd,sle->de", rows_two, grad_query, preferred_element_type=jnp.float32
    )
    grad_cross_pair = jnp.einsum(
        "msd,ksme->kde", memory_all, memory_stack, preferred_element_type=jnp.float32
    )
    grad_cross_in = jnp.concatenate([grad_cross_query[None], grad_cross_pair], 0)
    bias_query_cross = jnp.sum(grad_query.astype(jnp.float32), (0, 1))
    bias_value_cross = jnp.sum(memory_stack[1].astype(jnp.float32), (0, 1))

    def memory_back(start, count):
        return jnp.einsum(
            "ksme,kde->msd", memory_stack, w_cross_in[1:], preferred_element_type=jnp.float32
        )

    grad_memory = reduce_inputs(memory_back, memory_local)

    def cross_back(start, count):
        slice_part = lax.dynamic_slice_in_dim(grad_query, start, count, 1)
        return jnp.einsum(
            "sle,de->lsd", slice_part, w_cross_in[0], preferred_element_type=jnp.float32
        )

    grad_normed2 = reduce_inputs(cross_back, local_rows)
    back_two, gain_two, shift_two = normalize_back(grad_normed2, gains[1], unit_two, inverse_two)
    grad_hidden1 = grad_hidden2 + back_two
    grad_rows1 = gather_grads(grad_hidden1.astype(jnp.bfloat16))
    grad_self_out = jnp.einsum(
        "sle,lsd->ed", mixed_self, grad_rows1, preferred_element_type=jnp.float32
    )
    grad_mixed = (
        jnp.einsum("lsd,ed->sle", grad_rows1, w_self_out, preferred_element_type=jnp.float32)
        .astype(jnp.bfloat16)
        .reshape(shape_heads)
    )
    grad_query, grad_key, grad_value = lax.map(
        partial(run_backward, causal=True),
        (queries_self, keys_self, values_self, totals_self, grad_mixed, lengths),
    )
    flat_shape = (seq_count, length, local_width)
    self_stack = jnp.stack(
        [
            (grad_query.astype(jnp.bfloat16) * 0.125).reshape(flat_shape),
            grad_key.astype(jnp.bfloat16).reshape(flat_shape),
            grad_value.astype(jnp.bfloat16).reshape(flat_shape),
        ]
    )
    grad_self_in = jnp.einsum(
        "lsd,ksle->kde", rows_one, self_stack, preferred_element_type=jnp.float32
    )
    bias_query_self = jnp.sum(self_stack[0].astype(jnp.float32), (0, 1))
    bias_value_self = jnp.sum(self_stack[2].astype(jnp.float32), (0, 1))

    def self_back(start, count):
        slice_part = lax.dynamic_slice_in_dim(self_stack, start, count, 2)
        return jnp.einsum(
            "ksle,kde->lsd", slice_part, w_self_in, preferred_element_type=jnp.float32
        )

    grad_normed1 = reduce_inputs(self_back, local_rows)
    back_one, gain_one, shift_one = normalize_back(grad_normed1, gains[0], unit_one, inverse_one)
    grad_tokens = grad_hidden1 + back_one
    grad_heads = jnp.stack(
        [bias_query_self, bias_value_self, bias_query_cross, bias_value_cross]
    ).reshape(w_heads.shape)
    gain_grads = jnp.stack([gain_one, gain_two, gain_three])
    shift_grads = jnp.stack(
        [
            shift_one,
            shift_two,
            shift_three,
            jnp.sum(grad_hidden1, (0, 1)),
            jnp.sum(grad_hidden2, (0, 1)),
            jnp.sum(grad_out, (0, 1)),
        ]
    )
    grad_gains, grad_shifts = (
        lax.psum_scatter(gain_grads, ("dp", "mp"), scatter_dimension=1, tiled=True),
        lax.psum_scatter(shift_grads, ("dp", "mp"), scatter_dimension=1, tiled=True),
    )
    all_sums = (
        lax.psum_scatter(
            grad_self_in.astype(jnp.bfloat16), "dp", scatter_dimension=1, tiled=True
        ).astype(jnp.float32),
        lax.psum_scatter(
            grad_self_out.astype(jnp.bfloat16), "dp", scatter_dimension=1, tiled=True
        ).astype(jnp.float32),
        lax.psum_scatter(
            grad_cross_in.astype(jnp.bfloat16), "dp", scatter_dimension=1, tiled=True
        ).astype(jnp.float32),
        lax.psum_scatter(
            grad_cross_out.astype(jnp.bfloat16), "dp", scatter_dimension=1, tiled=True
        ).astype(jnp.float32),
        lax.psum_scatter(
            grad_fc_in.astype(jnp.bfloat16), "dp", scatter_dimension=0, tiled=True
        ).astype(jnp.float32),
        lax.psum_scatter(
            gradient_feedforward_output.astype(jnp.bfloat16), "dp", scatter_dimension=1, tiled=True
        ).astype(jnp.float32),
        lax.psum_scatter(
            grad_heads.astype(jnp.bfloat16), "dp", scatter_dimension=2, tiled=True
        ).astype(jnp.float32),
        lax.psum_scatter(
            grad_inner_bias.astype(jnp.bfloat16), "dp", scatter_dimension=1, tiled=True
        ).astype(jnp.float32),
    )
    (
        sum_self_in,
        sum_self_out,
        sum_cross_in,
        sum_cross_out,
        sum_fc_in,
        sum_fc_out,
        sum_heads,
        sum_inner,
    ) = all_sums
    return (
        output,
        grad_tokens,
        grad_memory,
        sum_self_in,
        sum_self_out,
        sum_cross_in,
        sum_cross_out,
        sum_fc_in,
        sum_fc_out,
        sum_heads,
        sum_inner,
        grad_gains,
        grad_shifts,
    )


LOG2E = 1.4426950408889634
LN2 = 0.6931471805599453
VM = pltpu.VMEM
ANYM = pltpu.HBM
F32 = jnp.float32
BF = jnp.bfloat16
NT_DIMS = (((1,), (1,)), ((), ()))
TN_DIMS = (((0,), (0,)), ((), ()))


def mm(a, b):
    return jnp.dot(a, b, preferred_element_type=F32)


def mm_nt(a, b):
    return lax.dot_general(a, b, NT_DIMS, preferred_element_type=F32)


def mm_tn(a, b):
    return lax.dot_general(a, b, TN_DIMS, preferred_element_type=F32)


def params_of(limit_mib, **more):
    return pltpu.CompilerParams(vmem_limit_bytes=limit_mib * 1024 * 1024, **more)


def cost(flops, data, exps=0):
    return pl.CostEstimate(flops=int(flops), bytes_accessed=int(data), transcendentals=int(exps))


def gated_call(after, kernel, *, grid_spec, out_shape, through=(), input_output_aliases=None, **settings):
    scalars, reads = grid_spec["num_scalar_prefetch"], len(grid_spec["in_specs"])
    used = scalars + reads
    after, through = values_of(after), list(through)
    single = not isinstance(out_shape, list)
    shapes = [out_shape] if single else out_shape
    out_specs = [grid_spec["out_specs"]] if single else list(grid_spec["out_specs"])
    outs, waits = len(shapes), len(after) + len(through)

    def body_of(*refs):
        kernel(*refs[:used], *refs[used + waits : used + waits + outs], *refs[used + waits + outs + len(through) :])

    anywhere = pl.BlockSpec(memory_space=ANYM)
    spec = dict(
        grid_spec,
        in_specs=list(grid_spec["in_specs"]) + [anywhere] * waits,
        out_specs=out_specs + [anywhere] * len(through),
    )
    aliases = dict(input_output_aliases or {})
    aliases.update({used + len(after) + i: outs + i for i in range(len(through))})
    passed = values_of(through)
    call = pl.pallas_call(body_of,
        grid_spec=pltpu.PrefetchScalarGridSpec(**spec),
        out_shape=list(shapes) + [jax.ShapeDtypeStruct(value.shape, value.dtype) for value in passed],
        input_output_aliases=aliases,
        **settings,
    )

    def run(*operands):
        results = call(*values_of(operands), *after, *passed)
        for cell, value in zip(through, results[outs:]):
            cell.value = value
        return results[0] if single else results[:outs]

    return run


def flow_meta(kind):
    corners = [(0, 0), (1, 0), (0, 1), (1, 1)]
    if kind == "zxy":
        near = [[(k, y, 0, x) for k in range(4)] for (x, y) in corners]
    else:
        near = [[(k, y, 0, x) for (x, y) in corners] for k in range(4)]
    return near + [[(k, y, 1, x) for quad in near for (k, y, _, x) in quad]]


def place_of(info, meta):
    k, y, c, x = meta
    slab = info[3] if x == 0 else 1 - info[3]
    zz = lax.rem(info[0] - k + 4, 4)
    yy = info[1] if y == 0 else 1 - info[1]
    cc = info[2] if c == 0 else 1 - info[2]
    return (slab, pl.multiple_of(zz * 256 + yy * 128 + cc * 64, 64))


def start_weight(info, pieces, kind, first, width, buffer, sems):
    for ref, metas in zip(pieces, flow_meta(kind)):
        for j, meta in enumerate(metas):
            slab, row = place_of(info, meta)
            pltpu.make_async_copy(
                ref.at[j, :, pl.ds(first, width)],
                buffer.at[slab, pl.ds(row, 64), :],
                sems.at[slab],
            ).start()


def start_all(pieces, first, width, buffer, sems):
    (ref,) = pieces
    for device in range(32):
        pltpu.make_async_copy(
            ref.at[device, :, pl.ds(first, width)],
            buffer.at[device % 2, pl.ds(device // 2 * 64, 64), :],
            sems.at[device % 2],
        ).start()


def wait_weight(buffer, sems, slab):
    pltpu.make_async_copy(buffer.at[slab], buffer.at[slab], sems.at[slab]).wait()


def ln_parts(hidden):
    average = jnp.mean(hidden, -1, keepdims=True)
    centred = hidden - average
    inverse = lax.rsqrt(jnp.mean(centred * centred, -1, keepdims=True) + eps)
    return (centred * inverse, inverse)


def ln_back(grad_normed, gain, unit, inverse):
    grad_unit = grad_normed * gain
    return inverse * (
        grad_unit
        - jnp.mean(grad_unit, -1, keepdims=True)
        - unit * jnp.mean(grad_unit * unit, -1, keepdims=True)
    )


def row_sum(values):
    return jnp.sum(values, 0, keepdims=True)


def transposed(values):
    return values.T


ROWS = 256
QB = 256


def qkv_kernel(info, par, x_ref, *rest):
    pieces, rest = rest[:10], rest[10:]
    q_ref, k_ref, v_ref, nt_ref, wq, wk, wv, sems = rest
    weights = (wq, wk, wv)

    @pl.when(pl.program_id(0) == 0)
    def _():
        start_self(info, pieces, weights, sems)
        for t in range(3):
            for slab in range(2):
                wait_weight(weights[t], sems.at[t], slab)

    unit, _ = ln_parts(x_ref[...].astype(F32))
    normed = (unit * par[0:1, :] + par[3:4, :]).astype(BF)
    nt_ref[...] = transposed(normed)
    for t in range(3):
        for slab in range(2):


            cols = slice(slab * 512, slab * 512 + 512)
            value = mm(normed, weights[t][slab])
            if t == 0:
                value = (value + par[9:10, cols]) * (0.125 * LOG2E)
            if t == 2:
                value = value + par[10:11, cols]
            (q_ref, k_ref, v_ref)[t][:, cols] = value.astype(BF)


def start_self(info, pieces, weights, sems):
    start_weight(info, pieces[:5], "zxy", 0, 512, weights[0], sems.at[0])
    start_weight(info, pieces[5:], "xyz", 0, 512, weights[1], sems.at[1])
    start_weight(info, pieces[:5], "zxy", 512, 512, weights[2], sems.at[2])


def call_qkv(info, par, x, pieces, after=(), through=()):
    n = x.shape[0]
    out = jax.ShapeDtypeStruct((n, 1024), BF)
    rows = pl.BlockSpec((ROWS, 1024), lambda i, s: (i, 0))
    return gated_call(
        after,
        qkv_kernel,
        grid_spec=dict(
            num_scalar_prefetch=1,
            grid=(n // ROWS,),
            in_specs=[pl.BlockSpec((24, 1024), lambda i, s: (0, 0)), rows]
            + [pl.BlockSpec(memory_space=ANYM)] * 10,
            out_specs=[rows, rows, rows, pl.BlockSpec((1024, ROWS), lambda i, s: (0, i))],
            scratch_shapes=[VM((2, 1024, 512), BF)] * 3 + [pltpu.SemaphoreType.DMA((3, 2))],
        ),
        out_shape=[out, out, out, jax.ShapeDtypeStruct((1024, n), BF)],
        compiler_params=params_of(60),
        cost_estimate=cost(6.4e9, 16e6),
        through=through,
        name="project_self",
    )(info, par, x, *pieces)


def kv_kernel(info, par, x_ref, *rest):
    pieces, rest = rest[:1], rest[1:]
    k_ref, v_ref, nt_ref, wk, wv, sems = rest
    weights = (wk, wv)

    @pl.when(pl.program_id(0) == 0)
    def _():
        for t in range(2):
            start_all(pieces, t * 512, 512, weights[t], sems.at[t])
        for t in range(2):
            for slab in range(2):
                wait_weight(weights[t], sems.at[t], slab)

    rows = x_ref[...]
    nt_ref[...] = transposed(rows)
    for t in range(2):
        for slab in range(2):


            cols = slice(slab * 512, slab * 512 + 512)
            value = mm(rows, weights[t][slab])
            if t == 1:
                value = value + par[12:13, cols]
            (k_ref, v_ref)[t][:, cols] = value.astype(BF)


def call_kv(info, par, x, pieces, after=(), through=()):
    n = x.shape[0]
    out = jax.ShapeDtypeStruct((n, 1024), BF)
    rows = pl.BlockSpec((ROWS, 1024), lambda i, s: (i, 0))
    return gated_call(
        after,
        kv_kernel,
        grid_spec=dict(
            num_scalar_prefetch=1,
            grid=(n // ROWS,),
            in_specs=[pl.BlockSpec((24, 1024), lambda i, s: (0, 0)), rows]
            + [pl.BlockSpec(memory_space=ANYM)],
            out_specs=[rows, rows, pl.BlockSpec((1024, ROWS), lambda i, s: (0, i))],
            scratch_shapes=[VM((2, 1024, 512), BF)] * 2 + [pltpu.SemaphoreType.DMA((2, 2))],
        ),
        out_shape=[out, out, jax.ShapeDtypeStruct((1024, n), BF)],
        compiler_params=params_of(60),
        cost_estimate=cost(4.3e9, 12e6),
        through=through,
        name="project_memory",
    )(info, par, x, *pieces)


def lane_ids(rows):
    return lax.broadcasted_iota(jnp.int32, (rows, 128), 1)


def split3(column):
    high = column.astype(BF)
    rest = column - high.astype(F32)
    middle = rest.astype(BF)
    return (high, middle, (rest - middle.astype(F32)).astype(BF))


def attend_kernel(causal, info, q_ref, k_ref, v_ref, *rest):
    o_ref, lse_ref = rest[-2:]
    lse_ref = lse_ref.at[0]
    n, nk = q_ref.shape[0], k_ref.shape[0]
    lanes_k, lanes_q = lane_ids(nk), lane_ids(QB)
    lane_all = lane_ids(n)

    one = jnp.ones((), BF)
    zero = jnp.zeros((), BF)
    k_aug, v_aug = [], []
    for head in range(2):
        own = (lanes_k >= 64) if head else (lanes_k < 64)
        spare = 0 if head else 64
        keys = jnp.where(own, k_ref[...], zero)
        if not causal:
            place = lax.broadcasted_iota(jnp.int32, (nk, 128), 0)
            shut = jnp.where(place < info[4], 0.0, floor_score).astype(BF)
            keys = jnp.where(lanes_k == spare, shut, keys)
        k_aug.append(keys)
        v_aug.append(jnp.where(own, v_ref[...], jnp.where(lanes_k == spare, one, zero)))
    items = [(first, head) for first in range(0, n, QB) for head in range(2)]

    def scores_of(first, head):
        span = first + QB if causal else nk
        block = q_ref[first : first + QB, :]
        query = block if causal else jnp.where(lanes_q == (0 if head else 64), one, block)
        scores = mm_nt(query, k_aug[head][:span])
        if causal:
            row = lax.broadcasted_iota(jnp.int32, (QB, QB), 0)
            col = lax.broadcasted_iota(jnp.int32, (QB, QB), 1)
            last = jnp.where(col <= row, scores[:, first:], floor_score)
            scores = jnp.concatenate([scores[:, :first], last], 1) if first else last
        return scores

    ahead = scores_of(*items[0])
    for index, (first, head) in enumerate(items):
        scores = ahead
        if index + 1 < len(items):
            ahead = scores_of(*items[index + 1])
        span = first + QB if causal else nk
        highest = jnp.max(scores, -1, keepdims=True)
        raised = jnp.exp2(scores - highest).astype(BF)
        mixed = mm(raised, v_aug[head][:span])
        total = jnp.sum(jnp.where(lanes_q == (0 if head else 64), mixed, 0.0), -1, keepdims=True)
        out, lse = mixed * (1.0 / total), highest + jnp.log2(total)
        if head == 0:
            out_a, lse_a = out, lse
        else:
            o_ref[first : first + QB, :] = jnp.where(lanes_q < 64, out_a, out).astype(BF)
            lse_ref[first : first + QB, :] = jnp.where(lanes_q < 64, lse, lse_a)


def call_attend(info, q, k, v, causal, first, count, earlier=None, after=(), through=()):
    n, nk = q.shape[0], k.shape[0]
    part = (0.625 if causal else 1.0) * count / 8
    heads = lambda rows: pl.BlockSpec((rows, 128), lambda i, s: (0, i + first))
    held = () if earlier is None else tuple(earlier)
    return gated_call(
        after,
        partial(attend_kernel, causal),
        grid_spec=dict(
            num_scalar_prefetch=1,
            grid=(count,),
            in_specs=[heads(n), heads(nk), heads(nk)] + [pl.BlockSpec(memory_space=ANYM)] * len(held),
            out_specs=[heads(n), pl.BlockSpec((1, n, 128), lambda i, s: (i + first, 0, 0))],
        ),
        out_shape=[jax.ShapeDtypeStruct((n, 1024), BF), jax.ShapeDtypeStruct((8, n, 128), F32)],
        input_output_aliases={4: 0, 5: 1} if held else {},
        compiler_params=params_of(60),
        cost_estimate=cost(110.4e9 * part, 1e6),
        name="attend_self" if causal else "attend_cross",
    )(info, q, k, v, *held)


def attend_back_kernel(causal, info, q_ref, k_ref, v_ref, o_ref, g_ref, lse_ref, *rest):
    dq_ref, dk_ref, dv_ref, bias_ref, acc = rest[-5:]
    lse_ref = lse_ref.at[0]
    n, nk = q_ref.shape[0], k_ref.shape[0]
    lanes_k, lanes_q = lane_ids(nk), lane_ids(n)
    one = jnp.ones((), BF)
    zero = jnp.zeros((), BF)
    block_rows = 256 if causal else 512
    q_all, g_all = q_ref[...], g_ref[...]
    k_turned = k_ref[...].T
    product = g_all.astype(F32) * o_ref[...].astype(F32)
    row = lax.broadcasted_iota(jnp.int32, (128, 128), 0)
    col = lax.broadcasted_iota(jnp.int32, (128, 128), 1)
    crossing = jnp.where((row < 64) != (col < 64), one, zero)
    inner = sum(mm(part, crossing) for part in split3(product))
    slot_q, slot_k = lanes_q % 64, lanes_k % 64

    def in_slots(column):
        first, second, third = split3(-column)
        rest = jnp.where(slot_q == 2, third, jnp.where(slot_q == 3, one, zero))
        return jnp.where(slot_q == 0, first, jnp.where(slot_q == 1, second, rest))

    spare_q, spare_g = in_slots(lse_ref[...]), in_slots(inner)
    spare_v = jnp.where(slot_k < 3, one, zero)
    spare_k = spare_v
    if not causal:
        place = lax.broadcasted_iota(jnp.int32, (nk, 128), 0)
        shut = jnp.where(place < info[4], 0.0, floor_score).astype(BF)
        spare_k = jnp.where(slot_k == 3, shut, spare_k)
    k_all, v_all = k_ref[...], v_ref[...]
    sets = []
    for head in range(2):
        own_k = (lanes_k >= 64) if head else (lanes_k < 64)
        own_q = (lanes_q >= 64) if head else (lanes_q < 64)
        sets.append(
            (
                jnp.where(own_q, q_all, zero),
                jnp.where(own_q, g_all, zero),
                jnp.where(own_q, q_all, spare_q),
                jnp.where(own_q, g_all, spare_g),
                jnp.where(own_k, k_all, spare_k),
                jnp.where(own_k, v_all, spare_v),
            )
        )
    items = [(first, head) for first in range(0, nk, block_rows) for head in range(2)]

    def scores_of(first, head):
        from_q = first if causal else 0
        q_own, g_own, q_aug, g_aug, k_aug, v_aug = sets[head]
        keys = slice(first, first + block_rows)
        scores = mm_nt(k_aug[keys], q_aug[from_q:])
        if causal:
            row = lax.broadcasted_iota(jnp.int32, (block_rows, block_rows), 0)
            col = lax.broadcasted_iota(jnp.int32, (block_rows, block_rows), 1)
            head_part = jnp.where(col >= row, scores[:, :block_rows], floor_score)
            if first + block_rows < n:
                scores = jnp.concatenate([head_part, scores[:, block_rows:]], 1)
            else:
                scores = head_part
        return (scores, mm_nt(v_aug[keys], g_aug[from_q:]))

    ahead = scores_of(*items[0])
    acc[...] = jnp.zeros(acc.shape, F32)
    bias = None
    for index, (first, head) in enumerate(items):
        scores, grad_probs = ahead
        if index + 1 < len(items):
            ahead = scores_of(*items[index + 1])
        from_q = first if causal else 0
        q_own, g_own, q_aug, g_aug, k_aug, v_aug = sets[head]
        keys = slice(first, first + block_rows)
        probs = jnp.exp2(scores)
        grad_scores = (probs * grad_probs).astype(BF)
        add_v = mm(probs.astype(BF), g_own[from_q:])
        add_k = mm(grad_scores, q_own[from_q:])
        own = slice(64 * head, 64 * head + 64)
        acc[own, from_q:] += mm(k_turned[own, keys], grad_scores)
        if head == 0:
            dv, dk = add_v, add_k
        else:
            dv = (dv + add_v).astype(BF)
            dv_ref[keys, :] = dv
            dk_ref[keys, :] = ((dk + add_k) * LN2).astype(BF)
            sums = row_sum(dv.astype(F32))
            bias = sums if bias is None else bias + sums
    bias_ref[1:2, :] = bias
    dq = acc[...].T.astype(BF) * jnp.asarray(0.125, BF)
    dq_ref[...] = dq
    bias_ref[0:1, :] = row_sum(dq.astype(F32))


def own_or_other(info, other):
    return 1 - info[3] if other else info[3]


def call_attend_back(info, q, k, v, o, g, lse, causal, first, count, earlier=None, other=None, after=(), through=()):
    n, nk = q.shape[0], k.shape[0]
    part = (0.625 if causal else 1.0) * count / 8
    place = lambda i, s: i + first if other is None else i + first + 4 * own_or_other(s, other)
    heads = lambda rows: pl.BlockSpec((rows, 128), lambda i, s: (0, place(i, s)))
    out = lambda rows: jax.ShapeDtypeStruct((rows, 1024), BF)
    held = () if earlier is None else tuple(earlier)
    return gated_call(
        after,
        partial(attend_back_kernel, causal),
        grid_spec=dict(
            num_scalar_prefetch=1,
            grid=(count,),
            in_specs=[heads(n), heads(nk), heads(nk), heads(n), heads(n)]
            + [pl.BlockSpec((1, n, 128), lambda i, s: (place(i, s), 0, 0))]
            + [pl.BlockSpec(memory_space=ANYM)] * len(held),
            out_specs=[heads(n), heads(nk), heads(nk), heads(8)],
            scratch_shapes=[VM((128, n), F32)],
        ),
        out_shape=[out(n), out(nk), out(nk), jax.ShapeDtypeStruct((8, 1024), F32)],
        input_output_aliases={7: 0, 8: 1, 9: 2, 10: 3} if held else {},
        compiler_params=params_of(60),
        cost_estimate=cost(142.6e9 * part, 1e6),
        name="attend_back_self" if causal else "attend_back_cross",
    )(info, q, k, v, o, g, lse, *held)


def after_self_kernel(info, par, x_ref, o_ref, *rest):
    pieces, rest = rest[:1], rest[1:]
    h_ref, q_ref, nt_ref, wo, wq, sems = rest

    @pl.when(pl.program_id(0) == 0)
    def _():
        start_all(pieces, 1024, 512, wo, sems.at[0])
        start_all(pieces, 1536, 512, wq, sems.at[1])
        for slab in range(2):
            wait_weight(wo, sems.at[0], slab)
        for slab in range(2):
            wait_weight(wq, sems.at[1], slab)

    total = x_ref[...].astype(F32) + par[6:7, :]
    for slab in range(2):


        total = total + mm_nt(o_ref[:, slab * 512 : slab * 512 + 512], wo[slab])
    h_ref[...] = total.astype(BF)
    unit, _ = ln_parts(total)
    normed = (unit * par[1:2, :] + par[4:5, :]).astype(BF)
    nt_ref[...] = transposed(normed)
    for slab in range(2):


        cols = slice(slab * 512, slab * 512 + 512)
        value = (mm(normed, wq[slab]) + par[11:12, cols]) * (0.125 * LOG2E)
        q_ref[:, cols] = value.astype(BF)


def call_after_self(info, par, x, o, pieces, after=(), through=()):
    n = x.shape[0]
    rows = pl.BlockSpec((ROWS, 1024), lambda i, s: (i, 0))
    return gated_call(
        after,
        after_self_kernel,
        grid_spec=dict(
            num_scalar_prefetch=1,
            grid=(n // ROWS,),
            in_specs=[pl.BlockSpec((24, 1024), lambda i, s: (0, 0)), rows, rows]
            + [pl.BlockSpec(memory_space=ANYM)],
            out_specs=[rows, rows, pl.BlockSpec((1024, ROWS), lambda i, s: (0, i))],
            scratch_shapes=[VM((2, 1024, 512), BF)] * 2 + [pltpu.SemaphoreType.DMA((2, 2))],
        ),
        out_shape=[
            jax.ShapeDtypeStruct((n, 1024), BF),
            jax.ShapeDtypeStruct((n, 1024), BF),
            jax.ShapeDtypeStruct((1024, n), BF),
        ],
        compiler_params=params_of(60),
        cost_estimate=cost(4.3e9, 16e6),
        through=through,
        name="after_self",
    )(info, par, x, o, *pieces)


def after_cross_kernel(info, par, scale, h_in, o_ref, cot_ref, *rest):
    pieces, rest = rest[:1], rest[1:]
    h_ref, n_ref, nt_ref, g_ref, gt_ref, gsum_ref, wo, sems = rest
    step = pl.program_id(0)

    @pl.when(step == 0)
    def _():
        start_all(pieces, 4096, 512, wo, sems)
        for slab in range(2):
            wait_weight(wo, sems, slab)

    place = step * ROWS + lax.broadcasted_iota(jnp.int32, (ROWS, 1), 0)
    weight = jnp.where(place < info[5], scale[0, 0], 0.0)
    grad = cot_ref[...].astype(F32) * weight
    rounded = grad.astype(BF)
    g_ref[...] = rounded
    gt_ref[...] = transposed(rounded)
    sums = row_sum(grad)

    @pl.when(step == 0)
    def _():
        gsum_ref[...] = jnp.zeros(gsum_ref.shape, F32)

    gsum_ref[0:1, :] += sums
    total = h_in[...].astype(F32) + par[7:8, :]
    for slab in range(2):


        total = total + mm_nt(o_ref[:, slab * 512 : slab * 512 + 512], wo[slab])
    h_ref[...] = total.astype(BF)
    unit, _ = ln_parts(total)
    normed = (unit * par[2:3, :] + par[5:6, :]).astype(BF)
    n_ref[...] = normed
    nt_ref[...] = transposed(normed)


def call_after_cross(info, par, scale, h, o, cot, pieces, after=(), through=()):
    n = h.shape[0]
    rows = pl.BlockSpec((ROWS, 1024), lambda i, s: (i, 0))
    turned = pl.BlockSpec((1024, ROWS), lambda i, s: (0, i))
    act = jax.ShapeDtypeStruct((n, 1024), BF)
    act_t = jax.ShapeDtypeStruct((1024, n), BF)
    return gated_call(
        after,
        after_cross_kernel,
        grid_spec=dict(
            num_scalar_prefetch=1,
            grid=(n // ROWS,),
            in_specs=[
                pl.BlockSpec((24, 1024), lambda i, s: (0, 0)),
                pl.BlockSpec((8, 128), lambda i, s: (0, 0)),
                rows,
                rows,
                rows,
            ]
            + [pl.BlockSpec(memory_space=ANYM)],
            out_specs=[rows, rows, turned, rows, turned, pl.BlockSpec((8, 1024), lambda i, s: (0, 0))],
            scratch_shapes=[VM((2, 1024, 512), BF), pltpu.SemaphoreType.DMA((2,))],
        ),
        out_shape=[
            jax.ShapeDtypeStruct((n, 1024), BF),
            act,
            act_t,
            act,
            act_t,
            jax.ShapeDtypeStruct((8, 1024), F32),
        ],
        compiler_params=params_of(60),
        cost_estimate=cost(2.2e9, 26e6),
        through=through,
        name="after_cross",
    )(info, par, scale, h, o, cot, *pieces)


GELU_A = 0.7978845608028654
GELU_B = 0.044715


def store_blocks(info, temp, send_ref, keep_ref, zrel, kind, width):
    for yrel in range(2):
        yy = info[1] if yrel == 0 else 1 - info[1]
        for crel in range(2):
            cc = info[2] if crel == 0 else 1 - info[2]
            row = pl.multiple_of(yy * 128 + cc * 64, 64)
            block = temp[pl.ds(row, 64), :]
            target = send_ref if crel else keep_ref
            if kind == "zxy":
                target[yrel, 0, zrel, :, :] = block
            else:
                target[zrel, yrel, 0, :, :] = block


FFB = 512
FFR = 512


def ffn_kernel(info, par, bias_ref, n_ref, nt_ref, g_ref, gt_ref, h_ref, *rest):
    pieces, rest = rest[:6], rest[6:]
    (out_ref, other_ref, dn_ref, send_ref, keep_ref, dbias_ref, w_in, w_out, acc, dn_acc, active, du, temp, sems) = rest
    half, part = pl.program_id(0), pl.program_id(1)
    parts = pl.num_programs(1)
    n = n_ref.shape[0]
    slab = lax.rem(half + info[3], 2)
    first_step = (half == 0) & (part == 0)

    @pl.when(first_step)
    def _():
        start_all(pieces[:1], 2048, 2048, w_in, sems.at[0])
        start_weight(info, pieces[1:], "xyz", 0, 2048, w_out, sems.at[1])
        acc[...] = jnp.zeros(acc.shape, F32)
        dn_acc[...] = jnp.zeros(dn_acc.shape, F32)

    @pl.when(part == 0)
    def _():
        wait_weight(w_in, sems.at[0], slab)
        wait_weight(w_out, sems.at[1], slab)

    cols = pl.ds(pl.multiple_of(part * FFB, FFB), FFB)
    first = w_in.at[slab, :, cols]
    second = w_out.at[slab, :, cols]
    total_bias = None
    chunks = [slice(start, start + FFR) for start in range(0, n, FFR)]

    def products(rows):
        return (mm(n_ref[rows, :], first[...]) + bias_ref[0:1, :], mm(g_ref[rows, :], second[...]))

    ahead = products(chunks[0])
    for index, rows in enumerate(chunks):
        u, dr = ahead
        if index + 1 < len(chunks):
            ahead = products(chunks[index + 1])
        square = u * u
        bend = jnp.tanh(u * (GELU_A + GELU_A * GELU_B * square))
        half_up = 0.5 + 0.5 * bend
        r = (u * half_up).astype(BF)
        active[rows, :] = r
        slope = half_up + 0.5 * u * (1.0 - bend * bend) * (GELU_A + 3.0 * GELU_A * GELU_B * square)
        d = (dr * slope).astype(BF)
        du[rows, :] = d
        sums = row_sum(d.astype(F32))
        total_bias = sums if total_bias is None else total_bias + sums
        acc[rows, :] += mm_nt(r, second[...])
        dn_acc[rows, :] += mm_nt(d, first[...])

    dbias_ref[0:1, :] = total_bias
    for zrel in range(4):
        zz = lax.rem(info[0] + zrel, 4)
        rows = pl.ds(pl.multiple_of(zz * 256, 256), 256)
        for kind, (left, right) in enumerate(((nt_ref, du), (gt_ref, active))):
            temp[kind] = mm(left[rows, :], right[...]).astype(BF)
            for yrel in range(2):
                yy = info[1] if yrel == 0 else 1 - info[1]
                for crel, target in enumerate((keep_ref, send_ref)):
                    cc = info[2] if crel == 0 else 1 - info[2]
                    row = pl.multiple_of(yy * 128 + cc * 64, 64)
                    target[yrel, 0, zrel, kind, :, :] = temp[kind, pl.ds(row, 64), :]

    @pl.when((half == 1) & (part == parts - 1))
    def _():
        dn_ref[...] = dn_acc[...].astype(BF)
        for chunk in range(n // ROWS):
            start = lax.rem(info[3] * (n // 2) + chunk * ROWS, n)
            rows = pl.ds(pl.multiple_of(start, ROWS), ROWS)
            value = h_ref[rows, :].astype(F32) + acc[rows, :] + par[8:9, :]
            target = out_ref if chunk * ROWS < n // 2 else other_ref
            at = chunk * ROWS % (n // 2)
            target[at : at + ROWS, :] = value.astype(BF)


def call_ffn(info, par, bias, normed, normed_t, grad, grad_t, hidden, pieces, after=(), through=()):
    n = normed.shape[0]
    parts = 2048 // FFB
    whole = lambda shape: pl.BlockSpec(shape, lambda x, t, s: (0, 0))
    blocks = pl.BlockSpec((2, 1, 4, 2, 64, FFB), lambda x, t, s: (0, x, 0, 0, 0, t))
    bias_spec = lambda rows: pl.BlockSpec((rows, FFB), lambda x, t, s: (0, lax.rem(x + s[3], 2) * parts + t))
    return gated_call(
        after,
        ffn_kernel,
        grid_spec=dict(
            num_scalar_prefetch=1,
            grid=(2, parts),
            in_specs=[
                whole((24, 1024)),
                bias_spec(8),
                whole((n, 1024)),
                whole((1024, n)),
                whole((n, 1024)),
                whole((1024, n)),
                whole((n, 1024)),
            ]
            + [pl.BlockSpec(memory_space=ANYM)] * 6,
            out_specs=[
                whole((n // 2, 1024)),
                whole((n // 2, 1024)),
                whole((n, 1024)),
                blocks,
                blocks,
                bias_spec(8),
            ],
            scratch_shapes=[
                VM((2, 1024, 2048), BF),
                VM((2, 1024, 2048), BF),
                VM((n, 1024), F32),
                VM((n, 1024), F32),
                VM((n, FFB), BF),
                VM((n, FFB), BF),
                VM((2, 256, FFB), BF),
                pltpu.SemaphoreType.DMA((2, 2)),
            ],
        ),
        out_shape=[
            jax.ShapeDtypeStruct((n // 2, 1024), BF),
            jax.ShapeDtypeStruct((n // 2, 1024), BF),
            jax.ShapeDtypeStruct((n, 1024), BF),
            jax.ShapeDtypeStruct((2, 2, 4, 2, 64, 2048), BF),
            jax.ShapeDtypeStruct((2, 2, 4, 2, 64, 2048), BF),
            jax.ShapeDtypeStruct((8, 4096), F32),
        ],
        compiler_params=params_of(60),
        cost_estimate=cost(51.5e9, 60e6, 4e6),
        through=through,
        name="feedforward",
    )(info, par, bias, normed, normed_t, grad, grad_t, hidden, *pieces)


def back_three_kernel(info, par, dn_ref, h_ref, g_ref, *rest):
    pieces, rest = rest[:1], rest[1:]
    dh_ref, do_ref, gt_ref, sum_ref, wo, sems = rest
    step = pl.program_id(0)

    @pl.when(step == 0)
    def _():
        start_all(pieces, 4096, 512, wo, sems)
        sum_ref[...] = jnp.zeros(sum_ref.shape, F32)
        for slab in range(2):
            wait_weight(wo, sems, slab)

    back_rows(par, 2, dn_ref[...].astype(F32), h_ref[...].astype(F32), g_ref[...].astype(F32), dh_ref, gt_ref, sum_ref, do_ref, wo, sems)


def back_rows(par, index, dn, hidden, residual, dh_ref, gt_ref, sum_ref, do_ref, wo, sems):
    unit, inverse = ln_parts(hidden)
    grad = residual + ln_back(dn, par[index : index + 1, :], unit, inverse)
    dh_ref[...] = grad.astype(BF)
    sum_ref[0:1, :] += row_sum(dn * unit)
    sum_ref[1:2, :] += row_sum(dn)
    sum_ref[2:3, :] += row_sum(grad)
    rounded = grad.astype(BF)
    gt_ref[...] = transposed(rounded)
    for slab in range(2):


        do_ref[:, slab * 512 : slab * 512 + 512] = mm(rounded, wo[slab]).astype(BF)


def call_back_three(info, par, dn, h, g, pieces, after=(), through=()):
    n = h.shape[0]
    rows = pl.BlockSpec((ROWS, 1024), lambda i, s: (i, 0))
    return gated_call(
        after,
        back_three_kernel,
        grid_spec=dict(
            num_scalar_prefetch=1,
            grid=(n // ROWS,),
            in_specs=[pl.BlockSpec((24, 1024), lambda i, s: (0, 0)), rows, rows, rows]
            + [pl.BlockSpec(memory_space=ANYM)],
            out_specs=[
                rows,
                rows,
                pl.BlockSpec((1024, ROWS), lambda i, s: (0, i)),
                pl.BlockSpec((8, 1024), lambda i, s: (0, 0)),
            ],
            scratch_shapes=[VM((2, 1024, 512), BF), pltpu.SemaphoreType.DMA((2,))],
        ),
        out_shape=[
            jax.ShapeDtypeStruct((n, 1024), BF),
            jax.ShapeDtypeStruct((n, 1024), BF),
            jax.ShapeDtypeStruct((1024, n), BF),
            jax.ShapeDtypeStruct((8, 1024), F32),
        ],
        compiler_params=params_of(60),
        cost_estimate=cost(2.2e9, 20e6),
        through=through,
        name="back_three",
    )(info, par, dn, h, g, *pieces)


def back_two_kernel(info, par, dq_ref, h_ref, dh2_ref, *rest):
    pieces, rest = rest[:1], rest[1:]
    dh_ref, do_ref, gt_ref, sum_ref, wq, wo, sems = rest
    step = pl.program_id(0)

    @pl.when(step == 0)
    def _():
        start_all(pieces, 1536, 512, wq, sems.at[0])
        start_all(pieces, 1024, 512, wo, sems.at[1])
        sum_ref[...] = jnp.zeros(sum_ref.shape, F32)
        for slab in range(2):
            wait_weight(wq, sems.at[0], slab)
        for slab in range(2):
            wait_weight(wo, sems.at[1], slab)

    dn = None
    for slab in range(2):


        term = mm_nt(dq_ref[:, slab * 512 : slab * 512 + 512], wq[slab])
        dn = term if dn is None else dn + term
    back_rows(par, 1, dn, h_ref[...].astype(F32), dh2_ref[...].astype(F32), dh_ref, gt_ref, sum_ref, do_ref, wo, sems.at[1])


def call_back_two(info, par, dq, h, dh2, pieces, after=(), through=()):
    n = h.shape[0]
    rows = pl.BlockSpec((ROWS, 1024), lambda i, s: (i, 0))
    return gated_call(
        after,
        back_two_kernel,
        grid_spec=dict(
            num_scalar_prefetch=1,
            grid=(n // ROWS,),
            in_specs=[pl.BlockSpec((24, 1024), lambda i, s: (0, 0)), rows, rows, rows]
            + [pl.BlockSpec(memory_space=ANYM)],
            out_specs=[
                rows,
                rows,
                pl.BlockSpec((1024, ROWS), lambda i, s: (0, i)),
                pl.BlockSpec((8, 1024), lambda i, s: (0, 0)),
            ],
            scratch_shapes=[VM((2, 1024, 512), BF)] * 2 + [pltpu.SemaphoreType.DMA((2, 2))],
        ),
        out_shape=[
            jax.ShapeDtypeStruct((n, 1024), BF),
            jax.ShapeDtypeStruct((n, 1024), BF),
            jax.ShapeDtypeStruct((1024, n), BF),
            jax.ShapeDtypeStruct((8, 1024), F32),
        ],
        compiler_params=params_of(60),
        cost_estimate=cost(4.3e9, 24e6),
        through=through,
        name="back_two",
    )(info, par, dq, h, dh2, *pieces)


def memory_back_kernel(info, dk_ref, dv_ref, *rest):
    pieces, rest = rest[:1], rest[1:]
    out_ref, other_ref, wk, wv, sems = rest

    @pl.when(pl.program_id(0) == 0)
    def _():
        start_all(pieces, 0, 512, wk, sems.at[0])
        start_all(pieces, 512, 512, wv, sems.at[1])
        for slab in range(2):
            wait_weight(wk, sems.at[0], slab)
        for slab in range(2):
            wait_weight(wv, sems.at[1], slab)

    total = None
    for t, (ref, weight) in enumerate(((dk_ref, wk), (dv_ref, wv))):
        for slab in range(2):


            term = mm_nt(ref[:, slab * 512 : slab * 512 + 512], weight[slab])
            total = term if total is None else total + term
    own = pl.program_id(0) < pl.num_programs(0) // 2

    @pl.when(own)
    def _():
        out_ref[...] = total.astype(BF)

    @pl.when(jnp.logical_not(own))
    def _():
        other_ref[...] = total.astype(BF)


def call_memory_back(info, dk, dv, pieces, after=(), through=()):
    n = dk.shape[0]
    steps = n // 2 // ROWS
    rows = pl.BlockSpec((ROWS, 1024), lambda i, s: (lax.rem(i + steps * s[3], 2 * steps), 0))
    return gated_call(
        after,
        memory_back_kernel,
        grid_spec=dict(
            num_scalar_prefetch=1,
            grid=(n // ROWS,),
            in_specs=[rows, rows] + [pl.BlockSpec(memory_space=ANYM)],
            out_specs=[
                pl.BlockSpec((ROWS, 1024), lambda i, s: (jnp.minimum(i, steps - 1), 0)),
                pl.BlockSpec((ROWS, 1024), lambda i, s: (jnp.maximum(i - steps, 0), 0)),
            ],
            scratch_shapes=[VM((2, 1024, 512), BF)] * 2 + [pltpu.SemaphoreType.DMA((2, 2))],
        ),
        out_shape=[jax.ShapeDtypeStruct((n // 2, 1024), BF)] * 2,
        compiler_params=params_of(60),
        cost_estimate=cost(4.3e9, 12e6),
        through=through,
        name="memory_back",
    )(info, dk, dv, *pieces)


def back_one_kernel(info, par, dq_ref, dk_ref, dv_ref, x_ref, dh1_ref, *rest):
    pieces, rest = rest[:10], rest[10:]
    out_ref, sum_ref, wq, wk, wv, sems = rest
    weights = (wq, wk, wv)
    step = pl.program_id(0)

    @pl.when(step == 0)
    def _():
        start_self(info, pieces, weights, sems)
        sum_ref[...] = jnp.zeros(sum_ref.shape, F32)
        for t in range(3):
            for slab in range(2):
                wait_weight(weights[t], sems.at[t], slab)

    dn = None
    for t, ref in enumerate((dq_ref, dk_ref, dv_ref)):
        for slab in range(2):


            term = mm_nt(ref[:, slab * 512 : slab * 512 + 512], weights[t][slab])
            dn = term if dn is None else dn + term
    unit, inverse = ln_parts(x_ref[...].astype(F32))
    grad = dh1_ref[...].astype(F32) + ln_back(dn, par[0:1, :], unit, inverse)
    out_ref[...] = grad.astype(BF)
    sum_ref[0:1, :] += row_sum(dn * unit)
    sum_ref[1:2, :] += row_sum(dn)


def call_back_one(info, par, dq, dk, dv, x, dh1, pieces, other, after=(), through=()):
    n = x.shape[0]
    steps = n // 2 // ROWS
    rows = pl.BlockSpec((ROWS, 1024), lambda i, s: (i + steps * own_or_other(s, other), 0))
    return gated_call(
        after,
        back_one_kernel,
        grid_spec=dict(
            num_scalar_prefetch=1,
            grid=(steps,),
            in_specs=[pl.BlockSpec((24, 1024), lambda i, s: (0, 0)), rows, rows, rows, rows, rows]
            + [pl.BlockSpec(memory_space=ANYM)] * 10,
            out_specs=[pl.BlockSpec((ROWS, 1024), lambda i, s: (i, 0)), pl.BlockSpec((8, 1024), lambda i, s: (0, 0))],
            scratch_shapes=[VM((2, 1024, 512), BF)] * 3 + [pltpu.SemaphoreType.DMA((3, 2))],
        ),
        out_shape=[jax.ShapeDtypeStruct((n // 2, 1024), BF), jax.ShapeDtypeStruct((8, 1024), F32)],
        compiler_params=params_of(60),
        cost_estimate=cost(6.4e9, 20e6),
        through=through,
        name="back_one",
    )(info, par, dq, dk, dv, x, dh1, *pieces)


def block_out(kind, width, total):
    if kind == "zxy":
        shape, block = (2, 2, 4, 64, total), (2, 1, 4, 64, width)
        spec = lambda index: pl.BlockSpec(block, index(lambda x, t: (0, x, 0, 0, t)))
    else:
        shape, block = (4, 2, 2, 64, total), (4, 2, 1, 64, width)
        spec = lambda index: pl.BlockSpec(block, index(lambda x, t: (0, 0, x, 0, t)))
    return (jax.ShapeDtypeStruct(shape, BF), spec)


def weight_grad_kernel(kind, picks, count, info, *refs):
    lefts, rights = refs[:count], refs[count : count + len(picks)]
    send_ref, keep_ref, temp = refs[count + len(picks) :]
    for t, pick in enumerate(picks):

        @pl.when(pl.program_id(1) == t)
        def _():
            for zrel in range(4):
                zz = lax.rem(info[0] + zrel, 4)
                rows = pl.ds(pl.multiple_of(zz * 256, 256), 256)
                temp[...] = mm(lefts[pick][rows, :], rights[t][...]).astype(BF)
                store_blocks(info, temp, send_ref, keep_ref, zrel, kind, 512)


def call_weight_grad(info, kind, lefts, rights, picks, name, after=(), through=()):
    n = rights[0].shape[0]
    shape, spec = block_out(kind, 512, 512 * len(rights))
    index = lambda f: (lambda x, t, s: f(x, t))
    return gated_call(
        after,
        partial(weight_grad_kernel, kind, picks, len(lefts)),
        grid_spec=dict(
            num_scalar_prefetch=1,
            grid=(2, len(rights)),
            in_specs=[pl.BlockSpec((1024, n), lambda x, t, s: (0, 0))] * len(lefts)
            + [pl.BlockSpec((n, 512), lambda x, t, s: (0, lax.rem(x + s[3], 2)))] * len(rights),
            out_specs=[spec(index), spec(index)],
            scratch_shapes=[VM((256, 512), BF)],
        ),
        out_shape=[shape, shape],
        compiler_params=params_of(60),
        cost_estimate=cost(10.3e9 * len(rights), 1e6),
        through=through,
        name=name,
    )(info, *lefts, *rights)


def half_grad_kernel(picks, count, info, *refs):
    lefts, rights = refs[:count], refs[count : count + len(picks)]
    send_ref, keep_ref, temp = refs[count + len(picks) :]
    for t, pick in enumerate(picks):

        @pl.when(pl.program_id(0) == t)
        def _():
            for zrel in range(4):
                zz = lax.rem(info[0] + zrel, 4)
                rows = pl.ds(pl.multiple_of(zz * 256, 256), 256)
                temp[...] = mm(lefts[pick][rows, :], rights[t][...]).astype(BF)
                for yrel in range(2):
                    yy = info[1] if yrel == 0 else 1 - info[1]
                    for crel, target in enumerate((keep_ref, send_ref)):
                        cc = info[2] if crel == 0 else 1 - info[2]
                        row = pl.multiple_of(yy * 128 + cc * 64, 64)
                        target[yrel, zrel, :, :] = temp[pl.ds(row, 64), :]


def call_half_grad(info, other, lefts, rights, picks, name, after=(), through=()):
    n = rights[0].shape[0]
    shape = jax.ShapeDtypeStruct((2, 4, 64, 512 * len(rights)), BF)
    spec = pl.BlockSpec((2, 4, 64, 512), lambda t, s: (0, 0, 0, t))
    return gated_call(
        after,
        partial(half_grad_kernel, picks, len(lefts)),
        grid_spec=dict(
            num_scalar_prefetch=1,
            grid=(len(rights),),
            in_specs=[pl.BlockSpec((1024, n), lambda t, s: (0, 0))] * len(lefts)
            + [pl.BlockSpec((n, 512), lambda t, s: (0, own_or_other(s, other)))] * len(rights),
            out_specs=[spec, spec],
            scratch_shapes=[VM((256, 512), BF)],
        ),
        out_shape=[shape, shape],
        compiler_params=params_of(60),
        cost_estimate=cost(10e9, 1e6),
        through=through,
        name=name,
    )(info, *lefts, *rights)


def pack_kernel(one_a, one_b, two, three, cot, own, cross, inner, out_ref):
    out_ref[...] = jnp.zeros(out_ref.shape, F32)
    out_ref[0:1, :] = one_a[0:1, :] + one_b[0:1, :]
    out_ref[3:4, :] = one_a[1:2, :] + one_b[1:2, :]
    for k, ref in ((1, two), (2, three)):
        out_ref[k : k + 1, :] = ref[0:1, :]
        out_ref[3 + k : 4 + k, :] = ref[1:2, :]
        out_ref[5 + k : 6 + k, :] = ref[2:3, :]
    out_ref[8:9, :] = cot[0:1, :]
    out_ref[9:11, :] = own[0:2, :]
    out_ref[11:13, :] = cross[0:2, :]
    for k in range(4):
        out_ref[13 + k : 14 + k, :] = inner[0:1, k * 1024 : k * 1024 + 1024]


def call_pack(*sums):
    return pl.pallas_call(
        pack_kernel,
        out_shape=jax.ShapeDtypeStruct((24, 1024), F32),
        compiler_params=params_of(60),
        name="pack_sums",
    )(*sums)


def along(axis_bit):
    return [(i, i ^ axis_bit) for i in range(16)]


RING = [(i, (i + 4) % 16) for i in range(16)]
FAR_Z = [(i, i ^ 8) for i in range(16)]
BACK = [(i, (i + 12) % 16) for i in range(16)]


def swap_x(value):
    return lax.ppermute(value, "mp", [(0, 1), (1, 0)])


def swap_y(value):
    return lax.ppermute(value, "dp", along(2))


def swap_core(value):
    return lax.ppermute(value, "dp", along(1))


def next_z(value):
    return lax.ppermute(value, "dp", RING)


class Cell:
    def __init__(self, value):
        self.value = value


def values_of(items):
    return [item.value if isinstance(item, Cell) else item for item in items]


class GatherZXY:
    def __init__(self, shard):
        self.steps = [Cell(shard)]

    def z(self):
        self.steps.append(Cell(next_z(self.steps[-1].value)))
        return self.steps[-1]

    def x(self):
        self.base = Cell(jnp.stack(values_of(self.steps)))
        self.over_x = Cell(swap_x(self.base.value))
        return self.over_x

    def y(self):
        self.over_y = Cell(swap_y(self.base.value))
        return self.over_y

    def xy(self):
        self.over_xy = Cell(swap_y(self.over_x.value))
        return self.over_xy

    def core(self):
        self.quads = [self.base, self.over_x, self.over_y, self.over_xy]
        self.other = Cell(swap_core(jnp.concatenate(values_of(self.quads), 0)))
        return self.other

    def pieces(self):
        return values_of(self.quads + [self.other])


class GatherXYZ:
    def __init__(self, shard):
        self.shard = Cell(shard)

    def x(self):
        self.pair = Cell(jnp.stack([self.shard.value, swap_x(self.shard.value)]))
        return self.pair

    def y(self):
        over_y = swap_y(self.pair.value)
        self.quads = [Cell(jnp.concatenate([self.pair.value, over_y], 0))]
        return self.quads[0]

    def z(self):
        self.quads.append(Cell(next_z(self.quads[-1].value)))
        return self.quads[-1]

    def core(self):
        self.other = Cell(swap_core(jnp.concatenate(values_of(self.quads), 0)))
        return self.other

    def pieces(self):
        return values_of(self.quads + [self.other])


def hold(cells, after):
    def kernel(*refs):
        pass

    gated_call(
        after,
        kernel,
        through=cells,
        grid_spec=dict(num_scalar_prefetch=0, grid=(), in_specs=[], out_specs=[]),
        out_shape=[],
        compiler_params=params_of(60),
        name="hold",
    )()


def sum_rest(value):
    value = value + swap_core(value)
    value = value + swap_y(value)
    one, two, three = next_z(value), lax.ppermute(value, "dp", FAR_Z), lax.ppermute(value, "dp", BACK)
    return (value + two) + (one + three)


def join(kept, received):
    return (kept.astype(F32) + received.astype(F32)).astype(kept.dtype)


class ReduceZXY:
    def __init__(self, send, keep):
        self.send, self.keep, self.moving = Cell(send), keep, None

    def core(self):
        self.received = Cell(swap_core(self.send.value))

    def y(self):
        got = self.received.value
        arrived = swap_y(join(self.keep[1], got[1]))
        self.keep, self.also = join(self.keep[0], got[0]), None
        self.received = Cell(arrived)

    def x(self):
        got = self.received.value
        arrived = swap_x(join(self.keep[1], got[1]))
        self.keep, self.also = self.keep[0], got[0]
        self.received = Cell(arrived)
        self.left = 4

    def z(self):
        self.moving = Cell(next_z(self.total(BF)))

    def total(self, kind):
        self.left -= 1
        k = self.left
        value = self.keep[k].astype(F32) + self.also[k].astype(F32) + self.received.value[k].astype(F32)
        if self.moving is not None:
            value = value + self.moving.value.astype(F32)
        return value.astype(kind)

    def result(self):
        return self.total(F32)


class ReduceXYZ:
    def __init__(self, send, keep):
        self.send, self.keep, self.moving = Cell(send), keep, None

    def core(self):
        self.received = Cell(swap_core(self.send.value))
        self.left = 4

    def z(self):
        self.left -= 1
        self.moving = Cell(next_z(self.total(BF, ())))

    def total(self, kind, index):
        k = self.left
        value = self.keep[k][index].astype(F32) + self.received.value[k][index].astype(F32)
        if self.moving is not None:
            value = value + self.moving.value[index].astype(F32)
        return value.astype(kind)

    def y(self):
        self.left -= 1
        self.arrived = Cell(swap_y(self.total(BF, 1)))

    def x(self):
        self.across = Cell(swap_x((self.total(F32, (0, 1)) + self.arrived.value[1].astype(F32)).astype(BF)))

    def result(self):
        return self.total(F32, (0, 0)) + self.arrived.value[0].astype(F32) + self.across.value.astype(F32)


def join_halves(mine, other, me):
    return jnp.where(me == 0, jnp.concatenate([mine, other], 0), jnp.concatenate([other, mine], 0))


class Exchange:
    def __init__(self, local, me):
        self.me = me
        self.mine = jnp.where(me == 0, local[:, 0], local[:, 1])
        self.theirs = Cell(jnp.where(me == 0, local[:, 1], local[:, 0]))

    def go(self):
        self.other = swap_x(self.theirs.value)

    def whole(self):
        return join_halves(self.mine, self.other, self.me)


def both_sequences(mine, other, me):
    return jnp.where(me == 0, jnp.stack([mine, other], 1), jnp.stack([other, mine], 1))


class ReduceHalves:
    def __init__(self, send, keep):
        self.send, self.keep, self.across = Cell(send), keep, None

    def core(self):
        self.received = Cell(swap_core(self.send.value))

    def y(self):
        self.arrived = Cell(swap_y(join(self.keep[1], self.received.value[1])))

    def sum(self, k):
        terms = (self.keep[0], self.received.value[0], self.arrived.value)
        if self.across is not None:
            terms += (self.across.value,)
        return sum(term[k].astype(F32) for term in terms)

    def x(self):
        return Cell(swap_x(self.sum(slice(None)).astype(BF)))

    def z(self, moving=None):
        k = 3 if moving is None else moving[0] - 1
        value = self.sum(k) if moving is None else self.sum(k) + moving[1].astype(F32)
        return (k, next_z(value.astype(BF)))


SMALL = 17 * 1024


def place_small(norm_gains, feature_biases, head_biases, inner_bias, dp, me):
    column = 32 * (2 * dp + me)
    put = lax.dynamic_update_slice
    gains = put(jnp.zeros((3, 1024), F32), norm_gains, (0, column))
    shifts = put(jnp.zeros((6, 1024), F32), feature_biases, (0, column))
    heads = put(jnp.zeros((4, 16, 64), F32), head_biases.astype(F32), (0, me * 8, dp * 4))
    inner = put(jnp.zeros((16, 256), F32), inner_bias.astype(F32), (me * 8, dp * 16))
    return jnp.concatenate([gains, shifts, heads.reshape(4, 1024), inner.reshape(4, 1024)], 0)


def one_sequence_body(
    tokens,
    memory,
    cotangent,
    lengths,
    memory_lengths,
    pair_ids,
    pair_counts,
    self_in,
    self_out,
    cross_in,
    cross_out,
    fc_in,
    fc_out,
    head_biases,
    inner_bias,
    norm_gains,
    feature_biases,
):
    dp, me = lax.axis_index("dp"), lax.axis_index("mp")
    own_length = lax.dynamic_index_in_dim(lengths, me, 0, keepdims=False)
    own_memory = lax.dynamic_index_in_dim(memory_lengths, me, 0, keepdims=False)
    info = jnp.stack([dp // 4, (dp // 2) % 2, dp % 2, me, own_memory, own_length, dp, dp]).astype(jnp.int32)
    counts = pair_counts.astype(F32)
    matches = (pair_ids[:, None] == jnp.arange(counts.shape[0], dtype=jnp.int32)[None, :]).astype(F32)
    scales = jnp.mean(counts) / jnp.sum(matches * counts[None, :], -1)
    scale = jnp.broadcast_to(lax.dynamic_index_in_dim(scales, me, 0, keepdims=False), (8, 128))

    small = place_small(norm_gains, feature_biases, head_biases, inner_bias, dp, me)
    info = Cell(info)
    rest = jnp.concatenate([cross_in[1], cross_in[2], self_out.T, cross_in[0], fc_in, cross_out.T], 1)
    w_rest = [lax.all_gather(rest, ("dp", "mp"), axis=0, tiled=False)]
    own_k = GatherXYZ(self_in[1])
    own_qv = GatherZXY(jnp.concatenate([self_in[0], self_in[2]], 1))
    outer = GatherXYZ(fc_out.T)
    x, mem, cot = Exchange(tokens, me), Exchange(memory, me), Exchange(cotangent, me)
    small = Cell(small + swap_x(small))
    own_k.x(), own_qv.z()
    hold([x.theirs, small], [])
    small = sum_rest(small.value)
    own_k.y(), own_qv.z(), x.go()
    own_k.z(), own_qv.z()
    own_k.z(), own_qv.x(), own_qv.y()
    hold([mem.theirs, outer.shard, own_k.quads[2], own_qv.over_x], [x.other])
    own_k.z(), own_qv.xy(), outer.x()
    hold([own_k.quads[3], own_qv.over_xy, outer.pair], [])
    own_k.core(), own_qv.core(), outer.y()
    par = jnp.concatenate([small[:13], jnp.zeros((11, 1024), F32)], 0)
    inner = jnp.broadcast_to(small[13:17].reshape(1, 4096), (8, 4096))
    x = x.whole()
    hold([info, outer.quads[0], mem.theirs], [own_k.other, own_qv.other, x, par, inner])
    outer.z(), mem.go()
    w_self = own_qv.pieces() + own_k.pieces()
    q1, k1, v1, n1_t = call_qkv(info, par, x, w_self)
    o1, lse1 = call_attend(info, q1, k1, v1, True, 0, 8)
    hold([info, outer.quads[1], cot.theirs], [o1, mem.other])
    outer.z(), cot.go()
    h1, q2, n2_t = call_after_self(info, par, x, o1, w_rest)
    mem = mem.whole()
    k2, v2, mem_t = call_kv(info, par, mem, w_rest, after=[q2])
    hold([info, outer.quads[2]], [k2])
    outer.z()
    o2, lse2 = call_attend(info, q2, k2, v2, False, 0, 8)
    hold([info, outer.quads[3]], [o2, cot.other])
    outer.core()
    h2, n3, n3_t, g3, g3_t, g_sum = call_after_cross(info, par, scale, h1, o2, cot.whole(), w_rest)
    w_fc = w_rest + outer.pieces()
    out, out_peer, dn3, send_fc, keep_fc, d_inner = call_ffn(info, par, inner, n3, n3_t, g3, g3_t, h2, w_fc)

    sum_f = ReduceZXY(send_fc, keep_fc)
    sum_f.core()
    out_other = swap_x(out_peer)
    dh2, do2, g2_t, sums3 = call_back_three(info, par, dn3, h2, g3, w_rest)
    hold([info, sum_f.received], [do2])
    sum_f.y()
    dq2, dk2, dv2, bias2 = call_attend_back(info, q2, k2, v2, o2, do2, lse2, False, 0, 8)
    dh1, do1, g1_t, sums2 = call_back_two(info, par, dq2, h1, dh2, w_rest)
    cross = call_weight_grad(
        info, "zxy", [mem_t, n2_t, g2_t, g1_t], [dk2, dv2, dq2, o2, o1], (0, 0, 1, 2, 3), "weight_grad_cross", after=[do1]
    )
    sum_c = ReduceZXY(*cross)
    hold([info, sum_c.send, sum_f.received], [out_other, sum_c.keep])
    sum_c.core(), sum_f.x()
    grad_mem, mem_peer = call_memory_back(info, dk2, dv2, w_rest)
    mem_peer = Cell(mem_peer)
    hold([info, sum_c.received], [grad_mem])
    sum_c.y()
    back = call_attend_back(info, q1, k1, v1, o1, do1, lse1, True, 0, 4, other=True)
    hold([info, mem_peer], [back[0]])
    memory_other = swap_x(mem_peer.value)
    sum_s1 = ReduceHalves(*call_half_grad(info, True, [n1_t], back[:3], (0, 0, 0), "weight_grad_self_1"))
    hold([info, sum_s1.send, sum_f.received], [sum_s1.keep])
    sum_s1.core(), sum_f.z()
    back = call_attend_back(info, q1, k1, v1, o1, do1, lse1, True, 0, 2, back, other=False)
    hold([info, sum_s1.received, sum_c.received, sum_f.moving], [back[0]])
    sum_s1.y(), sum_c.x(), sum_f.z()
    dq1, dk1, dv1, bias1 = call_attend_back(info, q1, k1, v1, o1, do1, lse1, True, 2, 2, back, other=False)
    hold([info, sum_s1.arrived, sum_f.moving], [bias1, memory_other])
    across = sum_s1.x()
    sum_f.z()
    sum_s0 = ReduceHalves(*call_half_grad(info, False, [n1_t], [dq1, dk1, dv1], (0, 0, 0), "weight_grad_self_0"))
    hold([info, sum_s0.send, sum_c.received], [sum_s0.keep, sum_f.moving])
    sum_s0.core(), sum_c.z()
    grad_other, sums1a = call_back_one(info, par, dq1, dk1, dv1, x, dh1, w_self, True)
    grad_other = Cell(grad_other)
    hold([info, sum_s0.received, sum_c.moving, grad_other, across], [])
    sum_s0.y(), sum_c.z()
    tokens_other = swap_x(grad_other.value)
    grad_own, sums1b = call_back_one(info, par, dq1, dk1, dv1, x, dh1, w_self, False)
    d_small = Cell(call_pack(sums1a, sums1b, sums2, sums3, g_sum, bias1, bias2, d_inner))
    hold([sum_s0.arrived, sum_c.moving, d_small], [tokens_other])
    sum_s0.across = across
    moving = sum_s0.z()
    d_small = sum_rest(d_small.value)
    d_small = d_small + swap_x(d_small)
    moving = sum_s0.z(moving)
    sum_c.z()
    moving = sum_s0.z(moving)
    output = both_sequences(out, out_other, me)
    grad_tokens = both_sequences(grad_own, tokens_other, me).astype(F32)
    grad_memory = both_sequences(grad_mem, memory_other, me).astype(F32)
    fc = sum_f.result()
    self_all = sum_s0.sum(0) + moving[1].astype(F32)
    column = 32 * (2 * dp + me)
    take = lax.dynamic_slice
    crossed = sum_c.result()
    return (
        output,
        grad_tokens,
        grad_memory,
        jnp.stack([self_all[:, :512], self_all[:, 512:1024], self_all[:, 1024:]]),
        crossed[:, 2048:].T,
        jnp.stack([crossed[:, 1024:1536], crossed[:, :512], crossed[:, 512:1024]]),
        crossed[:, 1536:2048].T,
        fc[0],
        fc[1].T,
        take(d_small[9:13].reshape(4, 16, 64), (0, me * 8, dp * 4), (4, 8, 4)),
        take(d_small[13:17].reshape(16, 256), (me * 8, dp * 16), (8, 16)),
        take(d_small[:3], (0, column), (3, 32)),
        take(d_small[3:9], (0, column), (6, 32)),
    )


def solution(mesh):
    in_specs = (
        P("mp", "dp", None),
        P("mp", "dp", None),
        P("mp", "dp", None),
        P("dp"),
        P("dp"),
        P("dp"),
        P(),
        P(None, "dp", "mp"),
        P("mp", "dp"),
        P(None, "dp", "mp"),
        P("mp", "dp"),
        P("dp", "mp"),
        P("mp", "dp"),
        P(None, "mp", "dp"),
        P("mp", "dp"),
        P(None, ("dp", "mp")),
        P(None, ("dp", "mp")),
    )
    out_specs = (
        P("mp", "dp", None),
        P("mp", "dp", None),
        P("mp", "dp", None),
        P(None, "dp", "mp"),
        P("mp", "dp"),
        P(None, "dp", "mp"),
        P("mp", "dp"),
        P("dp", "mp"),
        P("mp", "dp"),
        P(None, "mp", "dp"),
        P("mp", "dp"),
        P(None, ("dp", "mp")),
        P(None, ("dp", "mp")),
    )
    sizes = dict(mesh.shape)
    chosen = one_sequence_body if (sizes["dp"], sizes["mp"]) == (16, 2) else body
    return jax.shard_map(chosen, mesh=mesh, in_specs=in_specs, out_specs=out_specs, check_vma=False)
```
